256 devices in a mesh: leaf: 64 (over z, x, core), chan: 4 (over y).
Axes of the slice: x: 4, y: 4, z: 8, core: 2. Of those that a mesh axis runs over, the one named last changes fastest.
Arguments:
- features: bfloat16 [192, 65536], P('chan', 'leaf'), may hold values from -6 to 6
- in_factor: bfloat16 [192, 48], P('chan'), may hold values from -0.4375 to 0.4375
- core: bfloat16 [27, 48, 48], P(None, 'chan'), may hold values from -0.15625 to 0.15625
- out_factor: bfloat16 [48, 192], P(None, 'chan'), may hold values from -0.875 to 0.875
- neighbours: int32 [27, 65536], P(None, 'leaf'), may hold values from -1 to 5119, as said below
- halo_blocks: int32 [64, 8, 8], P('leaf'), may hold values from -1 to 1023, as said below
- row_mask: int32 [65536], P('leaf'), may hold values 0 or 1
- cotangent: bfloat16 [192, 65536], P('chan', 'leaf'), may hold values from -6 to 6
Outputs:
- output: bfloat16 [192, 65536], P('chan', 'leaf')
- grad_features: bfloat16 [192, 65536], P('chan', 'leaf')
- grad_in: float32 [192, 48], P('chan')
- grad_core: float32 [27, 48, 48], P(None, 'chan')
- grad_out: float32 [48, 192], P(None, 'chan')
The draws below stay inside these ranges and needn't reach their ends.
Inputs may be any that keep to these rules, and one draw needn't show every extreme that they name: Peer slot s of leaf device d stands for device p = d + s - 4 for s < 4 and p = d + s - 3 otherwise. If 0 <= p < 64, halo_blocks[d, s, :] are 8 consecutive blocks owned by p, ids p * 16 to p * 16 + 15; otherwise they are -1. `neighbours`: offset 13 is the octant itself (e equals its local row); -1 marks a missing neighbour; every other entry is a local row or a received slot as in the first step, whose peer slot stands for a device of the axis.
All inputs are finite; a program needn't handle non-finite values. No bound on the sum of `row_mask` on one device may be relied on, other than what follows from the above.
Results may differ from the reference program's by a relative error of at most 0.0057.
Values may be sent and summed in bfloat16 or wider, within the bound.
No kernel may reach another device: no remote copies, remote signals or barrier semaphores. Data moves between devices by JAX's collectives and lax.ppermute only.
A program may use at most 64 MiB of HBM per device.

```python
import jax
import jax.numpy as jnp
from jax import lax

C = 192
R = 48
OFFSETS = 27
BLOCK = 64
BLOCKS_DEV = 16
SPAN = 4
CAP = 8
NEAR = 8
ROWS_DEV = 1024
TOTAL = 65536
N_LEAF = 64


def peer_layout(shape):
    target = lax.broadcasted_iota(jnp.int32, shape, 0)
    slot = lax.broadcasted_iota(jnp.int32, shape, 1)
    delta = jnp.where(slot < SPAN, slot - SPAN, slot - SPAN + 1)
    owner = target + delta
    valid = (owner >= 0) & (owner < N_LEAF)
    return (target, slot, owner, valid)


def pair_counts(key):
    counts = jax.random.randint(key, (N_LEAF, NEAR), 0, CAP + 1)
    target, slot, owner, valid = peer_layout((N_LEAF, NEAR))
    forced = jnp.where(target < N_LEAF - 1, slot == SPAN, slot == SPAN - 1)
    counts = jnp.where(forced, CAP, counts)
    return jnp.where(valid, counts, 0)


def draw_halo_blocks(key, part):
    key = jax.random.fold_in(key, 11)
    first = jax.random.randint(key, (N_LEAF, NEAR, 1), 0, BLOCKS_DEV - CAP + 1)
    target, slot, owner, valid = peer_layout((N_LEAF, NEAR, 1))
    first = jnp.where((target == N_LEAF - 2) & (slot == SPAN), BLOCKS_DEV - CAP, first)
    slots = lax.broadcasted_iota(jnp.int32, (N_LEAF, NEAR, CAP), 2)
    blocks = owner * BLOCKS_DEV + first + slots
    return jnp.where(valid, blocks, -1).astype(jnp.int32)


def draw_neighbours(key, part):
    counts = pair_counts(key)
    key = jax.random.fold_in(key, 12)
    keys = jax.random.split(key, 5)
    shape = (OFFSETS, TOTAL)
    row = lax.broadcasted_iota(jnp.int32, shape, 1)
    offset = lax.broadcasted_iota(jnp.int32, shape, 0)
    device = row // ROWS_DEV
    inner = row % ROWS_DEV
    kind = jax.random.randint(keys[0], shape, 0, 100)
    delta = jax.random.randint(keys[1], shape, -96, 97)
    own = jnp.clip(inner + delta, 0, ROWS_DEV - 1)
    peer = jax.random.randint(keys[2], shape, 0, NEAR)
    slot = jax.random.randint(keys[3], shape, 0, CAP)
    octant = jax.random.randint(keys[4], shape, 0, BLOCK)
    have = counts[device, peer]
    fallback = jnp.where(device < N_LEAF - 1, SPAN, SPAN - 1)
    peer_used = jnp.where(have > 0, peer, fallback)
    have_used = jnp.where(have > 0, have, CAP)
    far = ROWS_DEV + (peer_used * CAP + slot % have_used) * BLOCK + octant
    value = jnp.where(kind < 10, -1, jnp.where(kind < 65, own, far))
    value = jnp.where(offset == 13, inner, value)
    value = jnp.where((offset == 0) & (row == 0), -1, value)
    value = jnp.where((offset == 1) & (row == 0), ROWS_DEV + NEAR * CAP * BLOCK - 1, value)
    return value.astype(jnp.int32)


def touch_ends(array, own_key, low, top_value):
    longest = array.shape.index(max(array.shape))
    spots = []
    for shift in (0, 1):
        where = [jax.random.randint(jax.random.fold_in(own_key, axis), (), 0, length) for axis, length in enumerate(array.shape)]
        where[longest] = (where[longest] + shift) % array.shape[longest]
        spots.append(tuple(where))
    return array.at[spots[0]].set(low).at[spots[1]].set(top_value)


def steps_of(key, extent, cuts, least, high):
    def one(dim, parts):
        draws = jax.random.uniform(jax.random.fold_in(jax.random.fold_in(key, 6), dim), (parts,), jnp.float32, least / len(cuts), high / len(cuts))
        return jnp.repeat(jnp.exp(draws), extent[dim] // parts).reshape((-1,) + (1,) * (len(extent) - dim - 1))

    gain = one(*cuts[0])
    for cut in cuts[1:]:
        gain = gain * one(*cut)
    return gain


def scatter_about(own_key, dims, deviation, most, pieces=(), kind=jnp.bfloat16):
    values = deviation * jax.random.normal(own_key, dims, jnp.float32)
    if pieces:
        values = values * steps_of(own_key, dims, pieces, -0.22, 0.18)
    return jnp.clip(values, -most, most).astype(kind)


def setup_inputs(seed: int = 0) -> dict:
    key_of = jax.random.split(jax.random.key(seed), 9)
    features = scatter_about(key_of[0], (C, TOTAL), 1.0, 6.0, ((0, 4), (1, 64)))
    in_factor = scatter_about(key_of[1], (C, R), C ** -0.5, 0.4375, ((0, 4),))
    core = scatter_about(key_of[2], (OFFSETS, R, R), (OFFSETS * R) ** -0.5, 0.15625, ((1, 4),))
    out_factor = scatter_about(key_of[3], (R, C), R ** -0.5, 0.875, ((1, 4),))
    neighbours = draw_neighbours(jax.random.fold_in(key_of[8], 71), 0)
    halo_blocks = draw_halo_blocks(jax.random.fold_in(key_of[8], 71), 0)
    row_mask = touch_ends((jax.random.randint(key_of[6], (TOTAL,), 0, 8) < 7).astype(jnp.int32), jax.random.fold_in(key_of[6], 1), 0, 1)
    cotangent = scatter_about(key_of[7], (C, TOTAL), 1.0, 6.0, ((0, 4), (1, 64)))
    return {"features": features, "in_factor": in_factor, "core": core, "out_factor": out_factor, "neighbours": neighbours, "halo_blocks": halo_blocks, "row_mask": row_mask, "cotangent": cotangent}


def reference(features, in_factor, core, out_factor, neighbours, halo_blocks, row_mask, cotangent):
    keep_rows = row_mask.astype(jnp.float32)[:, None]
    reduced = (jnp.dot(features.T, in_factor, preferred_element_type=jnp.float32) * keep_rows).astype(jnp.bfloat16)
    core_flat = core.astype(jnp.float32).reshape(OFFSETS * R, R)
    scale = float(TOTAL) ** -0.5

    def device_step(carry, device):
        grad_sum, grad_right, grad_reduced = carry
        start = (device * ROWS_DEV).astype(jnp.int32)
        entries = lax.dynamic_slice_in_dim(neighbours, start, ROWS_DEV, 1)
        present = entries >= 0
        far_index = entries - ROWS_DEV
        source_peer = jnp.clip(far_index // (CAP * BLOCK), 0, NEAR - 1)
        source_slot = jnp.clip((far_index // BLOCK) % CAP, 0, CAP - 1)
        owner_blocks = halo_blocks[device]
        far_rows = owner_blocks[source_peer, source_slot] * BLOCK + far_index % BLOCK
        source = jnp.where(entries < ROWS_DEV, start + entries, far_rows)
        source = jnp.where(present, source, 0).astype(jnp.int32)
        gathered = jnp.where(present[:, :, None], reduced[source], jnp.zeros((), jnp.bfloat16))
        flat = jnp.transpose(gathered, (1, 0, 2)).reshape(ROWS_DEV, OFFSETS * R).astype(jnp.float32)
        mixed = jnp.dot(flat, core_flat).astype(jnp.bfloat16)
        output_rows = jnp.dot(mixed, out_factor, preferred_element_type=jnp.float32).astype(jnp.bfloat16)
        cot_rows = lax.dynamic_slice_in_dim(cotangent, start, ROWS_DEV, 1).T
        grad_mixed = jnp.dot(cot_rows, out_factor.T, preferred_element_type=jnp.float32).astype(jnp.bfloat16)
        grad_right = grad_right + jnp.dot(mixed.T, cot_rows, preferred_element_type=jnp.float32)
        grad_sum = grad_sum + jnp.dot(flat.T, grad_mixed.astype(jnp.float32))
        grad_flat = jnp.dot(grad_mixed.astype(jnp.float32), core_flat.T).reshape(ROWS_DEV, OFFSETS, R)
        grad_flat = jnp.where(jnp.transpose(present)[:, :, None], grad_flat, jnp.zeros((), jnp.float32))
        grad_reduced = grad_reduced.at[jnp.transpose(source).reshape(-1)].add(grad_flat.reshape(-1, R))
        return (grad_sum, grad_right, grad_reduced), output_rows

    init = (jnp.zeros((OFFSETS * R, R), jnp.float32), jnp.zeros((R, C), jnp.float32), jnp.zeros((TOTAL, R), jnp.float32))
    (grad_sum, grad_right, grad_reduced), outputs = lax.scan(device_step, init, jnp.arange(N_LEAF, dtype=jnp.int32))
    output = outputs.reshape(TOTAL, C).T
    reduced_grad = (grad_reduced * keep_rows).astype(jnp.bfloat16)
    grad_features = jnp.dot(in_factor, reduced_grad.T, preferred_element_type=jnp.float32).astype(jnp.bfloat16)
    grad_in = jnp.dot(features, reduced_grad, preferred_element_type=jnp.float32)
    return (output, grad_features, grad_in * scale, grad_sum.reshape(OFFSETS, R, R) * scale, grad_right * scale)
```

```python
import jax
import jax.numpy as jnp
from jax import lax
from jax.experimental import pallas as pl
from jax.experimental.pallas import tpu as pltpu
from jax.sharding import PartitionSpec as P

BF = jnp.bfloat16
F32 = jnp.float32
LOW = 256
SLAB = 16
VMEM = pl.BlockSpec(memory_space=pltpu.VMEM)
SMEM = pl.BlockSpec(memory_space=pltpu.SMEM)
ROOMY = pltpu.CompilerParams(vmem_limit_bytes=40 * 2**20)


def dot(a, b, contract=((1,), (0,))):
    return lax.dot_general(a, b, (contract, ((), ())), preferred_element_type=F32)


NT = ((1,), (1,))
TN = ((0,), (0,))


def rank_picker(shape, slab_dim, group, group_count, width, sign):
    padded = lax.broadcasted_iota(jnp.int32, shape, slab_dim)
    rank = lax.broadcasted_iota(jnp.int32, shape, 1 - slab_dim)
    step = padded // SLAB
    lane = padded % SLAB
    slab = lax.rem(group + sign * step + group_count, group_count)
    hit = (rank == slab * width + lane) & (lane < width)
    return jnp.where(hit, 1.0, 0.0).astype(BF)


def project_kernel(group_ref, feat_ref, in_ref, cot_ref, outf_ref, *payload_refs):
    group_count = len(payload_refs)
    rank = in_ref.shape[1]
    width = rank // group_count
    pick = rank_picker((group_count * SLAB, rank), 0, group_ref[0], group_count, width, 1)
    weights = dot(pick, in_ref[...], NT).astype(BF)
    reduced = dot(weights, feat_ref[...]).astype(BF)
    grad_mixed = dot(outf_ref[...], cot_ref[...]).astype(BF)
    for j in range(group_count):
        payload_refs[j][0:SLAB, :] = reduced[j * SLAB : (j + 1) * SLAB]
        payload_refs[j][SLAB:, :] = grad_mixed


def low_onehot(low):
    shape = (LOW, low.shape[1])
    want = jnp.broadcast_to(low.astype(F32), shape).astype(BF)
    have = lax.broadcasted_iota(jnp.int32, shape, 0).astype(F32).astype(BF)
    return jnp.where(have == want, jnp.ones((), BF), jnp.zeros((), BF))


def scatter_kernel(halo_ref, p0, p1, p2, p3, core_ref, nbr_ref, gm_ref, own_ref, left_ref, right_ref,
                   far_left_ref, far_right_ref, terms_ref, acc_ref):
    rows = nbr_ref.shape[1]
    tiles = acc_ref.shape[0] // SLAB
    total = (p0[SLAB:, :].astype(F32) + p1[SLAB:, :].astype(F32)) + (
        p2[SLAB:, :].astype(F32) + p3[SLAB:, :].astype(F32)
    )
    grad_mixed = total.astype(BF)
    gm_ref[...] = grad_mixed
    terms_ref[...] = dot(core_ref[...], grad_mixed).astype(BF)
    acc_ref[...] = jnp.zeros_like(acc_ref)

    def step(k, carry):
        index = nbr_ref[pl.ds(k, 1), :]
        onehot = low_onehot(index & (LOW - 1))
        high = jnp.broadcast_to((index >> 8).astype(F32), (SLAB, rows)).astype(BF)
        terms = terms_ref[pl.ds(pl.multiple_of(k * SLAB, SLAB), SLAB), :]
        spread = jnp.concatenate(
            [jnp.where(high == jnp.full((), t, BF), terms, jnp.zeros((), BF)) for t in range(tiles)], 0
        )
        acc_ref[...] += dot(spread, onehot, NT)
        return carry

    lax.fori_loop(0, nbr_ref.shape[0], step, 0, unroll=9)

    def tile(t):
        return acc_ref[t * SLAB : (t + 1) * SLAB, :]

    own_tiles = rows // LOW
    own_ref[...] = jnp.concatenate([tile(t) for t in range(own_tiles)], 1)
    near = halo_ref.shape[0]
    per_peer = (tiles - own_tiles) // near
    for s in range(near):
        first = jnp.clip(halo_ref[s, 0] & 15, 0, 8) * 64
        start = own_tiles + s * per_peer
        window = jnp.concatenate(
            [tile(start + i) for i in range(per_peer)]
            + [jnp.zeros((SLAB, rows - per_peer * LOW), F32)],
            1,
        )
        block = pltpu.roll(window, first, 1).astype(BF)
        if s < 3:
            far_left_ref[s * SLAB : (s + 1) * SLAB, :] = block
        elif s == 3:
            left_ref[...] = block
        elif s == 4:
            right_ref[...] = block
        else:
            far_right_ref[(s - 5) * SLAB : (s - 4) * SLAB, :] = block


def gather_kernel(halo_ref, own_ref, u_ref, v_ref, p_ref, q_ref, gm_ref, core_ref, nbr_ref,
                  mix_ref, gc_ref, table_ref, ga_ref):
    rows = nbr_ref.shape[1]
    tiles = table_ref.shape[0] // SLAB
    own_tiles = rows // LOW
    near = halo_ref.shape[0]
    per_peer = (tiles - own_tiles) // near
    for t in range(own_tiles):
        table_ref[t * SLAB : (t + 1) * SLAB, :] = own_ref[:, t * LOW : (t + 1) * LOW]
    for s in range(near):
        if s < 3:
            block = p_ref[s * SLAB : (s + 1) * SLAB, :]
        elif s == 3:
            block = u_ref[...]
        elif s == 4:
            block = v_ref[...]
        else:
            block = q_ref[(s - 5) * SLAB : (s - 4) * SLAB, :]
        first = jnp.clip(halo_ref[s, 0] & 15, 0, 8) * 64
        window = pltpu.roll(block.astype(F32), rows - first, 1).astype(BF)
        for i in range(per_peer):
            t = own_tiles + s * per_peer + i
            table_ref[t * SLAB : (t + 1) * SLAB, :] = window[:, i * LOW : (i + 1) * LOW]

    def step(k, carry):
        index = nbr_ref[pl.ds(k, 1), :]
        onehot = low_onehot(index & (LOW - 1))
        high = jnp.broadcast_to(index >> 8, (SLAB, rows))
        picked = dot(table_ref[...], onehot)
        found = jnp.zeros((SLAB, rows), F32)
        for t in range(tiles):
            found = jnp.where(high == t, picked[t * SLAB : (t + 1) * SLAB], found)
        ga_ref[pl.ds(pl.multiple_of(k * SLAB, SLAB), SLAB), :] = found.astype(BF)
        return carry

    lax.fori_loop(0, nbr_ref.shape[0], step, 0, unroll=9)
    gathered = ga_ref[...]
    mix_ref[...] = dot(core_ref[...], gathered, TN).astype(BF)
    gc_ref[...] = dot(gm_ref[...], gathered, NT)


def output_kernel(m0, m1, m2, m3, outf_ref, mixed_ref, out_ref):
    total = (m0[...].astype(F32) + m1[...].astype(F32)) + (m2[...].astype(F32) + m3[...].astype(F32))
    mixed = total.astype(BF)
    mixed_ref[...] = mixed
    out_ref[...] = dot(outf_ref[...], mixed, TN).astype(BF)


def gradient_kernel(group_ref, g0, g1, g2, g3, in_ref, feat_ref, mixed_ref, cot_ref, gc_ref,
                    gf_ref, packed_ref):
    rank = in_ref.shape[1]
    rows = feat_ref.shape[1]
    pick = rank_picker((rank, 4 * SLAB), 1, group_ref[0], 4, rank // 4, -1)
    slabs = jnp.concatenate([g0[...], g1[...], g2[...], g3[...]], 0)
    grad_rows = dot(pick, slabs).astype(BF)
    gf_ref[...] = dot(in_ref[...], grad_rows).astype(BF)
    wide = gc_ref.shape[1]
    right = jnp.concatenate([cot_ref[...], jnp.zeros((80, rows), BF)], 0)
    left = jnp.concatenate([jnp.zeros((64, rows), BF), grad_rows, jnp.zeros((16, rows), BF)], 0)
    packed_ref[:, 0:128] = dot(mixed_ref[...], right, NT) + dot(feat_ref[...], left, NT)
    packed_ref[:, 128 : 128 + wide] = gc_ref[...]
    packed_ref[:, 128 + wide :] = jnp.zeros_like(packed_ref[:, 128 + wide :])


def unpack_kernel(factor, packed_ref, left_ref, core_ref, right_ref):
    tail = packed_ref[:, 0:128] * factor
    right_ref[...] = tail[:, 0:48]
    left_ref[...] = tail[:, 64:112]
    flat = (packed_ref[:, 128:] * factor).T
    for k in range(core_ref.shape[0]):
        core_ref[k] = flat[k * SLAB : k * SLAB + core_ref.shape[1], :]


def shifted(block, axis, distance):
    count = lax.axis_size(axis)
    return lax.ppermute(block, axis, [(i, (i + distance) % count) for i in range(count)])


def leaf_sum(total):
    for bit in (1, 2, 4, 8, 16, 32):
        total = total + lax.ppermute(total, "leaf", [(i, i ^ bit) for i in range(lax.axis_size("leaf"))])
    return total


def struct(shape, dtype):
    return jax.ShapeDtypeStruct(shape, dtype)


def body(features, in_factor, core, out_factor, neighbours, halo_blocks, row_mask, cotangent):
    channels, rows = features.shape
    offsets, width, rank = core.shape
    near, slots = halo_blocks.shape[1:]
    table_rows = (rows + near * slots * 64) // LOW * SLAB
    group = lax.axis_index("chan").astype(jnp.int32).reshape(1)
    keep = row_mask.astype(F32).reshape(1, rows)
    halo = halo_blocks[0]
    core_rows = jnp.pad(core, ((0, 0), (0, SLAB - width), (0, 0))).reshape(offsets * SLAB, rank)

    payload = pl.pallas_call(
        project_kernel,
        out_shape=[struct((SLAB + rank, rows), BF)] * 4,
        in_specs=[SMEM] + [VMEM] * 4,
        out_specs=[VMEM] * 4,
        name="project",
    )(group, features, in_factor, cotangent, out_factor)
    parts = [payload[0]] + [shifted(payload[j], "chan", j) for j in (1, 2, 3)]
    reduced = sum(part[:SLAB].astype(F32) for part in parts) * keep
    reduced = reduced.astype(BF)

    from_left = shifted(reduced, "leaf", 1)
    from_right = shifted(reduced, "leaf", -1)
    bundle = jnp.concatenate([from_left, reduced, from_right], 0)
    far_from_left = shifted(bundle, "leaf", 3)
    far_from_right = shifted(bundle, "leaf", -3)

    slab = struct((SLAB, rows), BF)
    triple = struct((3 * SLAB, rows), BF)
    grad_mixed, own, to_left, to_right, far_left, far_right = pl.pallas_call(
        scatter_kernel,
        out_shape=[struct((rank, rows), BF), struct((SLAB, rows), F32), slab, slab, triple, triple],
        in_specs=[SMEM] + [VMEM] * 6,
        out_specs=[VMEM] * 6,
        scratch_shapes=[pltpu.VMEM((offsets * SLAB, rows), BF), pltpu.VMEM((table_rows, LOW), F32)],
        compiler_params=ROOMY,
        cost_estimate=pl.CostEstimate(flops=5 * 10**9, bytes_accessed=2**20, transcendentals=0),
        name="scatter",
    )(halo, *parts, core_rows, neighbours)

    back_right = shifted(far_left, "leaf", -3)
    back_left = shifted(far_right, "leaf", 3)
    back = back_right.astype(F32) + back_left.astype(F32)
    near_left = shifted((to_left.astype(F32) + back[:SLAB]).astype(BF), "leaf", -1)
    near_right = shifted((to_right.astype(F32) + back[2 * SLAB :]).astype(BF), "leaf", 1)

    mixed_part, grad_core = pl.pallas_call(
        gather_kernel,
        out_shape=[struct((rank, rows), BF), struct((rank, offsets * SLAB), F32)],
        in_specs=[SMEM] + [VMEM] * 8,
        out_specs=[VMEM] * 2,
        scratch_shapes=[pltpu.VMEM((table_rows, LOW), BF), pltpu.VMEM((offsets * SLAB, rows), BF)],
        compiler_params=ROOMY,
        cost_estimate=pl.CostEstimate(flops=5 * 10**9, bytes_accessed=2**20, transcendentals=0),
        name="gather",
    )(halo, reduced, from_left, from_right, far_from_left, far_from_right, grad_mixed, core_rows, neighbours)
    mixed_parts = [mixed_part] + [shifted(mixed_part, "chan", j) for j in (1, 2, 3)]

    grad_slab = own + back[SLAB : 2 * SLAB] + near_left.astype(F32) + near_right.astype(F32)
    grad_slab = (grad_slab * keep).astype(BF)
    slabs = [grad_slab] + [shifted(grad_slab, "chan", j) for j in (1, 2, 3)]

    mixed, output = pl.pallas_call(
        output_kernel,
        out_shape=[struct((rank, rows), BF), struct((channels, rows), BF)],
        in_specs=[VMEM] * 5,
        out_specs=[VMEM] * 2,
        name="output",
    )(*mixed_parts, out_factor)

    packed_width = 128 + (offsets * SLAB + 127) // 128 * 128
    grad_features, packed = pl.pallas_call(
        gradient_kernel,
        out_shape=[struct((channels, rows), BF), struct((rank, packed_width), F32)],
        in_specs=[SMEM] + [VMEM] * 9,
        out_specs=[VMEM] * 2,
        name="gradient",
    )(group, *slabs, in_factor, features, mixed, cotangent, grad_core)
    packed = leaf_sum(packed)

    factor = float(rows * lax.axis_size("leaf")) ** (-0.5)
    grad_in, grad_core, grad_out = pl.pallas_call(
        lambda *refs: unpack_kernel(factor, *refs),
        out_shape=[struct((channels, rank), F32), struct((offsets, width, rank), F32), struct((rank, channels), F32)],
        in_specs=[VMEM],
        out_specs=[VMEM] * 3,
        name="unpack",
    )(packed)
    return (output, grad_features, grad_in, grad_core, grad_out)


def solution(mesh):
    placed = (
        P("chan", "leaf"),
        P("chan", None),
        P(None, "chan", None),
        P(None, "chan"),
        P(None, "leaf"),
        P("leaf", None, None),
        P("leaf"),
        P("chan", "leaf"),
    )
    return jax.shard_map(
        body,
        mesh=mesh,
        in_specs=placed,
        out_specs=(
            P("chan", "leaf"),
            P("chan", "leaf"),
            P("chan", None),
            P(None, "chan", None),
            P(None, "chan"),
        ),
        check_vma=False,
    )
```

```python
import jax
import jax.numpy as jnp
from jax import lax
from jax.experimental import pallas as pl
from jax.experimental.pallas import tpu as pltpu
from jax.sharding import PartitionSpec as P

BF = jnp.bfloat16
F32 = jnp.float32
LOW = 256
SLAB = 16
VMEM = pl.BlockSpec(memory_space=pltpu.VMEM)
SMEM = pl.BlockSpec(memory_space=pltpu.SMEM)
ROOMY = pltpu.CompilerParams(vmem_limit_bytes=40 * 2**20)


def dot(a, b, contract=((1,), (0,))):
    return lax.dot_general(a, b, (contract, ((), ())), preferred_element_type=F32)


NT = ((1,), (1,))
TN = ((0,), (0,))


def rank_picker(shape, slab_dim, group, group_count, width, sign):
    padded = lax.broadcasted_iota(jnp.int32, shape, slab_dim)
    rank = lax.broadcasted_iota(jnp.int32, shape, 1 - slab_dim)
    step = padded // SLAB
    lane = padded % SLAB
    slab = lax.rem(group + sign * step + group_count, group_count)
    hit = (rank == slab * width + lane) & (lane < width)
    return jnp.where(hit, 1.0, 0.0).astype(BF)


def project_kernel(place_ref, feat_ref, in_ref, cot_ref, outf_ref, *payload_refs):
    group_count = len(payload_refs)
    rank = in_ref.shape[1]
    width = rank // group_count
    pick = rank_picker((group_count * SLAB, rank), 0, place_ref[0], group_count, width, 1)
    weights = dot(pick, in_ref[...], NT).astype(BF)
    reduced = dot(weights, feat_ref[...])
    grad_mixed = dot(outf_ref[...], cot_ref[...])
    for j in range(group_count):
        payload_refs[j][0:SLAB, :] = reduced[j * SLAB : (j + 1) * SLAB].astype(payload_refs[j].dtype)
        payload_refs[j][SLAB:, :] = grad_mixed.astype(payload_refs[j].dtype)


def low_onehot(low):
    shape = (LOW, low.shape[1])
    want = jnp.broadcast_to(low.astype(F32), shape).astype(BF)
    have = lax.broadcasted_iota(jnp.int32, shape, 0).astype(F32).astype(BF)
    return jnp.where(have == want, jnp.ones((), BF), jnp.zeros((), BF))


def first_octant(halo_ref, slot):
    return jnp.clip(halo_ref[slot, 0] & 15, 0, 8) * 64


def mirrored(core, view, near):
    return jnp.where(core == 0, view, near - 1 - view)


def scatter_kernel(place_ref, halo_ref, p0, p1, p2, p3, core_ref, nbr_ref, gm_ref, own_ref, kept_ref,
                   cross_ref, terms_ref, acc_ref):
    rows = nbr_ref.shape[1]
    tiles = acc_ref.shape[0] // SLAB
    total = (p0[SLAB:, :] + p1[SLAB:, :].astype(F32)) + (
        p2[SLAB:, :].astype(F32) + p3[SLAB:, :].astype(F32)
    )
    grad_mixed = total.astype(BF)
    gm_ref[...] = grad_mixed
    terms_ref[...] = dot(core_ref[...], grad_mixed).astype(BF)
    acc_ref[...] = jnp.zeros_like(acc_ref)

    def step(k, carry):
        index = nbr_ref[pl.ds(k, 1), :]
        onehot = low_onehot(index & (LOW - 1))
        high = jnp.broadcast_to((index >> 8).astype(F32), (SLAB, rows)).astype(BF)
        terms = terms_ref[pl.ds(pl.multiple_of(k * SLAB, SLAB), SLAB), :]
        spread = jnp.concatenate(
            [jnp.where(high == jnp.full((), t, BF), terms, jnp.zeros((), BF)) for t in range(tiles)], 0
        )
        acc_ref[...] += dot(spread, onehot, NT)
        return carry

    lax.fori_loop(0, nbr_ref.shape[0], step, 0, unroll=9)

    def tile(t):
        return acc_ref[pl.ds(pl.multiple_of(t * SLAB, SLAB), SLAB), :]

    own_tiles = rows // LOW
    own_ref[...] = jnp.concatenate([tile(t) for t in range(own_tiles)], 1)
    near = halo_ref.shape[0]
    per_peer = (tiles - own_tiles) // near
    blank = jnp.zeros((SLAB, rows - per_peer * LOW), F32)
    for view in range(near):
        slot = mirrored(place_ref[1], view, near)
        start = own_tiles + slot * per_peer
        window = jnp.concatenate([tile(start + i) for i in range(per_peer)] + [blank], 1)
        block = pltpu.roll(window, first_octant(halo_ref, slot), 1)
        if view < 4:
            kept_ref[view * SLAB : (view + 1) * SLAB, :] = block
        else:
            cross_ref[(view - 4) * SLAB : (view - 3) * SLAB, :] = block.astype(BF)


def gather_kernel(place_ref, halo_ref, own_ref, pair_ref, near_ref, far_ref, cross_ref, gm_ref, core_ref,
                  nbr_ref, mix_ref, gc_ref, table_ref, ga_ref):
    rows = nbr_ref.shape[1]
    tiles = table_ref.shape[0] // SLAB
    own_tiles = rows // LOW
    near = halo_ref.shape[0]
    per_peer = (tiles - own_tiles) // near
    for t in range(own_tiles):
        table_ref[t * SLAB : (t + 1) * SLAB, :] = own_ref[:, t * LOW : (t + 1) * LOW]
    views = (
        far_ref[0:SLAB, :],
        far_ref[SLAB:, :],
        near_ref[0:SLAB, :],
        near_ref[SLAB:, :],
        pair_ref[...],
        cross_ref[SLAB : 2 * SLAB, :],
        cross_ref[0:SLAB, :],
        cross_ref[3 * SLAB :, :],
    )
    for view in range(near):
        slot = mirrored(place_ref[1], view, near)
        window = pltpu.roll(views[view].astype(F32), rows - first_octant(halo_ref, slot), 1).astype(BF)
        for i in range(per_peer):
            t = own_tiles + slot * per_peer + i
            table_ref[pl.ds(pl.multiple_of(t * SLAB, SLAB), SLAB), :] = window[:, i * LOW : (i + 1) * LOW]

    def step(k, carry):
        index = nbr_ref[pl.ds(k, 1), :]
        onehot = low_onehot(index & (LOW - 1))
        high = jnp.broadcast_to(index >> 8, (SLAB, rows))
        picked = dot(table_ref[...], onehot)
        found = jnp.zeros((SLAB, rows), F32)
        for t in range(tiles):
            found = jnp.where(high == t, picked[t * SLAB : (t + 1) * SLAB], found)
        ga_ref[pl.ds(pl.multiple_of(k * SLAB, SLAB), SLAB), :] = found.astype(BF)
        return carry

    lax.fori_loop(0, nbr_ref.shape[0], step, 0, unroll=9)
    gathered = ga_ref[...]
    mix_ref[...] = dot(core_ref[...], gathered, TN)
    gc_ref[...] = dot(gm_ref[...], gathered, NT)


def finish_kernel(place_ref, mix_ref, e0, e1, e2, e3, in_ref, feat_ref, outf_ref, cot_ref, gc_ref,
                  gf_ref, out_ref, packed_ref):
    rank = in_ref.shape[1]
    rows = feat_ref.shape[1]
    pick = rank_picker((rank, 4 * SLAB), 1, place_ref[0], 4, rank // 4, -1)
    slabs = jnp.concatenate([e[0:SLAB, :] for e in (e0, e1, e2, e3)], 0)
    grad_rows = dot(pick, slabs).astype(BF)
    gf_ref[...] = dot(in_ref[...], grad_rows).astype(BF)
    total = (mix_ref[...] + e1[SLAB:, :].astype(F32)) + (e2[SLAB:, :].astype(F32) + e3[SLAB:, :].astype(F32))
    mixed = total.astype(BF)
    out_ref[...] = dot(outf_ref[...], mixed, TN).astype(BF)
    wide = gc_ref.shape[1]
    right = jnp.concatenate([cot_ref[...], jnp.zeros((80, rows), BF)], 0)
    left = jnp.concatenate([jnp.zeros((64, rows), BF), grad_rows, jnp.zeros((16, rows), BF)], 0)
    packed_ref[:, 0:128] = dot(mixed, right, NT) + dot(feat_ref[...], left, NT)
    packed_ref[:, 128 : 128 + wide] = gc_ref[...]
    packed_ref[:, 128 + wide :] = jnp.zeros_like(packed_ref[:, 128 + wide :])


def unpack_kernel(factor, packed_ref, left_ref, core_ref, right_ref, flat_ref):
    tail = packed_ref[:, 0:128] * factor
    right_ref[...] = tail[:, 0:48]
    left_ref[...] = tail[:, 64:112]
    flat_ref[...] = (packed_ref[:, 128:] * factor).T
    width, offsets, rank = core_ref.shape
    for c in range(width):
        core_ref[c] = flat_ref[pl.ds(c, offsets, stride=SLAB), :]


def shifted(block, axis, distance):
    count = lax.axis_size(axis)
    return lax.ppermute(block, axis, [(i, (i + distance) % count) for i in range(count)])


def crossed(block, mask):
    return lax.ppermute(block, "leaf", [(i, i ^ mask) for i in range(lax.axis_size("leaf"))])


def outward(block, chips):
    count = lax.axis_size("leaf")
    return lax.ppermute(
        block, "leaf", [(i, (i + (2 * chips if i % 2 == 0 else -2 * chips)) % count) for i in range(count)]
    )


def leaf_sum(total, core):
    half = total.shape[0] // 2
    low, high = total[:half], total[half:]
    mine = jnp.where(core == 0, low, high) + crossed(jnp.where(core == 0, high, low), 1)
    for masks in ((8,), (2, 4, 6), (16, 32, 48)):
        mine = mine + sum(crossed(mine, mask) for mask in masks)
    other = crossed(mine, 1)
    return jnp.concatenate([jnp.where(core == 0, mine, other), jnp.where(core == 0, other, mine)], 0)


def struct(shape, dtype):
    return jax.ShapeDtypeStruct(shape, dtype)


def body(features, in_factor, core, out_factor, neighbours, halo_blocks, row_mask, cotangent):
    channels, rows = features.shape
    offsets, width, rank = core.shape
    near, slots = halo_blocks.shape[1:]
    table_rows = (rows + near * slots * 64) // LOW * SLAB
    core_bit = lax.axis_index("leaf") % 2
    place = jnp.stack([lax.axis_index("chan"), core_bit]).astype(jnp.int32)
    keep = row_mask.astype(F32).reshape(1, rows)
    halo = halo_blocks[0]
    core_rows = jnp.pad(core, ((0, 0), (0, SLAB - width), (0, 0))).reshape(offsets * SLAB, rank)
    estimate = pl.CostEstimate(flops=5 * 10**9, bytes_accessed=2**20, transcendentals=0)

    payload = pl.pallas_call(
        project_kernel,
        out_shape=[struct((SLAB + rank, rows), F32)] + [struct((SLAB + rank, rows), BF)] * 3,
        in_specs=[SMEM] + [VMEM] * 4,
        out_specs=[VMEM] * 4,
        name="project",
    )(place, features, in_factor, cotangent, out_factor)
    parts = [payload[0]] + [shifted(payload[j], "chan", j) for j in (1, 2, 3)]
    reduced = sum(part[:SLAB].astype(F32) for part in parts) * keep
    reduced = reduced.astype(BF)

    pair = crossed(reduced, 1)
    both, parts = lax.optimization_barrier((jnp.concatenate([reduced, pair], 0), parts))
    near_pair = outward(both, 1)
    far_pair = outward(both, 2)

    grad_mixed, own, kept, cross = pl.pallas_call(
        scatter_kernel,
        out_shape=[
            struct((rank, rows), BF),
            struct((SLAB, rows), F32),
            struct((4 * SLAB, rows), F32),
            struct((4 * SLAB, rows), BF),
        ],
        in_specs=[SMEM] * 2 + [VMEM] * 6,
        out_specs=[VMEM] * 4,
        scratch_shapes=[pltpu.VMEM((offsets * SLAB, rows), BF), pltpu.VMEM((table_rows, LOW), F32)],
        compiler_params=ROOMY,
        cost_estimate=estimate,
        name="scatter",
    )(place, halo, *parts, core_rows, neighbours)

    beyond = crossed(jnp.concatenate([near_pair, far_pair], 0), 1)
    handed = crossed(cross, 1).astype(F32)
    own = own + handed[:SLAB]
    to_near = jnp.concatenate(
        [kept[2 * SLAB : 3 * SLAB] + handed[2 * SLAB : 3 * SLAB], kept[3 * SLAB :] + handed[SLAB : 2 * SLAB]], 0
    ).astype(BF)
    to_far = jnp.concatenate([kept[:SLAB], kept[SLAB : 2 * SLAB] + handed[3 * SLAB :]], 0).astype(BF)
    beyond, to_near, to_far = lax.optimization_barrier((beyond, to_near, to_far))
    from_near = outward(to_near, -1).astype(F32)
    from_far = outward(to_far, -2).astype(F32)

    mixed_part, grad_core = pl.pallas_call(
        gather_kernel,
        out_shape=[struct((rank, rows), F32), struct((rank, offsets * SLAB), F32)],
        in_specs=[SMEM] * 2 + [VMEM] * 8,
        out_specs=[VMEM] * 2,
        scratch_shapes=[pltpu.VMEM((table_rows, LOW), BF), pltpu.VMEM((offsets * SLAB, rows), BF)],
        compiler_params=ROOMY,
        cost_estimate=estimate,
        name="gather",
    )(place, halo, reduced, pair, near_pair, far_pair, beyond, grad_mixed, core_rows, neighbours)

    returned = from_near + from_far
    last = crossed(returned[SLAB:].astype(BF), 1).astype(F32)
    grad_slab = ((own + returned[:SLAB] + last) * keep).astype(BF)
    shared = jnp.concatenate([grad_slab, mixed_part.astype(BF)], 0)
    exchanged = [shared] + [shifted(shared, "chan", j) for j in (1, 2, 3)]

    packed_width = 128 + (offsets * SLAB + 127) // 128 * 128
    grad_features, output, packed = pl.pallas_call(
        finish_kernel,
        out_shape=[struct((channels, rows), BF)] * 2 + [struct((rank, packed_width), F32)],
        in_specs=[SMEM] + [VMEM] * 10,
        out_specs=[VMEM] * 3,
        name="finish",
    )(place, mixed_part, *exchanged, in_factor, features, out_factor, cotangent, grad_core)
    packed = leaf_sum(packed, core_bit)

    factor = float(rows * lax.axis_size("leaf")) ** (-0.5)
    grad_in, grad_core, grad_out = pl.pallas_call(
        lambda *refs: unpack_kernel(factor, *refs),
        out_shape=[struct((channels, rank), F32), struct((width, offsets, rank), F32), struct((rank, channels), F32)],
        in_specs=[VMEM],
        out_specs=[VMEM] * 3,
        scratch_shapes=[pltpu.VMEM((packed_width - 128, rank), F32)],
        name="unpack",
    )(packed)
    return (output, grad_features, grad_in, jnp.transpose(grad_core, (1, 0, 2)), grad_out)


def solution(mesh):
    placed = (
        P("chan", "leaf"),
        P("chan", None),
        P(None, "chan", None),
        P(None, "chan"),
        P(None, "leaf"),
        P("leaf", None, None),
        P("leaf"),
        P("chan", "leaf"),
    )
    return jax.shard_map(
        body,
        mesh=mesh,
        in_specs=placed,
        out_specs=(
            P("chan", "leaf"),
            P("chan", "leaf"),
            P("chan", None),
            P(None, "chan", None),
            P(None, "chan"),
        ),
        check_vma=False,
    )
```

```python
import jax
import jax.numpy as jnp
from jax import lax
from jax.experimental import pallas as pl
from jax.experimental.pallas import tpu as pltpu
from jax.sharding import PartitionSpec as P

BF = jnp.bfloat16
F32 = jnp.float32
LOW = 256
SLAB = 16
VMEM = pl.BlockSpec(memory_space=pltpu.VMEM)
SMEM = pl.BlockSpec(memory_space=pltpu.SMEM)
ROOMY = pltpu.CompilerParams(vmem_limit_bytes=40 * 2**20)
SNUG = pltpu.CompilerParams(vmem_limit_bytes=12 * 2**20)


def dot(a, b, contract=((1,), (0,))):
    return lax.dot_general(a, b, (contract, ((), ())), preferred_element_type=F32)


NT = ((1,), (1,))
TN = ((0,), (0,))


def rank_picker(shape, slab_dim, group, group_count, width, sign):
    padded = lax.broadcasted_iota(jnp.int32, shape, slab_dim)
    rank = lax.broadcasted_iota(jnp.int32, shape, 1 - slab_dim)
    step = padded // SLAB
    lane = padded % SLAB
    slab = lax.rem(group + sign * step + group_count, group_count)
    hit = (rank == slab * width + lane) & (lane < width)
    return jnp.where(hit, 1.0, 0.0).astype(BF)


def project_kernel(feat_ref, in_ref, cot_ref, outf_ref, *payload_refs):
    group_count = len(payload_refs)
    rank = in_ref.shape[1]
    width = rank // group_count
    pick = rank_picker((group_count * SLAB, rank), 0, lax.axis_index("chan"), group_count, width, 1)
    weights = dot(pick, in_ref[...], NT).astype(BF)
    reduced = dot(weights, feat_ref[...])
    grad_mixed = dot(outf_ref[...], cot_ref[...])
    for j in range(group_count):
        payload_refs[j][0:SLAB, :] = reduced[j * SLAB : (j + 1) * SLAB].astype(payload_refs[j].dtype)
        payload_refs[j][SLAB:, :] = grad_mixed.astype(payload_refs[j].dtype)


def low_onehot(low):
    shape = (LOW, low.shape[1])
    want = jnp.broadcast_to(low.astype(F32), shape).astype(BF)
    have = lax.broadcasted_iota(jnp.int32, shape, 0).astype(F32).astype(BF)
    return jnp.where(have == want, jnp.ones((), BF), jnp.zeros((), BF))


def core_bit():
    return lax.axis_index("leaf") % 2


def first_octant(halo_ref, slot):
    return jnp.clip(halo_ref[slot, 0] & 15, 0, 8) * 64


def mirrored(core, view, near):
    return jnp.where(core == 0, view, near - 1 - view)


def scatter_kernel(halo_ref, p0, p1, p2, p3, core_ref, nbr_ref, gm_ref, own_ref, kept_ref,
                   cross_ref, terms_ref, acc_ref):
    rows = nbr_ref.shape[1]
    tiles = acc_ref.shape[0] // SLAB
    total = (p0[SLAB:, :] + p1[SLAB:, :].astype(F32)) + (
        p2[SLAB:, :].astype(F32) + p3[SLAB:, :].astype(F32)
    )
    grad_mixed = total.astype(BF)
    gm_ref[...] = grad_mixed
    terms_ref[...] = dot(core_ref[...], grad_mixed).astype(BF)
    acc_ref[...] = jnp.zeros_like(acc_ref)

    def step(k, carry):
        index = nbr_ref[pl.ds(k, 1), :]
        onehot = low_onehot(index & (LOW - 1))
        high = jnp.broadcast_to((index >> 8).astype(F32), (SLAB, rows)).astype(BF)
        terms = terms_ref[pl.ds(pl.multiple_of(k * SLAB, SLAB), SLAB), :]
        spread = jnp.concatenate(
            [jnp.where(high == jnp.full((), t, BF), terms, jnp.zeros((), BF)) for t in range(tiles)], 0
        )
        acc_ref[...] += dot(spread, onehot, NT)
        return carry

    lax.fori_loop(0, nbr_ref.shape[0], step, 0, unroll=9)

    def tile(t):
        return acc_ref[pl.ds(pl.multiple_of(t * SLAB, SLAB), SLAB), :]

    own_tiles = rows // LOW
    own_ref[...] = jnp.concatenate([tile(t) for t in range(own_tiles)], 1)
    near = halo_ref.shape[0]
    per_peer = (tiles - own_tiles) // near
    blank = jnp.zeros((SLAB, rows - per_peer * LOW), F32)
    for view in range(near):
        slot = mirrored(core_bit(), view, near)
        start = own_tiles + slot * per_peer
        window = jnp.concatenate([tile(start + i) for i in range(per_peer)] + [blank], 1)
        block = pltpu.roll(window, first_octant(halo_ref, slot), 1)
        if view < 4:
            kept_ref[view * SLAB : (view + 1) * SLAB, :] = block
        else:
            cross_ref[(view - 4) * SLAB : (view - 3) * SLAB, :] = block.astype(BF)


def gather_kernel(halo_ref, own_ref, pair_ref, near_ref, far_ref, cross_ref, gm_ref, core_ref,
                  nbr_ref, mix_ref, gc_ref, table_ref, ga_ref):
    rows = nbr_ref.shape[1]
    tiles = table_ref.shape[0] // SLAB
    own_tiles = rows // LOW
    near = halo_ref.shape[0]
    per_peer = (tiles - own_tiles) // near
    for t in range(own_tiles):
        table_ref[t * SLAB : (t + 1) * SLAB, :] = own_ref[:, t * LOW : (t + 1) * LOW]
    views = (
        far_ref[0:SLAB, :],
        far_ref[SLAB:, :],
        near_ref[0:SLAB, :],
        near_ref[SLAB:, :],
        pair_ref[...],
        cross_ref[SLAB : 2 * SLAB, :],
        cross_ref[0:SLAB, :],
        cross_ref[3 * SLAB :, :],
    )
    for view in range(near):
        slot = mirrored(core_bit(), view, near)
        window = pltpu.roll(views[view].astype(F32), rows - first_octant(halo_ref, slot), 1).astype(BF)
        for i in range(per_peer):
            t = own_tiles + slot * per_peer + i
            table_ref[pl.ds(pl.multiple_of(t * SLAB, SLAB), SLAB), :] = window[:, i * LOW : (i + 1) * LOW]

    def step(k, carry):
        index = nbr_ref[pl.ds(k, 1), :]
        onehot = low_onehot(index & (LOW - 1))
        high = jnp.broadcast_to(index >> 8, (SLAB, rows))
        picked = dot(table_ref[...], onehot)
        found = jnp.zeros((SLAB, rows), F32)
        for t in range(tiles):
            found = jnp.where(high == t, picked[t * SLAB : (t + 1) * SLAB], found)
        ga_ref[pl.ds(pl.multiple_of(k * SLAB, SLAB), SLAB), :] = found.astype(BF)
        return carry

    lax.fori_loop(0, nbr_ref.shape[0], step, 0, unroll=9)
    used = core_ref.shape[0]
    ga_ref[used:, :] = jnp.zeros_like(ga_ref[used:, :])
    mix_ref[...] = dot(core_ref[...], ga_ref[:used, :], TN)
    gc_ref[...] = dot(gm_ref[...], ga_ref[...], NT)


def finish_kernel(mix_ref, e0, e1, e2, e3, in_ref, feat_ref, outf_ref, cot_ref, gc_ref,
                  gf_ref, out_ref, keep_ref, give_ref):
    rank = in_ref.shape[1]
    rows = feat_ref.shape[1]
    wide = gc_ref.shape[1]
    group = lax.axis_index("chan")
    pick = rank_picker((rank, 4 * SLAB), 1, group, 4, rank // 4, -1)
    slabs = jnp.concatenate([e[0:SLAB, :] for e in (e0, e1, e2, e3)], 0)
    grad_rows = dot(pick, slabs).astype(BF)
    gf_ref[...] = dot(in_ref[...], grad_rows).astype(BF)
    total = (mix_ref[...] + e1[SLAB:, :].astype(F32)) + (e2[SLAB:, :].astype(F32) + e3[SLAB:, :].astype(F32))
    mixed = total.astype(BF)
    out_ref[...] = dot(outf_ref[...], mixed, TN).astype(BF)
    column = lax.broadcasted_iota(jnp.int32, (wide, rank), 0)
    wanted = lax.broadcasted_iota(jnp.int32, (wide, rank), 1)
    free = column % SLAB - (SLAB - 4)
    place = jnp.where((free >= 0) & (column // SLAB * 4 + free == wanted), 1.0, 0.0).astype(BF)
    spread = dot(place, grad_rows).astype(BF)
    right = jnp.concatenate([jnp.zeros((48, rows), BF), cot_ref[...], jnp.zeros((32, rows), BF)], 0)
    tail = dot(mixed, right, NT)
    packed = gc_ref[...] + dot(feat_ref[...], spread, NT)
    packed = jnp.concatenate([packed[:, : wide - 128], packed[:, wide - 128 :] + tail], 1)
    half = rank // 2
    first = core_bit() == 0
    keep_ref[...] = jnp.where(first, packed[:half], packed[half:])
    give_ref[...] = jnp.where(first, packed[half:], packed[:half])


def unpack_kernel(factor, mine_ref, other_ref, left_ref, core_ref, right_ref, flat_ref, turned_ref):
    width, offsets, rank = core_ref.shape
    mine, other = mine_ref[...] * factor, other_ref[...] * factor
    first = core_bit() == 0
    packed = jnp.concatenate([jnp.where(first, mine, other), jnp.where(first, other, mine)], 0)
    flat_ref[...] = packed.T
    for c in range(width):
        core_ref[c] = flat_ref[pl.ds(c, offsets, stride=SLAB), :]
    for j in range(4):
        turned_ref[pl.ds(j, rank // 4, stride=4), :] = flat_ref[pl.ds(width + j, rank // 4, stride=SLAB), :]
    left_ref[...] = turned_ref[...].T
    right_ref[...] = flat_ref[offsets * SLAB : offsets * SLAB + rank, :].T


def shifted(block, axis, distance):
    count = lax.axis_size(axis)
    return lax.ppermute(block, axis, [(i, (i + distance) % count) for i in range(count)])


def crossed(block, mask):
    return lax.ppermute(block, "leaf", [(i, i ^ mask) for i in range(lax.axis_size("leaf"))])


def outward(block, chips):
    count = lax.axis_size("leaf")
    return lax.ppermute(
        block, "leaf", [(i, (i + (2 * chips if i % 2 == 0 else -2 * chips)) % count) for i in range(count)]
    )


def leaf_sum(mine, give):
    mine = mine + crossed(give, 1)
    for masks in ((8,), (2, 4, 6), (16, 32, 48)):
        mine = mine + sum(crossed(mine, mask) for mask in masks)
    return mine, crossed(mine, 1)


def struct(shape, dtype):
    return jax.ShapeDtypeStruct(shape, dtype)


def body(features, in_factor, core, out_factor, neighbours, halo_blocks, row_mask, cotangent):
    channels, rows = features.shape
    offsets, width, rank = core.shape
    near, slots = halo_blocks.shape[1:]
    table_rows = (rows + near * slots * 64) // LOW * SLAB
    packed_width = (offsets * SLAB + 127) // 128 * 128
    keep = row_mask.astype(F32).reshape(1, rows)
    halo = halo_blocks[0]
    core_rows = jnp.pad(core, ((0, 0), (0, SLAB - width), (0, 0))).reshape(offsets * SLAB, rank)
    estimate = pl.CostEstimate(flops=5 * 10**9, bytes_accessed=2**20, transcendentals=0)

    payload = pl.pallas_call(
        project_kernel,
        out_shape=[struct((SLAB + rank, rows), F32)] + [struct((SLAB + rank, rows), BF)] * 3,
        in_specs=[VMEM] * 4,
        out_specs=[VMEM] * 4,
        name="project",
    )(features, in_factor, cotangent, out_factor)
    parts = [payload[0]] + [shifted(payload[j], "chan", j) for j in (1, 2, 3)]
    reduced = sum(part[:SLAB].astype(F32) for part in parts) * keep
    reduced = reduced.astype(BF)

    pair = crossed(reduced, 1)
    both, parts = lax.optimization_barrier((jnp.concatenate([reduced, pair], 0), parts))
    near_pair = outward(both, 1)
    far_pair = outward(both, 2)

    grad_mixed, own, kept, cross = pl.pallas_call(
        scatter_kernel,
        out_shape=[
            struct((rank, rows), BF),
            struct((SLAB, rows), F32),
            struct((4 * SLAB, rows), F32),
            struct((4 * SLAB, rows), BF),
        ],
        in_specs=[SMEM] + [VMEM] * 6,
        out_specs=[VMEM] * 4,
        scratch_shapes=[pltpu.VMEM((offsets * SLAB, rows), BF), pltpu.VMEM((table_rows, LOW), F32)],
        compiler_params=ROOMY,
        cost_estimate=estimate,
        name="scatter",
    )(halo, *parts, core_rows, neighbours)

    beyond = crossed(jnp.concatenate([near_pair, far_pair], 0), 1)
    handed = crossed(cross, 1).astype(F32)
    own = own + handed[:SLAB]
    to_near = jnp.concatenate(
        [kept[2 * SLAB : 3 * SLAB] + handed[2 * SLAB : 3 * SLAB], kept[3 * SLAB :] + handed[SLAB : 2 * SLAB]], 0
    ).astype(BF)
    to_far = jnp.concatenate([kept[:SLAB], kept[SLAB : 2 * SLAB] + handed[3 * SLAB :]], 0).astype(BF)
    beyond, to_near, to_far = lax.optimization_barrier((beyond, to_near, to_far))
    from_near = outward(to_near, -1)
    from_far = outward(to_far, -2)

    mixed_part, grad_core = pl.pallas_call(
        gather_kernel,
        out_shape=[struct((rank, rows), F32), struct((rank, packed_width), F32)],
        in_specs=[SMEM] + [VMEM] * 8,
        out_specs=[VMEM] * 2,
        scratch_shapes=[pltpu.VMEM((table_rows, LOW), BF), pltpu.VMEM((packed_width, rows), BF)],
        compiler_params=ROOMY,
        cost_estimate=estimate,
        name="gather",
    )(halo, reduced, pair, near_pair, far_pair, beyond, grad_mixed, core_rows, neighbours)

    mixed_part, from_near, from_far = lax.optimization_barrier((mixed_part, from_near, from_far))
    returned = from_near.astype(F32) + from_far.astype(F32)
    last = crossed(returned[SLAB:].astype(BF), 1).astype(F32)
    grad_slab = ((own + returned[:SLAB] + last) * keep).astype(BF)
    shared = jnp.concatenate([grad_slab, mixed_part.astype(BF)], 0)
    exchanged = [shared] + [shifted(shared, "chan", j) for j in (1, 2, 3)]

    half = struct((rank // 2, packed_width), F32)
    grad_features, output, mine, give = pl.pallas_call(
        finish_kernel,
        out_shape=[struct((channels, rows), BF)] * 2 + [half] * 2,
        in_specs=[VMEM] * 10,
        out_specs=[VMEM] * 4,
        compiler_params=SNUG,
        name="finish",
    )(mixed_part, *exchanged, in_factor, features, out_factor, cotangent, grad_core)
    mine, other = leaf_sum(mine, give)

    factor = float(rows * lax.axis_size("leaf")) ** (-0.5)
    grad_in, grad_core, grad_out = pl.pallas_call(
        lambda *refs: unpack_kernel(factor, *refs),
        out_shape=[struct((channels, rank), F32), struct((width, offsets, rank), F32), struct((rank, channels), F32)],
        in_specs=[VMEM] * 2,
        out_specs=[VMEM] * 3,
        scratch_shapes=[pltpu.VMEM((packed_width, rank), F32), pltpu.VMEM((rank, channels), F32)],
        compiler_params=SNUG,
        name="unpack",
    )(mine, other)
    return (output, grad_features, grad_in, jnp.transpose(grad_core, (1, 0, 2)), grad_out)


def solution(mesh):
    placed = (
        P("chan", "leaf"),
        P("chan", None),
        P(None, "chan", None),
        P(None, "chan"),
        P(None, "leaf"),
        P("leaf", None, None),
        P("leaf"),
        P("chan", "leaf"),
    )
    return jax.shard_map(
        body,
        mesh=mesh,
        in_specs=placed,
        out_specs=(
            P("chan", "leaf"),
            P("chan", "leaf"),
            P("chan", None),
            P(None, "chan", None),
            P(None, "chan"),
        ),
        check_vma=False,
    )
```

```python
import jax
import jax.numpy as jnp
from jax import lax
from jax.experimental import pallas as pl
from jax.experimental.pallas import tpu as pltpu
from jax.sharding import PartitionSpec as P

BF = jnp.bfloat16
F32 = jnp.float32
LOW = 256
SLAB = 16
VMEM = pl.BlockSpec(memory_space=pltpu.VMEM)
SMEM = pl.BlockSpec(memory_space=pltpu.SMEM)
ROOMY = pltpu.CompilerParams(vmem_limit_bytes=40 * 2**20)
SNUG = pltpu.CompilerParams(vmem_limit_bytes=12 * 2**20)


def dot(a, b, contract=((1,), (0,))):
    return lax.dot_general(a, b, (contract, ((), ())), preferred_element_type=F32)


NT = ((1,), (1,))
TN = ((0,), (0,))


def rank_picker(shape, slab_dim, group, group_count, width, sign):
    padded = lax.broadcasted_iota(jnp.int32, shape, slab_dim)
    rank = lax.broadcasted_iota(jnp.int32, shape, 1 - slab_dim)
    step = padded // SLAB
    lane = padded % SLAB
    slab = lax.rem(group + sign * step + group_count, group_count)
    hit = (rank == slab * width + lane) & (lane < width)
    return jnp.where(hit, 1.0, 0.0).astype(BF)


def project_kernel(feat_ref, in_ref, cot_ref, outf_ref, own_reduced_ref, own_mixed_ref, *payload_refs):
    group_count = 1 + len(payload_refs)
    rank = in_ref.shape[1]
    width = rank // group_count
    pick = rank_picker((group_count * SLAB, rank), 0, lax.axis_index("chan"), group_count, width, 1)
    weights = dot(pick, in_ref[...], NT).astype(BF)
    reduced = dot(weights, feat_ref[...])
    grad_mixed = dot(outf_ref[...], cot_ref[...])
    own_reduced_ref[...] = reduced[:SLAB]
    own_mixed_ref[...] = grad_mixed
    for j, payload_ref in enumerate(payload_refs):
        payload_ref[0:SLAB, :] = reduced[(j + 1) * SLAB : (j + 2) * SLAB].astype(BF)
        payload_ref[SLAB:, :] = grad_mixed.astype(BF)


def low_onehot(low):
    shape = (LOW, low.shape[1])
    want = jnp.broadcast_to(low.astype(F32), shape).astype(BF)
    have = lax.broadcasted_iota(jnp.int32, shape, 0).astype(F32).astype(BF)
    return jnp.where(have == want, jnp.ones((), BF), jnp.zeros((), BF))


def core_bit():
    return lax.axis_index("leaf") % 2


def first_octant(halo_ref, slot):
    return jnp.clip(halo_ref[slot, 0] & 15, 0, 8) * 64


def mirrored(core, view, near):
    return jnp.where(core == 0, view, near - 1 - view)


def scatter_kernel(halo_ref, p0, p1, p2, p3, core_ref, nbr_ref, gm_ref, own_ref, kept_ref,
                   cross_ref, terms_ref, acc_ref):
    rows = nbr_ref.shape[1]
    tiles = acc_ref.shape[0] // SLAB
    total = (p0[...] + p1[SLAB:, :].astype(F32)) + (
        p2[SLAB:, :].astype(F32) + p3[SLAB:, :].astype(F32)
    )
    grad_mixed = total.astype(BF)
    gm_ref[...] = grad_mixed
    terms_ref[...] = dot(core_ref[...], grad_mixed).astype(BF)
    acc_ref[...] = jnp.zeros_like(acc_ref)

    def step(k, carry):
        index = nbr_ref[pl.ds(k, 1), :]
        onehot = low_onehot(index & (LOW - 1))
        high = jnp.broadcast_to((index >> 8).astype(F32), (SLAB, rows)).astype(BF)
        terms = terms_ref[pl.ds(pl.multiple_of(k * SLAB, SLAB), SLAB), :]
        spread = jnp.concatenate(
            [jnp.where(high == jnp.full((), t, BF), terms, jnp.zeros((), BF)) for t in range(tiles)], 0
        )
        acc_ref[...] += dot(spread, onehot, NT)
        return carry

    lax.fori_loop(0, nbr_ref.shape[0], step, 0, unroll=9)

    def tile(t):
        return acc_ref[pl.ds(pl.multiple_of(t * SLAB, SLAB), SLAB), :]

    own_tiles = rows // LOW
    own_ref[...] = jnp.concatenate([tile(t) for t in range(own_tiles)], 1)
    near = halo_ref.shape[0]
    per_peer = (tiles - own_tiles) // near
    blank = jnp.zeros((SLAB, rows - per_peer * LOW), F32)
    for view in range(near):
        slot = mirrored(core_bit(), view, near)
        start = own_tiles + slot * per_peer
        window = jnp.concatenate([tile(start + i) for i in range(per_peer)] + [blank], 1)
        block = pltpu.roll(window, first_octant(halo_ref, slot), 1)
        if view < 4:
            kept_ref[view * SLAB : (view + 1) * SLAB, :] = block
        else:
            cross_ref[(view - 4) * SLAB : (view - 3) * SLAB, :] = block.astype(BF)


def gather_kernel(halo_ref, own_ref, pair_ref, near_ref, far_ref, cross_ref, gm_ref, core_ref,
                  nbr_ref, mix_ref, gc_ref, table_ref, ga_ref):
    rows = nbr_ref.shape[1]
    tiles = table_ref.shape[0] // SLAB
    own_tiles = rows // LOW
    near = halo_ref.shape[0]
    per_peer = (tiles - own_tiles) // near
    for t in range(own_tiles):
        table_ref[t * SLAB : (t + 1) * SLAB, :] = own_ref[:, t * LOW : (t + 1) * LOW]
    views = (
        far_ref[0:SLAB, :],
        far_ref[SLAB:, :],
        near_ref[0:SLAB, :],
        near_ref[SLAB:, :],
        pair_ref[...],
        cross_ref[SLAB : 2 * SLAB, :],
        cross_ref[0:SLAB, :],
        cross_ref[3 * SLAB :, :],
    )
    for view in range(near):
        slot = mirrored(core_bit(), view, near)
        window = pltpu.roll(views[view].astype(F32), rows - first_octant(halo_ref, slot), 1).astype(BF)
        for i in range(per_peer):
            t = own_tiles + slot * per_peer + i
            table_ref[pl.ds(pl.multiple_of(t * SLAB, SLAB), SLAB), :] = window[:, i * LOW : (i + 1) * LOW]

    def step(k, carry):
        index = nbr_ref[pl.ds(k, 1), :]
        onehot = low_onehot(index & (LOW - 1))
        high = jnp.broadcast_to(index >> 8, (SLAB, rows))
        picked = dot(table_ref[...], onehot)
        found = jnp.zeros((SLAB, rows), F32)
        for t in range(tiles):
            found = jnp.where(high == t, picked[t * SLAB : (t + 1) * SLAB], found)
        ga_ref[pl.ds(pl.multiple_of(k * SLAB, SLAB), SLAB), :] = found.astype(BF)
        return carry

    lax.fori_loop(0, nbr_ref.shape[0], step, 0, unroll=9)
    used = core_ref.shape[0]
    ga_ref[used:, :] = jnp.zeros_like(ga_ref[used:, :])
    mix_ref[...] = dot(core_ref[...], ga_ref[:used, :], TN)
    gc_ref[...] = dot(gm_ref[...], ga_ref[...], NT)


def finish_kernel(mix_ref, e0, e2, e1, e3, in_ref, feat_ref, outf_ref, cot_ref, gc_ref,
                  gf_ref, out_ref, keep_ref, give_ref):
    rank = in_ref.shape[1]
    rows = feat_ref.shape[1]
    wide = gc_ref.shape[1]
    group = lax.axis_index("chan")
    pick = rank_picker((rank, 4 * SLAB), 1, group, 4, rank // 4, -1)
    slabs = jnp.concatenate([e[0:SLAB, :] for e in (e0, e1, e2, e3)], 0)
    grad_rows = dot(pick, slabs).astype(BF)
    gf_ref[...] = dot(in_ref[...], grad_rows).astype(BF)
    total = (mix_ref[...] + e1[SLAB:, :].astype(F32)) + (e2[SLAB:, :].astype(F32) + e3[SLAB:, :].astype(F32))
    mixed = total.astype(BF)
    out_ref[...] = dot(outf_ref[...], mixed, TN).astype(BF)
    column = lax.broadcasted_iota(jnp.int32, (wide, rank), 0)
    wanted = lax.broadcasted_iota(jnp.int32, (wide, rank), 1)
    free = column % SLAB - (SLAB - 4)
    place = jnp.where((free >= 0) & (column // SLAB * 4 + free == wanted), 1.0, 0.0).astype(BF)
    spread = dot(place, grad_rows).astype(BF)
    right = jnp.concatenate([jnp.zeros((48, rows), BF), cot_ref[...], jnp.zeros((32, rows), BF)], 0)
    tail = dot(mixed, right, NT)
    packed = gc_ref[...] + dot(feat_ref[...], spread, NT)
    packed = jnp.concatenate([packed[:, : wide - 128], packed[:, wide - 128 :] + tail], 1)
    half = rank // 2
    first = core_bit() == 0
    keep_ref[...] = jnp.where(first, packed[:half], packed[half:])
    give_ref[...] = jnp.where(first, packed[half:], packed[:half])


def unpack_kernel(factor, mine_ref, other_ref, left_ref, core_ref, right_ref, flat_ref, turned_ref):
    width, offsets, rank = core_ref.shape
    mine, other = mine_ref[...] * factor, other_ref[...] * factor
    first = core_bit() == 0
    packed = jnp.concatenate([jnp.where(first, mine, other), jnp.where(first, other, mine)], 0)
    flat_ref[...] = packed.T
    for c in range(width):
        core_ref[c] = flat_ref[pl.ds(c, offsets, stride=SLAB), :]
    for j in range(4):
        turned_ref[pl.ds(j, rank // 4, stride=4), :] = flat_ref[pl.ds(width + j, rank // 4, stride=SLAB), :]
    left_ref[...] = turned_ref[...].T
    right_ref[...] = flat_ref[offsets * SLAB : offsets * SLAB + rank, :].T


def shifted(block, axis, distance):
    count = lax.axis_size(axis)
    return lax.ppermute(block, axis, [(i, (i + distance) % count) for i in range(count)])


def crossed(block, mask):
    return lax.ppermute(block, "leaf", [(i, i ^ mask) for i in range(lax.axis_size("leaf"))])


def outward(block, chips):
    count = lax.axis_size("leaf")
    return lax.ppermute(
        block, "leaf", [(i, (i + (2 * chips if i % 2 == 0 else -2 * chips)) % count) for i in range(count)]
    )


def leaf_sum(mine, give):
    mine = mine + crossed(give, 1)
    for masks in ((8,), (4, 2, 6), (32, 16, 48)):
        mine = mine + sum(crossed(mine, mask) for mask in masks)
    return mine, crossed(mine, 1)


def struct(shape, dtype):
    return jax.ShapeDtypeStruct(shape, dtype)


def body(features, in_factor, core, out_factor, neighbours, halo_blocks, row_mask, cotangent):
    channels, rows = features.shape
    offsets, width, rank = core.shape
    near, slots = halo_blocks.shape[1:]
    table_rows = (rows + near * slots * 64) // LOW * SLAB
    packed_width = (offsets * SLAB + 127) // 128 * 128
    keep = row_mask.astype(F32).reshape(1, rows)
    halo = halo_blocks[0]
    core_rows = jnp.pad(core, ((0, 0), (0, SLAB - width), (0, 0))).reshape(offsets * SLAB, rank)
    estimate = pl.CostEstimate(flops=5 * 10**9, bytes_accessed=2**20, transcendentals=0)

    own_reduced, own_mixed, *payload = pl.pallas_call(
        project_kernel,
        out_shape=[struct((SLAB, rows), F32), struct((rank, rows), F32)] + [struct((SLAB + rank, rows), BF)] * 3,
        in_specs=[VMEM] * 4,
        out_specs=[VMEM] * 5,
        name="project",
    )(features, in_factor, cotangent, out_factor)
    arrived = {j: shifted(payload[j - 1], "chan", j) for j in (1, 3, 2)}
    parts = [arrived[1], arrived[3], arrived[2]]
    reduced = own_reduced + sum(part[:SLAB].astype(F32) for part in parts)
    reduced = (reduced * keep).astype(BF)

    pair = crossed(reduced, 1)
    both, parts = lax.optimization_barrier((jnp.concatenate([reduced, pair], 0), parts))
    far_pair = outward(both, 2)
    near_pair = outward(both, 1)

    grad_mixed, own, kept, cross = pl.pallas_call(
        scatter_kernel,
        out_shape=[
            struct((rank, rows), BF),
            struct((SLAB, rows), F32),
            struct((4 * SLAB, rows), F32),
            struct((4 * SLAB, rows), BF),
        ],
        in_specs=[SMEM] + [VMEM] * 6,
        out_specs=[VMEM] * 4,
        scratch_shapes=[pltpu.VMEM((offsets * SLAB, rows), BF), pltpu.VMEM((table_rows, LOW), F32)],
        compiler_params=ROOMY,
        cost_estimate=estimate,
        name="scatter",
    )(halo, own_mixed, *parts, core_rows, neighbours)

    swapped = crossed(jnp.concatenate([cross, near_pair, far_pair], 0), 1)
    handed, beyond = swapped[: 4 * SLAB].astype(F32), swapped[4 * SLAB :]
    own = own + handed[:SLAB]
    to_near = jnp.concatenate(
        [kept[2 * SLAB : 3 * SLAB] + handed[2 * SLAB : 3 * SLAB], kept[3 * SLAB :] + handed[SLAB : 2 * SLAB]], 0
    ).astype(BF)
    to_far = jnp.concatenate([kept[:SLAB], kept[SLAB : 2 * SLAB] + handed[3 * SLAB :]], 0).astype(BF)
    beyond, to_near, to_far = lax.optimization_barrier((beyond, to_near, to_far))
    from_near = outward(to_near, -1)
    from_far = outward(to_far, -2)

    mixed_part, grad_core = pl.pallas_call(
        gather_kernel,
        out_shape=[struct((rank, rows), F32), struct((rank, packed_width), F32)],
        in_specs=[SMEM] + [VMEM] * 8,
        out_specs=[VMEM] * 2,
        scratch_shapes=[pltpu.VMEM((table_rows, LOW), BF), pltpu.VMEM((packed_width, rows), BF)],
        compiler_params=ROOMY,
        cost_estimate=estimate,
        name="gather",
    )(halo, reduced, pair, near_pair, far_pair, beyond, grad_mixed, core_rows, neighbours)

    mixed_part, from_near, from_far = lax.optimization_barrier((mixed_part, from_near, from_far))
    returned = from_near.astype(F32) + from_far.astype(F32)
    last = crossed(returned[SLAB:].astype(BF), 1).astype(F32)
    grad_slab = ((own + returned[:SLAB] + last) * keep).astype(BF)
    shared = jnp.concatenate([grad_slab, mixed_part.astype(BF)], 0)
    exchanged = [shared] + [shifted(shared, "chan", j) for j in (2, 1, 3)]

    half = struct((rank // 2, packed_width), F32)
    grad_features, output, mine, give = pl.pallas_call(
        finish_kernel,
        out_shape=[struct((channels, rows), BF)] * 2 + [half] * 2,
        in_specs=[VMEM] * 10,
        out_specs=[VMEM] * 4,
        compiler_params=SNUG,
        name="finish",
    )(mixed_part, *exchanged, in_factor, features, out_factor, cotangent, grad_core)
    mine, other = leaf_sum(mine, give)

    factor = float(rows * lax.axis_size("leaf")) ** (-0.5)
    grad_in, grad_core, grad_out = pl.pallas_call(
        lambda *refs: unpack_kernel(factor, *refs),
        out_shape=[struct((channels, rank), F32), struct((width, offsets, rank), F32), struct((rank, channels), F32)],
        in_specs=[VMEM] * 2,
        out_specs=[VMEM] * 3,
        scratch_shapes=[pltpu.VMEM((packed_width, rank), F32), pltpu.VMEM((rank, channels), F32)],
        compiler_params=SNUG,
        name="unpack",
    )(mine, other)
    return (output, grad_features, grad_in, jnp.transpose(grad_core, (1, 0, 2)), grad_out)


def solution(mesh):
    placed = (
        P("chan", "leaf"),
        P("chan", None),
        P(None, "chan", None),
        P(None, "chan"),
        P(None, "leaf"),
        P("leaf", None, None),
        P("leaf"),
        P("chan", "leaf"),
    )
    return jax.shard_map(
        body,
        mesh=mesh,
        in_specs=placed,
        out_specs=(
            P("chan", "leaf"),
            P("chan", "leaf"),
            P("chan", None),
            P(None, "chan", None),
            P(None, "chan"),
        ),
        check_vma=False,
    )
```

```python
import jax
import jax.numpy as jnp
from jax import lax
from jax.experimental import pallas as pl
from jax.experimental.pallas import tpu as pltpu
from jax.sharding import PartitionSpec as P

BF = jnp.bfloat16
F32 = jnp.float32
LOW = 256
SLAB = 16
VMEM = pl.BlockSpec(memory_space=pltpu.VMEM)
SMEM = pl.BlockSpec(memory_space=pltpu.SMEM)
ROOMY = pltpu.CompilerParams(vmem_limit_bytes=40 * 2**20)
SNUG = pltpu.CompilerParams(vmem_limit_bytes=12 * 2**20)


def dot(a, b, contract=((1,), (0,))):
    return lax.dot_general(a, b, (contract, ((), ())), preferred_element_type=F32)


NT = ((1,), (1,))
TN = ((0,), (0,))


def rank_picker(shape, slab_dim, group, group_count, width, sign):
    padded = lax.broadcasted_iota(jnp.int32, shape, slab_dim)
    rank = lax.broadcasted_iota(jnp.int32, shape, 1 - slab_dim)
    step = padded // SLAB
    lane = padded % SLAB
    slab = lax.rem(group + sign * step + group_count, group_count)
    hit = (rank == slab * width + lane) & (lane < width)
    return jnp.where(hit, 1.0, 0.0).astype(BF)


def project_kernel(feat_ref, in_ref, cot_ref, outf_ref, own_reduced_ref, own_mixed_ref, mixed_ref,
                   *payload_refs):
    group_count = 1 + len(payload_refs)
    rank = in_ref.shape[1]
    width = rank // group_count
    pick = rank_picker((group_count * SLAB, rank), 0, lax.axis_index("chan"), group_count, width, 1)
    weights = dot(pick, in_ref[...], NT).astype(BF)
    reduced = dot(weights, feat_ref[...])
    grad_mixed = dot(outf_ref[...], cot_ref[...])
    own_reduced_ref[...] = reduced[:SLAB]
    own_mixed_ref[...] = grad_mixed
    for j, payload_ref in enumerate(payload_refs):
        payload_ref[...] = reduced[(j + 1) * SLAB : (j + 2) * SLAB].astype(BF)
    mixed_ref[...] = grad_mixed.astype(BF)


def low_onehot(low):
    shape = (LOW, low.shape[1])
    want = jnp.broadcast_to(low.astype(F32), shape).astype(BF)
    have = lax.broadcasted_iota(jnp.int32, shape, 0).astype(F32).astype(BF)
    return jnp.where(have == want, jnp.ones((), BF), jnp.zeros((), BF))


def core_bit():
    return lax.axis_index("leaf") % 2


def first_octant(halo_ref, slot):
    return jnp.clip(halo_ref[slot, 0] & 15, 0, 8) * 64


def mirrored(core, view, near):
    return jnp.where(core == 0, view, near - 1 - view)


def scatter_kernel(halo_ref, p0, p1, p2, p3, core_ref, nbr_ref, gm_ref, own_ref, kept_ref,
                   cross_ref, terms_ref, acc_ref):
    rows = nbr_ref.shape[1]
    tiles = acc_ref.shape[0] // SLAB
    total = (p0[...] + p1[...].astype(F32)) + (p2[...].astype(F32) + p3[...].astype(F32))
    grad_mixed = total.astype(BF)
    gm_ref[...] = grad_mixed
    terms_ref[...] = dot(core_ref[...], grad_mixed).astype(BF)
    acc_ref[...] = jnp.zeros_like(acc_ref)

    def step(k, carry):
        index = nbr_ref[pl.ds(k, 1), :]
        onehot = low_onehot(index & (LOW - 1))
        high = jnp.broadcast_to((index >> 8).astype(F32), (SLAB, rows)).astype(BF)
        terms = terms_ref[pl.ds(pl.multiple_of(k * SLAB, SLAB), SLAB), :]
        spread = jnp.concatenate(
            [jnp.where(high == jnp.full((), t, BF), terms, jnp.zeros((), BF)) for t in range(tiles)], 0
        )
        acc_ref[...] += dot(spread, onehot, NT)
        return carry

    offsets = nbr_ref.shape[0]
    middle = offsets // 2
    lax.fori_loop(0, offsets - 1, lambda i, carry: step(i + (i >= middle), carry), 0, unroll=13)

    def tile(t):
        return acc_ref[pl.ds(pl.multiple_of(t * SLAB, SLAB), SLAB), :]

    own_tiles = rows // LOW
    itself = terms_ref[middle * SLAB : (middle + 1) * SLAB, :].astype(F32)
    own_ref[...] = jnp.concatenate([tile(t) for t in range(own_tiles)], 1) + itself
    near = halo_ref.shape[0]
    per_peer = (tiles - own_tiles) // near
    blank = jnp.zeros((SLAB, rows - per_peer * LOW), F32)
    for view in range(near):
        slot = mirrored(core_bit(), view, near)
        start = own_tiles + slot * per_peer
        window = jnp.concatenate([tile(start + i) for i in range(per_peer)] + [blank], 1)
        block = pltpu.roll(window, first_octant(halo_ref, slot), 1)
        if view < 4:
            kept_ref[view * SLAB : (view + 1) * SLAB, :] = block
        else:
            cross_ref[(view - 4) * SLAB : (view - 3) * SLAB, :] = block.astype(BF)


def gather_kernel(halo_ref, own_ref, pair_ref, near_ref, far_ref, cross_ref, gm_ref, core_ref,
                  nbr_ref, mix_ref, gc_ref, table_ref, ga_ref):
    rows = nbr_ref.shape[1]
    tiles = table_ref.shape[0] // SLAB
    own_tiles = rows // LOW
    near = halo_ref.shape[0]
    per_peer = (tiles - own_tiles) // near
    for t in range(own_tiles):
        table_ref[t * SLAB : (t + 1) * SLAB, :] = own_ref[:, t * LOW : (t + 1) * LOW]
    views = (
        far_ref[0:SLAB, :],
        far_ref[SLAB:, :],
        near_ref[0:SLAB, :],
        near_ref[SLAB:, :],
        pair_ref[...],
        cross_ref[SLAB : 2 * SLAB, :],
        cross_ref[0:SLAB, :],
        cross_ref[3 * SLAB :, :],
    )
    for view in range(near):
        slot = mirrored(core_bit(), view, near)
        window = pltpu.roll(views[view].astype(F32), rows - first_octant(halo_ref, slot), 1).astype(BF)
        for i in range(per_peer):
            t = own_tiles + slot * per_peer + i
            table_ref[pl.ds(pl.multiple_of(t * SLAB, SLAB), SLAB), :] = window[:, i * LOW : (i + 1) * LOW]

    def step(k, carry):
        index = nbr_ref[pl.ds(k, 1), :]
        onehot = low_onehot(index & (LOW - 1))
        high = jnp.broadcast_to(index >> 8, (SLAB, rows))
        picked = dot(table_ref[...], onehot)
        found = jnp.zeros((SLAB, rows), F32)
        for t in range(tiles):
            found = jnp.where(high == t, picked[t * SLAB : (t + 1) * SLAB], found)
        ga_ref[pl.ds(pl.multiple_of(k * SLAB, SLAB), SLAB), :] = found.astype(BF)
        return carry

    offsets = nbr_ref.shape[0]
    middle = offsets // 2
    lax.fori_loop(0, offsets - 1, lambda i, carry: step(i + (i >= middle), carry), 0, unroll=13)
    ga_ref[middle * SLAB : (middle + 1) * SLAB, :] = own_ref[...]
    used = core_ref.shape[0]
    ga_ref[used:, :] = jnp.zeros_like(ga_ref[used:, :])
    mix_ref[...] = dot(core_ref[...], ga_ref[:used, :], TN)
    gc_ref[...] = dot(gm_ref[...], ga_ref[...], NT)


def finish_kernel(mix_ref, e0, e1, e3, e2, in_ref, feat_ref, outf_ref, cot_ref, gc_ref,
                  gf_ref, out_ref, keep_ref, give_ref):
    rank = in_ref.shape[1]
    rows = feat_ref.shape[1]
    wide = gc_ref.shape[1]
    group = lax.axis_index("chan")
    pick = rank_picker((rank, 4 * SLAB), 1, group, 4, rank // 4, -1)
    slabs = jnp.concatenate([e[0:SLAB, :] for e in (e0, e1, e2, e3)], 0)
    grad_rows = dot(pick, slabs).astype(BF)
    gf_ref[...] = dot(in_ref[...], grad_rows).astype(BF)
    total = (mix_ref[...] + e1[SLAB:, :].astype(F32)) + (e2[SLAB:, :].astype(F32) + e3[SLAB:, :].astype(F32))
    mixed = total.astype(BF)
    out_ref[...] = dot(outf_ref[...], mixed, TN).astype(BF)
    column = lax.broadcasted_iota(jnp.int32, (wide, rank), 0)
    wanted = lax.broadcasted_iota(jnp.int32, (wide, rank), 1)
    free = column % SLAB - (SLAB - 4)
    place = jnp.where((free >= 0) & (column // SLAB * 4 + free == wanted), 1.0, 0.0).astype(BF)
    spread = dot(place, grad_rows).astype(BF)
    right = jnp.concatenate([jnp.zeros((48, rows), BF), cot_ref[...], jnp.zeros((32, rows), BF)], 0)
    tail = dot(mixed, right, NT)
    packed = gc_ref[...] + dot(feat_ref[...], spread, NT)
    packed = jnp.concatenate([packed[:, : wide - 128], packed[:, wide - 128 :] + tail], 1)
    half = rank // 2
    first = core_bit() == 0
    keep_ref[...] = jnp.where(first, packed[:half], packed[half:])
    give_ref[...] = jnp.where(first, packed[half:], packed[:half])


def unpack_kernel(factor, mine_ref, other_ref, left_ref, core_ref, right_ref, flat_ref, turned_ref):
    width, offsets, rank = core_ref.shape
    mine, other = mine_ref[...] * factor, other_ref[...] * factor
    first = core_bit() == 0
    packed = jnp.concatenate([jnp.where(first, mine, other), jnp.where(first, other, mine)], 0)
    flat_ref[...] = packed.T
    for c in range(width):
        core_ref[c] = flat_ref[pl.ds(c, offsets, stride=SLAB), :]
    for j in range(4):
        turned_ref[pl.ds(j, rank // 4, stride=4), :] = flat_ref[pl.ds(width + j, rank // 4, stride=SLAB), :]
    left_ref[...] = turned_ref[...].T
    right_ref[...] = flat_ref[offsets * SLAB : offsets * SLAB + rank, :].T


def shifted(block, axis, distance):
    count = lax.axis_size(axis)
    return lax.ppermute(block, axis, [(i, (i + distance) % count) for i in range(count)])


def crossed(block, mask):
    return lax.ppermute(block, "leaf", [(i, i ^ mask) for i in range(lax.axis_size("leaf"))])


def outward(block, chips):
    count = lax.axis_size("leaf")
    return lax.ppermute(
        block, "leaf", [(i, (i + (2 * chips if i % 2 == 0 else -2 * chips)) % count) for i in range(count)]
    )


def leaf_sum(mine, give):
    mine = mine + crossed(give, 1)
    for masks in ((8,), (2, 6, 4), (16, 48, 32)):
        mine = mine + sum(crossed(mine, mask) for mask in masks)
    return mine, crossed(mine, 1)


def struct(shape, dtype):
    return jax.ShapeDtypeStruct(shape, dtype)


def body(features, in_factor, core, out_factor, neighbours, halo_blocks, row_mask, cotangent):
    channels, rows = features.shape
    offsets, width, rank = core.shape
    near, slots = halo_blocks.shape[1:]
    table_rows = (rows + near * slots * 64) // LOW * SLAB
    packed_width = (offsets * SLAB + 127) // 128 * 128
    keep = row_mask.astype(F32).reshape(1, rows)
    halo = halo_blocks[0]
    core_rows = jnp.pad(core, ((0, 0), (0, SLAB - width), (0, 0))).reshape(offsets * SLAB, rank)
    estimate = pl.CostEstimate(flops=5 * 10**9, bytes_accessed=2**20, transcendentals=0)

    slab = struct((SLAB, rows), BF)
    own_reduced, own_mixed, sent_mixed, *payload = pl.pallas_call(
        project_kernel,
        out_shape=[struct((SLAB, rows), F32), struct((rank, rows), F32), struct((rank, rows), BF)] + [slab] * 3,
        in_specs=[VMEM] * 4,
        out_specs=[VMEM] * 6,
        name="project",
    )(features, in_factor, cotangent, out_factor)
    reduced = own_reduced + sum(shifted(payload[j - 1], "chan", j).astype(F32) for j in (1, 3, 2))
    parts = [shifted(sent_mixed, "chan", j) for j in (1, 3, 2)]
    reduced = (reduced * keep).astype(BF)

    pair = crossed(reduced, 1)
    both = jnp.concatenate([reduced, pair], 0)
    parts, unused = lax.optimization_barrier((parts, pair))
    far_pair = outward(both, 2)
    near_pair = outward(both, 1)

    grad_mixed, own, kept, cross = pl.pallas_call(
        scatter_kernel,
        out_shape=[
            struct((rank, rows), BF),
            struct((SLAB, rows), F32),
            struct((4 * SLAB, rows), F32),
            struct((4 * SLAB, rows), BF),
        ],
        in_specs=[SMEM] + [VMEM] * 6,
        out_specs=[VMEM] * 4,
        scratch_shapes=[pltpu.VMEM((offsets * SLAB, rows), BF), pltpu.VMEM((table_rows, LOW), F32)],
        compiler_params=ROOMY,
        cost_estimate=estimate,
        name="scatter",
    )(halo, own_mixed, *parts, core_rows, neighbours)

    swapped = crossed(jnp.concatenate([cross, near_pair, far_pair], 0), 1)
    handed, beyond = swapped[: 4 * SLAB].astype(F32), swapped[4 * SLAB :]
    own = own + handed[:SLAB]
    to_near = jnp.concatenate(
        [kept[2 * SLAB : 3 * SLAB] + handed[2 * SLAB : 3 * SLAB], kept[3 * SLAB :] + handed[SLAB : 2 * SLAB]], 0
    ).astype(BF)
    to_far = jnp.concatenate([kept[:SLAB], kept[SLAB : 2 * SLAB] + handed[3 * SLAB :]], 0).astype(BF)
    beyond, to_near, to_far = lax.optimization_barrier((beyond, to_near, to_far))
    from_near = outward(to_near, -1)
    from_far = outward(to_far, -2)

    mixed_part, grad_core = pl.pallas_call(
        gather_kernel,
        out_shape=[struct((rank, rows), F32), struct((rank, packed_width), F32)],
        in_specs=[SMEM] + [VMEM] * 8,
        out_specs=[VMEM] * 2,
        scratch_shapes=[pltpu.VMEM((table_rows, LOW), BF), pltpu.VMEM((packed_width, rows), BF)],
        compiler_params=ROOMY,
        cost_estimate=estimate,
        name="gather",
    )(halo, reduced, pair, near_pair, far_pair, beyond, grad_mixed, core_rows, neighbours)

    mixed_part, from_near, from_far = lax.optimization_barrier((mixed_part, from_near, from_far))
    returned = from_near.astype(F32) + from_far.astype(F32)
    last = crossed(returned[SLAB:].astype(BF), 1).astype(F32)
    grad_slab = ((own + returned[:SLAB] + last) * keep).astype(BF)
    shared = jnp.concatenate([grad_slab, mixed_part.astype(BF)], 0)
    exchanged = [shared] + [shifted(shared, "chan", j) for j in (1, 3, 2)]

    half = struct((rank // 2, packed_width), F32)
    grad_features, output, mine, give = pl.pallas_call(
        finish_kernel,
        out_shape=[struct((channels, rows), BF)] * 2 + [half] * 2,
        in_specs=[VMEM] * 10,
        out_specs=[VMEM] * 4,
        compiler_params=SNUG,
        name="finish",
    )(mixed_part, *exchanged, in_factor, features, out_factor, cotangent, grad_core)
    mine, other = leaf_sum(mine, give)

    factor = float(rows * lax.axis_size("leaf")) ** (-0.5)
    grad_in, grad_core, grad_out = pl.pallas_call(
        lambda *refs: unpack_kernel(factor, *refs),
        out_shape=[struct((channels, rank), F32), struct((width, offsets, rank), F32), struct((rank, channels), F32)],
        in_specs=[VMEM] * 2,
        out_specs=[VMEM] * 3,
        scratch_shapes=[pltpu.VMEM((packed_width, rank), F32), pltpu.VMEM((rank, channels), F32)],
        compiler_params=SNUG,
        name="unpack",
    )(mine, other)
    return (output, grad_features, grad_in, jnp.transpose(grad_core, (1, 0, 2)), grad_out)


def solution(mesh):
    placed = (
        P("chan", "leaf"),
        P("chan", None),
        P(None, "chan", None),
        P(None, "chan"),
        P(None, "leaf"),
        P("leaf", None, None),
        P("leaf"),
        P("chan", "leaf"),
    )
    return jax.shard_map(
        body,
        mesh=mesh,
        in_specs=placed,
        out_specs=(
            P("chan", "leaf"),
            P("chan", "leaf"),
            P("chan", None),
            P(None, "chan", None),
            P(None, "chan"),
        ),
        check_vma=False,
    )
```

```python
import jax
import jax.numpy as jnp
from jax import lax
from jax.experimental import pallas as pl
from jax.experimental.pallas import tpu as pltpu
from jax.sharding import PartitionSpec as P

BF = jnp.bfloat16
F32 = jnp.float32
LOW = 256
SLAB = 16
VMEM = pl.BlockSpec(memory_space=pltpu.VMEM)
SMEM = pl.BlockSpec(memory_space=pltpu.SMEM)
ROOMY = pltpu.CompilerParams(vmem_limit_bytes=40 * 2**20)
SNUG = pltpu.CompilerParams(vmem_limit_bytes=12 * 2**20)


def dot(a, b, contract=((1,), (0,))):
    return lax.dot_general(a, b, (contract, ((), ())), preferred_element_type=F32)


NT = ((1,), (1,))
TN = ((0,), (0,))


def rank_picker(shape, slab_dim, group, group_count, width, sign):
    padded = lax.broadcasted_iota(jnp.int32, shape, slab_dim)
    rank = lax.broadcasted_iota(jnp.int32, shape, 1 - slab_dim)
    step = padded // SLAB
    lane = padded % SLAB
    slab = lax.rem(group + sign * step + group_count, group_count)
    hit = (rank == slab * width + lane) & (lane < width)
    return jnp.where(hit, 1.0, 0.0).astype(BF)


def project_kernel(feat_ref, in_ref, cot_ref, outf_ref, own_reduced_ref, own_mixed_ref, *payload_refs):
    group_count = 1 + len(payload_refs)
    rank = in_ref.shape[1]
    width = rank // group_count
    pick = rank_picker((group_count * SLAB, rank), 0, lax.axis_index("chan"), group_count, width, 1)
    weights = dot(pick, in_ref[...], NT).astype(BF)
    reduced = dot(weights, feat_ref[...])
    grad_mixed = dot(outf_ref[...], cot_ref[...])
    own_reduced_ref[...] = reduced[:SLAB]
    own_mixed_ref[...] = grad_mixed
    for j, payload_ref in enumerate(payload_refs):
        payload_ref[0:SLAB, :] = reduced[(j + 1) * SLAB : (j + 2) * SLAB].astype(BF)
        payload_ref[SLAB:, :] = grad_mixed.astype(BF)


def low_onehot(low):
    shape = (LOW, low.shape[1])
    want = jnp.broadcast_to(low.astype(F32), shape).astype(BF)
    have = lax.broadcasted_iota(jnp.int32, shape, 0).astype(F32).astype(BF)
    return jnp.where(have == want, jnp.ones((), BF), jnp.zeros((), BF))


def core_bit():
    return lax.axis_index("leaf") % 2


def first_octant(halo_ref, slot):
    return jnp.clip(halo_ref[slot, 0] & 15, 0, 8) * 64


def mirrored(core, view, near):
    return jnp.where(core == 0, view, near - 1 - view)


def scatter_kernel(halo_ref, r0, p0, p1, p2, p3, mask_ref, core_ref, nbr_ref, gm_ref, own_ref, kept_ref,
                   cross_ref, terms_ref, acc_ref):
    rows = nbr_ref.shape[1]
    tiles = acc_ref.shape[0] // SLAB
    total = (p0[...] + p1[SLAB:, :].astype(F32)) + (
        p2[SLAB:, :].astype(F32) + p3[SLAB:, :].astype(F32)
    )
    grad_mixed = total.astype(BF)
    gm_ref[...] = grad_mixed
    reduced = (r0[...] + p1[:SLAB, :].astype(F32)) + (p2[:SLAB, :].astype(F32) + p3[:SLAB, :].astype(F32))
    cross_ref[0:SLAB, :] = (reduced * mask_ref[...].astype(F32)).astype(BF)
    terms_ref[...] = dot(core_ref[...], grad_mixed).astype(BF)
    acc_ref[...] = jnp.zeros_like(acc_ref)

    def step(k, carry):
        index = nbr_ref[pl.ds(k, 1), :]
        onehot = low_onehot(index & (LOW - 1))
        high = jnp.broadcast_to((index >> 8).astype(F32), (SLAB, rows)).astype(BF)
        terms = terms_ref[pl.ds(pl.multiple_of(k * SLAB, SLAB), SLAB), :]
        spread = jnp.concatenate(
            [jnp.where(high == jnp.full((), t, BF), terms, jnp.zeros((), BF)) for t in range(tiles)], 0
        )
        acc_ref[...] += dot(spread, onehot, NT)
        return carry

    offsets = nbr_ref.shape[0]
    middle = offsets // 2
    lax.fori_loop(0, offsets - 1, lambda i, carry: step(i + (i >= middle), carry), 0, unroll=13)

    def tile(t):
        return acc_ref[pl.ds(pl.multiple_of(t * SLAB, SLAB), SLAB), :]

    own_tiles = rows // LOW
    itself = terms_ref[middle * SLAB : (middle + 1) * SLAB, :].astype(F32)
    own_ref[...] = jnp.concatenate([tile(t) for t in range(own_tiles)], 1) + itself
    near = halo_ref.shape[0]
    per_peer = (tiles - own_tiles) // near
    blank = jnp.zeros((SLAB, rows - per_peer * LOW), F32)
    for view in range(near):
        slot = mirrored(core_bit(), view, near)
        start = own_tiles + slot * per_peer
        window = jnp.concatenate([tile(start + i) for i in range(per_peer)] + [blank], 1)
        block = pltpu.roll(window, first_octant(halo_ref, slot), 1)
        if view < 5:
            cross_ref[(view + 1) * SLAB : (view + 2) * SLAB, :] = block.astype(BF)
        else:
            kept_ref[(view - 5) * SLAB : (view - 4) * SLAB, :] = block


def gather_kernel(halo_ref, own_ref, pair_ref, near_ref, far_ref, cross_ref, gm_ref, core_ref,
                  nbr_ref, mix_ref, gc_ref, table_ref, ga_ref):
    rows = nbr_ref.shape[1]
    tiles = table_ref.shape[0] // SLAB
    own_tiles = rows // LOW
    near = halo_ref.shape[0]
    per_peer = (tiles - own_tiles) // near
    for t in range(own_tiles):
        table_ref[t * SLAB : (t + 1) * SLAB, :] = own_ref[:, t * LOW : (t + 1) * LOW]
    views = (
        far_ref[0:SLAB, :],
        far_ref[SLAB:, :],
        near_ref[0:SLAB, :],
        near_ref[SLAB:, :],
        pair_ref[...],
        cross_ref[SLAB : 2 * SLAB, :],
        cross_ref[0:SLAB, :],
        cross_ref[3 * SLAB : 4 * SLAB, :],
    )
    for view in range(near):
        slot = mirrored(core_bit(), view, near)
        window = pltpu.roll(views[view].astype(F32), rows - first_octant(halo_ref, slot), 1).astype(BF)
        for i in range(per_peer):
            t = own_tiles + slot * per_peer + i
            table_ref[pl.ds(pl.multiple_of(t * SLAB, SLAB), SLAB), :] = window[:, i * LOW : (i + 1) * LOW]

    def step(k, carry):
        index = nbr_ref[pl.ds(k, 1), :]
        onehot = low_onehot(index & (LOW - 1))
        high = jnp.broadcast_to(index >> 8, (SLAB, rows))
        picked = dot(table_ref[...], onehot)
        found = jnp.zeros((SLAB, rows), F32)
        for t in range(tiles):
            found = jnp.where(high == t, picked[t * SLAB : (t + 1) * SLAB], found)
        ga_ref[pl.ds(pl.multiple_of(k * SLAB, SLAB), SLAB), :] = found.astype(BF)
        return carry

    offsets = nbr_ref.shape[0]
    middle = offsets // 2
    lax.fori_loop(0, offsets - 1, lambda i, carry: step(i + (i >= middle), carry), 0, unroll=13)
    ga_ref[middle * SLAB : (middle + 1) * SLAB, :] = own_ref[...]
    used = core_ref.shape[0]
    ga_ref[used:, :] = jnp.zeros_like(ga_ref[used:, :])
    mix_ref[...] = dot(core_ref[...], ga_ref[:used, :], TN)
    gc_ref[...] = dot(gm_ref[...], ga_ref[...], NT)


def finish_kernel(mix_ref, e0, e1, e3, e2, in_ref, feat_ref, outf_ref, cot_ref, gc_ref,
                  gf_ref, out_ref, keep_ref, give_ref):
    rank = in_ref.shape[1]
    rows = feat_ref.shape[1]
    wide = gc_ref.shape[1]
    group = lax.axis_index("chan")
    pick = rank_picker((rank, 4 * SLAB), 1, group, 4, rank // 4, -1)
    slabs = jnp.concatenate([e[0:SLAB, :] for e in (e0, e1, e2, e3)], 0)
    grad_rows = dot(pick, slabs).astype(BF)
    gf_ref[...] = dot(in_ref[...], grad_rows).astype(BF)
    total = (mix_ref[...] + e1[SLAB:, :].astype(F32)) + (e2[SLAB:, :].astype(F32) + e3[SLAB:, :].astype(F32))
    mixed = total.astype(BF)
    out_ref[...] = dot(outf_ref[...], mixed, TN).astype(BF)
    column = lax.broadcasted_iota(jnp.int32, (wide, rank), 0)
    wanted = lax.broadcasted_iota(jnp.int32, (wide, rank), 1)
    free = column % SLAB - (SLAB - 4)
    place = jnp.where((free >= 0) & (column // SLAB * 4 + free == wanted), 1.0, 0.0).astype(BF)
    spread = dot(place, grad_rows).astype(BF)
    right = jnp.concatenate([jnp.zeros((48, rows), BF), cot_ref[...], jnp.zeros((32, rows), BF)], 0)
    tail = dot(mixed, right, NT)
    packed = gc_ref[...] + dot(feat_ref[...], spread, NT)
    packed = jnp.concatenate([packed[:, : wide - 128], packed[:, wide - 128 :] + tail], 1)
    half = rank // 2
    first = core_bit() == 0
    keep_ref[...] = jnp.where(first, packed[:half], packed[half:])
    give_ref[...] = jnp.where(first, packed[half:], packed[:half])


def unpack_kernel(factor, mine_ref, other_ref, left_ref, core_ref, right_ref, flat_ref, turned_ref):
    width, offsets, rank = core_ref.shape
    mine, other = mine_ref[...] * factor, other_ref[...] * factor
    first = core_bit() == 0
    packed = jnp.concatenate([jnp.where(first, mine, other), jnp.where(first, other, mine)], 0)
    flat_ref[...] = packed.T
    for c in range(width):
        core_ref[c] = flat_ref[pl.ds(c, offsets, stride=SLAB), :]
    for j in range(4):
        turned_ref[pl.ds(j, rank // 4, stride=4), :] = flat_ref[pl.ds(width + j, rank // 4, stride=SLAB), :]
    left_ref[...] = turned_ref[...].T
    right_ref[...] = flat_ref[offsets * SLAB : offsets * SLAB + rank, :].T


def shifted(block, axis, distance):
    count = lax.axis_size(axis)
    return lax.ppermute(block, axis, [(i, (i + distance) % count) for i in range(count)])


def crossed(block, mask):
    return lax.ppermute(block, "leaf", [(i, i ^ mask) for i in range(lax.axis_size("leaf"))])


def outward(block, chips):
    count = lax.axis_size("leaf")
    return lax.ppermute(
        block, "leaf", [(i, (i + (2 * chips if i % 2 == 0 else -2 * chips)) % count) for i in range(count)]
    )


def leaf_sum(mine, give):
    mine = mine + crossed(give, 1)
    for masks in ((8,), (2, 6, 4), (16, 48, 32)):
        mine = mine + sum(crossed(mine, mask) for mask in masks)
    return mine, crossed(mine, 1)


def struct(shape, dtype):
    return jax.ShapeDtypeStruct(shape, dtype)


def body(features, in_factor, core, out_factor, neighbours, halo_blocks, row_mask, cotangent):
    channels, rows = features.shape
    offsets, width, rank = core.shape
    near, slots = halo_blocks.shape[1:]
    table_rows = (rows + near * slots * 64) // LOW * SLAB
    packed_width = (offsets * SLAB + 127) // 128 * 128
    keep = row_mask.reshape(1, rows)
    halo = halo_blocks[0]
    core_rows = jnp.pad(core, ((0, 0), (0, SLAB - width), (0, 0))).reshape(offsets * SLAB, rank)
    estimate = pl.CostEstimate(flops=5 * 10**9, bytes_accessed=2**20, transcendentals=0)

    own_reduced, own_mixed, *payload = pl.pallas_call(
        project_kernel,
        out_shape=[struct((SLAB, rows), F32), struct((rank, rows), F32)] + [struct((SLAB + rank, rows), BF)] * 3,
        in_specs=[VMEM] * 4,
        out_specs=[VMEM] * 5,
        name="project",
    )(features, in_factor, cotangent, out_factor)
    arrived = {j: shifted(payload[j - 1], "chan", j) for j in (1, 3, 2)}

    triple = struct((3 * SLAB, rows), F32)
    grad_mixed, own, kept, cross = pl.pallas_call(
        scatter_kernel,
        out_shape=[struct((rank, rows), BF), struct((SLAB, rows), F32), triple, struct((6 * SLAB, rows), BF)],
        in_specs=[SMEM] + [VMEM] * 8,
        out_specs=[VMEM] * 4,
        scratch_shapes=[pltpu.VMEM((offsets * SLAB, rows), BF), pltpu.VMEM((table_rows, LOW), F32)],
        compiler_params=ROOMY,
        cost_estimate=estimate,
        name="scatter",
    )(halo, own_reduced, own_mixed, arrived[1], arrived[3], arrived[2], keep, core_rows, neighbours)

    def slabs_of(block, first, last):
        return block[first * SLAB : last * SLAB]

    reduced = slabs_of(cross, 0, 1)
    handed = crossed(cross, 1)
    pair = slabs_of(handed, 0, 1)
    far_other, far_same, near_other, near_same, mine = (
        slabs_of(handed, i, i + 1).astype(F32) for i in range(1, 6)
    )
    to_near = [slabs_of(kept, 0, 1) + near_same, slabs_of(kept, 1, 2) + near_other]
    to_far = [slabs_of(kept, 2, 3) + far_same, far_other]
    near = outward(jnp.concatenate([reduced, pair] + [x.astype(BF) for x in to_near], 0), 1)
    far = outward(jnp.concatenate([reduced, pair] + [x.astype(BF) for x in to_far], 0), 2)
    near_pair, far_pair = slabs_of(near, 0, 2), slabs_of(far, 0, 2)
    passed = slabs_of(near, 3, 4).astype(F32) + slabs_of(far, 3, 4).astype(F32)
    beyond = crossed(jnp.concatenate([near_pair, far_pair, passed.astype(BF)], 0), 1)
    returned = (slabs_of(near, 2, 3).astype(F32) + slabs_of(far, 2, 3).astype(F32)) + slabs_of(beyond, 4, 5).astype(F32)
    grad_slab = (((own + mine) + returned) * keep.astype(F32)).astype(BF)

    mixed_part, grad_core = pl.pallas_call(
        gather_kernel,
        out_shape=[struct((rank, rows), F32), struct((rank, packed_width), F32)],
        in_specs=[SMEM] + [VMEM] * 8,
        out_specs=[VMEM] * 2,
        scratch_shapes=[pltpu.VMEM((table_rows, LOW), BF), pltpu.VMEM((packed_width, rows), BF)],
        compiler_params=ROOMY,
        cost_estimate=estimate,
        name="gather",
    )(halo, reduced, pair, near_pair, far_pair, beyond, grad_mixed, core_rows, neighbours)

    shared = jnp.concatenate([grad_slab, mixed_part.astype(BF)], 0)
    exchanged = [shared] + [shifted(shared, "chan", j) for j in (1, 3, 2)]

    half = struct((rank // 2, packed_width), F32)
    grad_features, output, mine, give = pl.pallas_call(
        finish_kernel,
        out_shape=[struct((channels, rows), BF)] * 2 + [half] * 2,
        in_specs=[VMEM] * 10,
        out_specs=[VMEM] * 4,
        compiler_params=SNUG,
        name="finish",
    )(mixed_part, *exchanged, in_factor, features, out_factor, cotangent, grad_core)
    mine, other = leaf_sum(mine, give)

    factor = float(rows * lax.axis_size("leaf")) ** (-0.5)
    grad_in, grad_core, grad_out = pl.pallas_call(
        lambda *refs: unpack_kernel(factor, *refs),
        out_shape=[struct((channels, rank), F32), struct((width, offsets, rank), F32), struct((rank, channels), F32)],
        in_specs=[VMEM] * 2,
        out_specs=[VMEM] * 3,
        scratch_shapes=[pltpu.VMEM((packed_width, rank), F32), pltpu.VMEM((rank, channels), F32)],
        compiler_params=SNUG,
        name="unpack",
    )(mine, other)
    return (output, grad_features, grad_in, jnp.transpose(grad_core, (1, 0, 2)), grad_out)


def solution(mesh):
    placed = (
        P("chan", "leaf"),
        P("chan", None),
        P(None, "chan", None),
        P(None, "chan"),
        P(None, "leaf"),
        P("leaf", None, None),
        P("leaf"),
        P("chan", "leaf"),
    )
    return jax.shard_map(
        body,
        mesh=mesh,
        in_specs=placed,
        out_specs=(
            P("chan", "leaf"),
            P("chan", "leaf"),
            P("chan", None),
            P(None, "chan", None),
            P(None, "chan"),
        ),
        check_vma=False,
    )
```

```python
import jax
import jax.numpy as jnp
from jax import lax
from jax.experimental import pallas as pl
from jax.experimental.pallas import tpu as pltpu
from jax.sharding import PartitionSpec as P

BF = jnp.bfloat16
F32 = jnp.float32
LOW = 256
SLAB = 16
VMEM = pl.BlockSpec(memory_space=pltpu.VMEM)
SMEM = pl.BlockSpec(memory_space=pltpu.SMEM)
ROOMY = pltpu.CompilerParams(vmem_limit_bytes=40 * 2**20)
SNUG = pltpu.CompilerParams(vmem_limit_bytes=12 * 2**20)


def dot(a, b, contract=((1,), (0,))):
    return lax.dot_general(a, b, (contract, ((), ())), preferred_element_type=F32)


NT = ((1,), (1,))
TN = ((0,), (0,))


def rank_picker(shape, slab_dim, group, group_count, width, sign):
    padded = lax.broadcasted_iota(jnp.int32, shape, slab_dim)
    rank = lax.broadcasted_iota(jnp.int32, shape, 1 - slab_dim)
    step = padded // SLAB
    lane = padded % SLAB
    slab = lax.rem(group + sign * step + group_count, group_count)
    hit = (rank == slab * width + lane) & (lane < width)
    return jnp.where(hit, 1.0, 0.0).astype(BF)


def project_kernel(feat_ref, in_ref, cot_ref, outf_ref, own_reduced_ref, own_mixed_ref, *payload_refs):
    group_count = 1 + len(payload_refs)
    rank = in_ref.shape[1]
    width = rank // group_count
    pick = rank_picker((group_count * SLAB, rank), 0, lax.axis_index("chan"), group_count, width, 1)
    weights = dot(pick, in_ref[...], NT).astype(BF)
    reduced = dot(weights, feat_ref[...])
    grad_mixed = dot(outf_ref[...], cot_ref[...])
    own_reduced_ref[...] = reduced[:SLAB]
    own_mixed_ref[...] = grad_mixed
    for j, payload_ref in enumerate(payload_refs):
        payload_ref[0:SLAB, :] = reduced[(j + 1) * SLAB : (j + 2) * SLAB].astype(BF)
        payload_ref[SLAB:, :] = grad_mixed.astype(BF)


def low_onehot(low):
    shape = (LOW, low.shape[1])
    want = jnp.broadcast_to(low.astype(F32), shape).astype(BF)
    have = lax.broadcasted_iota(jnp.int32, shape, 0).astype(F32).astype(BF)
    return jnp.where(have == want, jnp.ones((), BF), jnp.zeros((), BF))


def core_bit():
    return lax.axis_index("leaf") % 2


def first_octant(halo_ref, slot):
    return jnp.clip(halo_ref[slot, 0] & 15, 0, 8) * 64


def mirrored(core, view, near):
    return jnp.where(core == 0, view, near - 1 - view)


def scatter_kernel(halo_ref, r0, p0, p1, p2, p3, mask_ref, core_ref, nbr_ref, gm_ref, own_ref, kept_ref,
                   cross_ref, terms_ref, acc_ref):
    rows = nbr_ref.shape[1]
    tiles = acc_ref.shape[0] // SLAB
    total = (p0[...] + p1[SLAB:, :].astype(F32)) + (
        p2[SLAB:, :].astype(F32) + p3[SLAB:, :].astype(F32)
    )
    grad_mixed = total.astype(BF)
    gm_ref[...] = grad_mixed
    reduced = (r0[...] + p1[:SLAB, :].astype(F32)) + (p2[:SLAB, :].astype(F32) + p3[:SLAB, :].astype(F32))
    cross_ref[0:SLAB, :] = (reduced * mask_ref[...].astype(F32)).astype(BF)
    terms_ref[...] = dot(core_ref[...], grad_mixed).astype(BF)
    acc_ref[...] = jnp.zeros_like(acc_ref)

    def step(k, carry):
        index = nbr_ref[pl.ds(k, 1), :]
        onehot = low_onehot(index & (LOW - 1))
        high = jnp.broadcast_to((index >> 8).astype(F32), (SLAB, rows)).astype(BF)
        terms = terms_ref[pl.ds(pl.multiple_of(k * SLAB, SLAB), SLAB), :]
        spread = jnp.concatenate(
            [jnp.where(high == jnp.full((), t, BF), terms, jnp.zeros((), BF)) for t in range(tiles)], 0
        )
        acc_ref[...] += dot(spread, onehot, NT)
        return carry

    offsets = nbr_ref.shape[0]
    middle = offsets // 2
    lax.fori_loop(0, offsets - 1, lambda i, carry: step(i + (i >= middle), carry), 0, unroll=13)

    def tile(t):
        return acc_ref[pl.ds(pl.multiple_of(t * SLAB, SLAB), SLAB), :]

    own_tiles = rows // LOW
    itself = terms_ref[middle * SLAB : (middle + 1) * SLAB, :].astype(F32)
    own_ref[...] = jnp.concatenate([tile(t) for t in range(own_tiles)], 1) + itself
    near = halo_ref.shape[0]
    per_peer = (tiles - own_tiles) // near
    blank = jnp.zeros((SLAB, rows - per_peer * LOW), F32)
    for view in range(near):
        slot = mirrored(core_bit(), view, near)
        start = own_tiles + slot * per_peer
        window = jnp.concatenate([tile(start + i) for i in range(per_peer)] + [blank], 1)
        block = pltpu.roll(window, first_octant(halo_ref, slot), 1)
        if view < 5:
            cross_ref[(view + 1) * SLAB : (view + 2) * SLAB, :] = block.astype(BF)
        else:
            kept_ref[(view - 5) * SLAB : (view - 4) * SLAB, :] = block


def pick_rows(table_ref, nbr_ref, highs, start_of, store):
    rows = nbr_ref.shape[1]
    offsets = nbr_ref.shape[0]
    middle = offsets // 2

    def step(i, carry):
        k = i + (i >= middle)
        index = nbr_ref[pl.ds(k, 1), :]
        onehot = low_onehot(index & (LOW - 1))
        high = jnp.broadcast_to(index >> 8, (SLAB, rows))
        picked = dot(table_ref[...], onehot)
        place = pl.ds(pl.multiple_of(k * SLAB, SLAB), SLAB)
        found = start_of(place)
        for t, value in enumerate(highs):
            found = jnp.where(high == value, picked[t * SLAB : (t + 1) * SLAB], found)
        store(place, found.astype(BF))
        return carry

    lax.fori_loop(0, offsets - 1, step, 0, unroll=13)


def fill_window(table_ref, at, block, halo_ref, slot, per_peer):
    rows = block.shape[1]
    window = pltpu.roll(block.astype(F32), rows - first_octant(halo_ref, slot), 1).astype(BF)
    for i in range(per_peer):
        table_ref[at + i * SLAB : at + (i + 1) * SLAB, :] = window[:, i * LOW : (i + 1) * LOW]


def near_gather_kernel(halo_ref, own_ref, pair_ref, nbr_ref, ga_ref, table_ref):
    rows = nbr_ref.shape[1]
    own_tiles = rows // LOW
    per_peer = table_ref.shape[0] // SLAB - own_tiles
    for t in range(own_tiles):
        table_ref[t * SLAB : (t + 1) * SLAB, :] = own_ref[:, t * LOW : (t + 1) * LOW]
    slot = mirrored(core_bit(), 4, halo_ref.shape[0])
    fill_window(table_ref, own_tiles * SLAB, pair_ref[...], halo_ref, slot, per_peer)
    highs = list(range(own_tiles)) + [own_tiles + slot * per_peer + i for i in range(per_peer)]
    middle = nbr_ref.shape[0] // 2

    def store(place, found):
        ga_ref[place, :] = found

    pick_rows(table_ref, nbr_ref, highs, lambda place: jnp.zeros((SLAB, rows), F32), store)
    ga_ref[middle * SLAB : (middle + 1) * SLAB, :] = own_ref[...]


def far_gather_kernel(halo_ref, base_ref, near_ref, far_ref, cross_ref, core_ref, nbr_ref, mix_ref, ga_ref,
                      table_ref):
    rows = nbr_ref.shape[1]
    own_tiles = rows // LOW
    near = halo_ref.shape[0]
    views = {
        0: far_ref[0:SLAB, :],
        1: far_ref[SLAB:, :],
        2: near_ref[0:SLAB, :],
        3: near_ref[SLAB:, :],
        5: cross_ref[SLAB : 2 * SLAB, :],
        6: cross_ref[0:SLAB, :],
        7: cross_ref[3 * SLAB : 4 * SLAB, :],
    }
    per_peer = table_ref.shape[0] // SLAB // len(views)
    highs = []
    for n, (view, block) in enumerate(views.items()):
        slot = mirrored(core_bit(), view, near)
        fill_window(table_ref, n * per_peer * SLAB, block, halo_ref, slot, per_peer)
        highs += [own_tiles + slot * per_peer + i for i in range(per_peer)]
    used = core_ref.shape[0]
    middle = nbr_ref.shape[0] // 2
    itself = slice(middle * SLAB, (middle + 1) * SLAB)

    def store(place, found):
        ga_ref[place, :] = found

    pick_rows(table_ref, nbr_ref, highs, lambda place: base_ref[place, :].astype(F32), store)
    ga_ref[itself, :] = base_ref[itself, :]
    ga_ref[used:, :] = jnp.zeros_like(ga_ref[used:, :])
    mix_ref[...] = dot(core_ref[...], ga_ref[:used, :], TN)


def core_gradient_kernel(gm_ref, ga_ref, gc_ref):
    gc_ref[...] = dot(gm_ref[...], ga_ref[...], NT)


def finish_kernel(mix_ref, e0, e1, e3, e2, in_ref, feat_ref, outf_ref, cot_ref, gc_ref,
                  gf_ref, out_ref, keep_ref, give_ref):
    rank = in_ref.shape[1]
    rows = feat_ref.shape[1]
    wide = gc_ref.shape[1]
    group = lax.axis_index("chan")
    pick = rank_picker((rank, 4 * SLAB), 1, group, 4, rank // 4, -1)
    slabs = jnp.concatenate([e[0:SLAB, :] for e in (e0, e1, e2, e3)], 0)
    grad_rows = dot(pick, slabs).astype(BF)
    gf_ref[...] = dot(in_ref[...], grad_rows).astype(BF)
    total = (mix_ref[...] + e1[SLAB:, :].astype(F32)) + (e2[SLAB:, :].astype(F32) + e3[SLAB:, :].astype(F32))
    mixed = total.astype(BF)
    out_ref[...] = dot(outf_ref[...], mixed, TN).astype(BF)
    column = lax.broadcasted_iota(jnp.int32, (wide, rank), 0)
    wanted = lax.broadcasted_iota(jnp.int32, (wide, rank), 1)
    free = column % SLAB - (SLAB - 4)
    place = jnp.where((free >= 0) & (column // SLAB * 4 + free == wanted), 1.0, 0.0).astype(BF)
    spread = dot(place, grad_rows).astype(BF)
    right = jnp.concatenate([jnp.zeros((48, rows), BF), cot_ref[...], jnp.zeros((32, rows), BF)], 0)
    tail = dot(mixed, right, NT)
    packed = gc_ref[...] + dot(feat_ref[...], spread, NT)
    packed = jnp.concatenate([packed[:, : wide - 128], packed[:, wide - 128 :] + tail], 1)
    half = rank // 2
    first = core_bit() == 0
    keep_ref[...] = jnp.where(first, packed[:half], packed[half:])
    give_ref[...] = jnp.where(first, packed[half:], packed[:half])


def unpack_kernel(factor, mine_ref, other_ref, left_ref, core_ref, right_ref, flat_ref, turned_ref):
    width, offsets, rank = core_ref.shape
    mine, other = mine_ref[...] * factor, other_ref[...] * factor
    first = core_bit() == 0
    packed = jnp.concatenate([jnp.where(first, mine, other), jnp.where(first, other, mine)], 0)
    flat_ref[...] = packed.T
    for c in range(width):
        core_ref[c] = flat_ref[pl.ds(c, offsets, stride=SLAB), :]
    for j in range(4):
        turned_ref[pl.ds(j, rank // 4, stride=4), :] = flat_ref[pl.ds(width + j, rank // 4, stride=SLAB), :]
    left_ref[...] = turned_ref[...].T
    right_ref[...] = flat_ref[offsets * SLAB : offsets * SLAB + rank, :].T


def shifted(block, axis, distance):
    count = lax.axis_size(axis)
    return lax.ppermute(block, axis, [(i, (i + distance) % count) for i in range(count)])


def crossed(block, mask):
    return lax.ppermute(block, "leaf", [(i, i ^ mask) for i in range(lax.axis_size("leaf"))])


def outward(block, chips):
    count = lax.axis_size("leaf")
    return lax.ppermute(
        block, "leaf", [(i, (i + (2 * chips if i % 2 == 0 else -2 * chips)) % count) for i in range(count)]
    )


def leaf_sum(mine, give):
    mine = mine + crossed(give, 1)
    for masks in ((8,), (2, 6, 4), (16, 48, 32)):
        mine = mine + sum(crossed(mine, mask) for mask in masks)
    return mine, crossed(mine, 1)


def struct(shape, dtype):
    return jax.ShapeDtypeStruct(shape, dtype)


def body(features, in_factor, core, out_factor, neighbours, halo_blocks, row_mask, cotangent):
    channels, rows = features.shape
    offsets, width, rank = core.shape
    near, slots = halo_blocks.shape[1:]
    table_rows = (rows + near * slots * 64) // LOW * SLAB
    packed_width = (offsets * SLAB + 127) // 128 * 128
    keep = row_mask.reshape(1, rows)
    halo = halo_blocks[0]
    core_rows = jnp.pad(core, ((0, 0), (0, SLAB - width), (0, 0))).reshape(offsets * SLAB, rank)
    estimate = pl.CostEstimate(flops=5 * 10**9, bytes_accessed=2**20, transcendentals=0)

    own_reduced, own_mixed, *payload = pl.pallas_call(
        project_kernel,
        out_shape=[struct((SLAB, rows), F32), struct((rank, rows), F32)] + [struct((SLAB + rank, rows), BF)] * 3,
        in_specs=[VMEM] * 4,
        out_specs=[VMEM] * 5,
        name="project",
    )(features, in_factor, cotangent, out_factor)
    arrived = {j: shifted(payload[j - 1], "chan", j) for j in (1, 3, 2)}

    triple = struct((3 * SLAB, rows), F32)
    grad_mixed, own, kept, cross = pl.pallas_call(
        scatter_kernel,
        out_shape=[struct((rank, rows), BF), struct((SLAB, rows), F32), triple, struct((6 * SLAB, rows), BF)],
        in_specs=[SMEM] + [VMEM] * 8,
        out_specs=[VMEM] * 4,
        scratch_shapes=[pltpu.VMEM((offsets * SLAB, rows), BF), pltpu.VMEM((table_rows, LOW), F32)],
        compiler_params=ROOMY,
        cost_estimate=estimate,
        name="scatter",
    )(halo, own_reduced, own_mixed, arrived[1], arrived[3], arrived[2], keep, core_rows, neighbours)

    def slabs_of(block, first, last):
        return block[first * SLAB : last * SLAB]

    reduced = slabs_of(cross, 0, 1)
    handed = crossed(cross, 1)
    pair = slabs_of(handed, 0, 1)
    far_other, far_same, near_other, near_same, mine = (
        slabs_of(handed, i, i + 1).astype(F32) for i in range(1, 6)
    )
    to_near = [slabs_of(kept, 0, 1) + near_same, slabs_of(kept, 1, 2) + near_other]
    to_far = [slabs_of(kept, 2, 3) + far_same, far_other]
    near = outward(jnp.concatenate([reduced, pair] + [x.astype(BF) for x in to_near], 0), 1)
    far = outward(jnp.concatenate([reduced, pair] + [x.astype(BF) for x in to_far], 0), 2)
    per_peer = slots * 64 // LOW
    near_tiles = rows // LOW + per_peer
    found = pl.pallas_call(
        near_gather_kernel,
        out_shape=struct((offsets * SLAB, rows), BF),
        in_specs=[SMEM] + [VMEM] * 3,
        out_specs=VMEM,
        scratch_shapes=[pltpu.VMEM((near_tiles * SLAB, LOW), BF)],
        compiler_params=ROOMY,
        cost_estimate=estimate,
        name="near_gather",
    )(halo, reduced, pair, neighbours)
    near, far, found = lax.optimization_barrier((near, far, found))
    near_pair, far_pair = slabs_of(near, 0, 2), slabs_of(far, 0, 2)
    passed = slabs_of(near, 3, 4).astype(F32) + slabs_of(far, 3, 4).astype(F32)
    beyond = crossed(jnp.concatenate([near_pair, far_pair, passed.astype(BF)], 0), 1)
    returned = (slabs_of(near, 2, 3).astype(F32) + slabs_of(far, 2, 3).astype(F32)) + slabs_of(beyond, 4, 5).astype(F32)
    grad_slab = (((own + mine) + returned) * keep.astype(F32)).astype(BF)

    mixed_part, gathered = pl.pallas_call(
        far_gather_kernel,
        out_shape=[struct((rank, rows), F32), struct((packed_width, rows), BF)],
        in_specs=[SMEM] + [VMEM] * 6,
        out_specs=[VMEM] * 2,
        scratch_shapes=[pltpu.VMEM((table_rows - near_tiles * SLAB, LOW), BF)],
        compiler_params=ROOMY,
        cost_estimate=estimate,
        name="far_gather",
    )(halo, found, near_pair, far_pair, beyond, core_rows, neighbours)
    grad_core = pl.pallas_call(
        core_gradient_kernel,
        out_shape=struct((rank, packed_width), F32),
        in_specs=[VMEM] * 2,
        out_specs=VMEM,
        compiler_params=SNUG,
        cost_estimate=pl.CostEstimate(flops=5 * 10**8, bytes_accessed=2**20, transcendentals=0),
        name="core_gradient",
    )(grad_mixed, gathered)

    shared = jnp.concatenate([grad_slab, mixed_part.astype(BF)], 0)
    exchanged = [shared] + [shifted(shared, "chan", j) for j in (1, 3, 2)]

    half = struct((rank // 2, packed_width), F32)
    grad_features, output, mine, give = pl.pallas_call(
        finish_kernel,
        out_shape=[struct((channels, rows), BF)] * 2 + [half] * 2,
        in_specs=[VMEM] * 10,
        out_specs=[VMEM] * 4,
        compiler_params=SNUG,
        name="finish",
    )(mixed_part, *exchanged, in_factor, features, out_factor, cotangent, grad_core)
    mine, other = leaf_sum(mine, give)

    factor = float(rows * lax.axis_size("leaf")) ** (-0.5)
    grad_in, grad_core, grad_out = pl.pallas_call(
        lambda *refs: unpack_kernel(factor, *refs),
        out_shape=[struct((channels, rank), F32), struct((width, offsets, rank), F32), struct((rank, channels), F32)],
        in_specs=[VMEM] * 2,
        out_specs=[VMEM] * 3,
        scratch_shapes=[pltpu.VMEM((packed_width, rank), F32), pltpu.VMEM((rank, channels), F32)],
        compiler_params=SNUG,
        name="unpack",
    )(mine, other)
    return (output, grad_features, grad_in, jnp.transpose(grad_core, (1, 0, 2)), grad_out)


def solution(mesh):
    placed = (
        P("chan", "leaf"),
        P("chan", None),
        P(None, "chan", None),
        P(None, "chan"),
        P(None, "leaf"),
        P("leaf", None, None),
        P("leaf"),
        P("chan", "leaf"),
    )
    return jax.shard_map(
        body,
        mesh=mesh,
        in_specs=placed,
        out_specs=(
            P("chan", "leaf"),
            P("chan", "leaf"),
            P("chan", None),
            P(None, "chan", None),
            P(None, "chan"),
        ),
        check_vma=False,
    )
```

```python
import jax
import jax.numpy as jnp
from jax import lax
from jax.experimental import pallas as pl
from jax.experimental.pallas import tpu as pltpu
from jax.sharding import PartitionSpec as P

BF = jnp.bfloat16
F32 = jnp.float32
LOW = 256
SLAB = 16
VMEM = pl.BlockSpec(memory_space=pltpu.VMEM)
SMEM = pl.BlockSpec(memory_space=pltpu.SMEM)
ROOMY = pltpu.CompilerParams(vmem_limit_bytes=40 * 2**20)
SNUG = pltpu.CompilerParams(vmem_limit_bytes=12 * 2**20)


def dot(a, b, contract=((1,), (0,))):
    return lax.dot_general(a, b, (contract, ((), ())), preferred_element_type=F32)


NT = ((1,), (1,))
TN = ((0,), (0,))


def rank_picker(shape, slab_dim, group, group_count, width, sign):
    padded = lax.broadcasted_iota(jnp.int32, shape, slab_dim)
    rank = lax.broadcasted_iota(jnp.int32, shape, 1 - slab_dim)
    step = padded // SLAB
    lane = padded % SLAB
    slab = lax.rem(group + sign * step + group_count, group_count)
    hit = (rank == slab * width + lane) & (lane < width)
    return jnp.where(hit, 1.0, 0.0).astype(BF)


def project_kernel(feat_ref, in_ref, cot_ref, outf_ref, mask_ref, own_ref, *payload_refs):
    group_count = 1 + len(payload_refs)
    rank = in_ref.shape[1]
    width = rank // group_count
    pick = rank_picker((group_count * SLAB, rank), 0, lax.axis_index("chan"), group_count, width, 1)
    weights = dot(pick, in_ref[...], NT).astype(BF)
    reduced = dot(weights, feat_ref[...]) * mask_ref[...].astype(F32)
    grad_mixed = dot(outf_ref[...], cot_ref[...])
    own_ref[0:SLAB, :] = reduced[:SLAB]
    own_ref[SLAB:, :] = grad_mixed
    for j, payload_ref in enumerate(payload_refs):
        payload_ref[0:SLAB, :] = reduced[(j + 1) * SLAB : (j + 2) * SLAB].astype(BF)
        payload_ref[SLAB:, :] = grad_mixed.astype(BF)


def low_onehot(low):
    shape = (LOW, low.shape[1])
    want = jnp.broadcast_to(low.astype(F32), shape).astype(BF)
    have = lax.broadcasted_iota(jnp.int32, shape, 0).astype(F32).astype(BF)
    return jnp.where(have == want, jnp.ones((), BF), jnp.zeros((), BF))


def core_bit():
    return lax.axis_index("leaf") % 2


def first_octant(halo_ref, slot):
    return jnp.clip(halo_ref[slot, 0] & 15, 0, 8) * 64


def mirrored(core, view, near):
    return jnp.where(core == 0, view, near - 1 - view)


def scatter_kernel(halo_ref, p0, p1, p2, p3, core_ref, nbr_ref, gm_ref, own_ref, kept_ref,
                   cross_ref, terms_ref, acc_ref):
    rows = nbr_ref.shape[1]
    tiles = acc_ref.shape[0] // SLAB
    total = (p0[...] + p1[...].astype(F32)) + (p2[...].astype(F32) + p3[...].astype(F32))
    cross_ref[0:SLAB, :] = total[:SLAB].astype(BF)
    grad_mixed = total[SLAB:].astype(BF)
    gm_ref[...] = grad_mixed
    terms_ref[...] = dot(core_ref[...], grad_mixed).astype(BF)
    acc_ref[...] = jnp.zeros_like(acc_ref)

    def step(k, carry):
        index = nbr_ref[pl.ds(k, 1), :]
        onehot = low_onehot(index & (LOW - 1))
        high = jnp.broadcast_to((index >> 8).astype(F32), (SLAB, rows)).astype(BF)
        terms = terms_ref[pl.ds(pl.multiple_of(k * SLAB, SLAB), SLAB), :]
        spread = jnp.concatenate(
            [jnp.where(high == jnp.full((), t, BF), terms, jnp.zeros((), BF)) for t in range(tiles)], 0
        )
        acc_ref[...] += dot(spread, onehot, NT)
        return carry

    offsets = nbr_ref.shape[0]
    middle = offsets // 2
    lax.fori_loop(0, offsets - 1, lambda i, carry: step(i + (i >= middle), carry), 0, unroll=13)

    def tile(t):
        return acc_ref[pl.ds(pl.multiple_of(t * SLAB, SLAB), SLAB), :]

    own_tiles = rows // LOW
    itself = terms_ref[middle * SLAB : (middle + 1) * SLAB, :].astype(F32)
    own_ref[...] = jnp.concatenate([tile(t) for t in range(own_tiles)], 1) + itself
    near = halo_ref.shape[0]
    per_peer = (tiles - own_tiles) // near
    blank = jnp.zeros((SLAB, rows - per_peer * LOW), F32)
    for view in range(near):
        slot = mirrored(core_bit(), view, near)
        start = own_tiles + slot * per_peer
        window = jnp.concatenate([tile(start + i) for i in range(per_peer)] + [blank], 1)
        block = pltpu.roll(window, first_octant(halo_ref, slot), 1)
        if view < 5:
            cross_ref[(view + 1) * SLAB : (view + 2) * SLAB, :] = block.astype(BF)
        else:
            kept_ref[(view - 5) * SLAB : (view - 4) * SLAB, :] = block


def pick_rows(table_ref, nbr_ref, highs, start_of, store):
    rows = nbr_ref.shape[1]
    offsets = nbr_ref.shape[0]
    middle = offsets // 2

    def step(i, carry):
        k = i + (i >= middle)
        index = nbr_ref[pl.ds(k, 1), :]
        onehot = low_onehot(index & (LOW - 1))
        high = jnp.broadcast_to(index >> 8, (SLAB, rows))
        picked = dot(table_ref[...], onehot)
        place = pl.ds(pl.multiple_of(k * SLAB, SLAB), SLAB)
        found = start_of(place)
        for t, value in enumerate(highs):
            found = jnp.where(high == value, picked[t * SLAB : (t + 1) * SLAB], found)
        store(place, found.astype(BF))
        return carry

    lax.fori_loop(0, offsets - 1, step, 0, unroll=13)


def fill_window(table_ref, at, block, halo_ref, slot, per_peer):
    rows = block.shape[1]
    window = pltpu.roll(block.astype(F32), rows - first_octant(halo_ref, slot), 1).astype(BF)
    for i in range(per_peer):
        table_ref[at + i * SLAB : at + (i + 1) * SLAB, :] = window[:, i * LOW : (i + 1) * LOW]


def near_gather_kernel(halo_ref, own_ref, pair_ref, nbr_ref, ga_ref, table_ref):
    rows = nbr_ref.shape[1]
    own_tiles = rows // LOW
    per_peer = table_ref.shape[0] // SLAB - own_tiles
    for t in range(own_tiles):
        table_ref[t * SLAB : (t + 1) * SLAB, :] = own_ref[:, t * LOW : (t + 1) * LOW]
    slot = mirrored(core_bit(), 4, halo_ref.shape[0])
    fill_window(table_ref, own_tiles * SLAB, pair_ref[...], halo_ref, slot, per_peer)
    highs = list(range(own_tiles)) + [own_tiles + slot * per_peer + i for i in range(per_peer)]
    middle = nbr_ref.shape[0] // 2

    def store(place, found):
        ga_ref[place, :] = found

    pick_rows(table_ref, nbr_ref, highs, lambda place: jnp.zeros((SLAB, rows), F32), store)
    ga_ref[middle * SLAB : (middle + 1) * SLAB, :] = own_ref[...]


def far_gather_kernel(halo_ref, base_ref, near_ref, far_ref, cross_ref, core_ref, nbr_ref, mix_ref, ga_ref,
                      table_ref):
    rows = nbr_ref.shape[1]
    own_tiles = rows // LOW
    near = halo_ref.shape[0]
    views = {
        0: far_ref[0:SLAB, :],
        1: far_ref[SLAB:, :],
        2: near_ref[0:SLAB, :],
        3: near_ref[SLAB:, :],
        5: cross_ref[SLAB : 2 * SLAB, :],
        6: cross_ref[0:SLAB, :],
        7: cross_ref[3 * SLAB : 4 * SLAB, :],
    }
    per_peer = table_ref.shape[0] // SLAB // len(views)
    highs = []
    for n, (view, block) in enumerate(views.items()):
        slot = mirrored(core_bit(), view, near)
        fill_window(table_ref, n * per_peer * SLAB, block, halo_ref, slot, per_peer)
        highs += [own_tiles + slot * per_peer + i for i in range(per_peer)]
    used = core_ref.shape[0]
    middle = nbr_ref.shape[0] // 2
    itself = slice(middle * SLAB, (middle + 1) * SLAB)

    def store(place, found):
        ga_ref[place, :] = found

    pick_rows(table_ref, nbr_ref, highs, lambda place: base_ref[place, :].astype(F32), store)
    ga_ref[itself, :] = base_ref[itself, :]
    ga_ref[used:, :] = jnp.zeros_like(ga_ref[used:, :])
    mix_ref[...] = dot(core_ref[...], ga_ref[:used, :], TN)


def core_gradient_kernel(gm_ref, ga_ref, gc_ref):
    gc_ref[...] = dot(gm_ref[...], ga_ref[...], NT)


def sums_kernel(mix_ref, e0, e2, e3, e1, feat_ref, cot_ref, gc_ref, keep_ref, give_ref, rows_ref, mixed_ref):
    rank, rows = mix_ref.shape
    wide = gc_ref.shape[1]
    group = lax.axis_index("chan")
    pick = rank_picker((rank, 4 * SLAB), 1, group, 4, rank // 4, -1)
    slabs = jnp.concatenate([e[0:SLAB, :] for e in (e0, e1, e2, e3)], 0)
    grad_rows = dot(pick, slabs).astype(BF)
    rows_ref[...] = grad_rows
    total = (mix_ref[...] + e1[SLAB:, :].astype(F32)) + (e2[SLAB:, :].astype(F32) + e3[SLAB:, :].astype(F32))
    mixed = total.astype(BF)
    mixed_ref[...] = mixed
    column = lax.broadcasted_iota(jnp.int32, (wide, rank), 0)
    wanted = lax.broadcasted_iota(jnp.int32, (wide, rank), 1)
    free = column % SLAB - (SLAB - 4)
    place = jnp.where((free >= 0) & (column // SLAB * 4 + free == wanted), 1.0, 0.0).astype(BF)
    left = dot(feat_ref[...], grad_rows, NT)
    high = left.astype(BF)
    rest = left - high.astype(F32)
    middle = rest.astype(BF)
    low = (rest - middle.astype(F32)).astype(BF)
    right = jnp.concatenate([jnp.zeros((48, rows), BF), cot_ref[...], jnp.zeros((32, rows), BF)], 0)
    tail = dot(mixed, right, NT)
    packed = gc_ref[...] + (dot(high, place, NT) + dot(middle, place, NT) + dot(low, place, NT))
    packed = jnp.concatenate([packed[:, : wide - 128], packed[:, wide - 128 :] + tail], 1)
    half = rank // 2
    first = core_bit() == 0
    keep_ref[...] = jnp.where(first, packed[:half], packed[half:])
    give_ref[...] = jnp.where(first, packed[half:], packed[:half])


def outputs_kernel(rows_ref, mixed_ref, in_ref, outf_ref, gf_ref, out_ref):
    gf_ref[...] = dot(in_ref[...], rows_ref[...]).astype(BF)
    out_ref[...] = dot(outf_ref[...], mixed_ref[...], TN).astype(BF)


def unpack_kernel(factor, mine_ref, other_ref, left_ref, core_ref, right_ref, flat_ref, turned_ref):
    width, offsets, rank = core_ref.shape
    mine, other = mine_ref[...] * factor, other_ref[...] * factor
    first = core_bit() == 0
    packed = jnp.concatenate([jnp.where(first, mine, other), jnp.where(first, other, mine)], 0)
    flat_ref[...] = packed.T
    for c in range(width):
        core_ref[c] = flat_ref[pl.ds(c, offsets, stride=SLAB), :]
    for j in range(4):
        turned_ref[pl.ds(j, rank // 4, stride=4), :] = flat_ref[pl.ds(width + j, rank // 4, stride=SLAB), :]
    left_ref[...] = turned_ref[...].T
    right_ref[...] = flat_ref[offsets * SLAB : offsets * SLAB + rank, :].T


def shifted(block, axis, distance):
    count = lax.axis_size(axis)
    return lax.ppermute(block, axis, [(i, (i + distance) % count) for i in range(count)])


def crossed(block, mask):
    return lax.ppermute(block, "leaf", [(i, i ^ mask) for i in range(lax.axis_size("leaf"))])


def outward(block, chips):
    count = lax.axis_size("leaf")
    return lax.ppermute(
        block, "leaf", [(i, (i + (2 * chips if i % 2 == 0 else -2 * chips)) % count) for i in range(count)]
    )


def leaf_sum(mine, give):
    mine = mine + crossed(give, 1)
    for masks in ((8,), (2, 6, 4), (16, 48, 32)):
        mine = mine + sum(crossed(mine, mask) for mask in masks)
    return mine, crossed(mine, 1)


def struct(shape, dtype):
    return jax.ShapeDtypeStruct(shape, dtype)


def body(features, in_factor, core, out_factor, neighbours, halo_blocks, row_mask, cotangent):
    channels, rows = features.shape
    offsets, width, rank = core.shape
    near, slots = halo_blocks.shape[1:]
    table_rows = (rows + near * slots * 64) // LOW * SLAB
    packed_width = (offsets * SLAB + 127) // 128 * 128
    keep = row_mask.reshape(1, rows)
    halo = halo_blocks[0]
    core_rows = jnp.pad(core, ((0, 0), (0, SLAB - width), (0, 0))).reshape(offsets * SLAB, rank)
    estimate = pl.CostEstimate(flops=5 * 10**9, bytes_accessed=2**20, transcendentals=0)

    own_payload, *payload = pl.pallas_call(
        project_kernel,
        out_shape=[struct((SLAB + rank, rows), F32)] + [struct((SLAB + rank, rows), BF)] * 3,
        in_specs=[VMEM] * 5,
        out_specs=[VMEM] * 4,
        name="project",
    )(features, in_factor, cotangent, out_factor, keep)
    arrived = {j: shifted(payload[j - 1], "chan", j) for j in (1, 3, 2)}

    triple = struct((3 * SLAB, rows), F32)
    grad_mixed, own, kept, cross = pl.pallas_call(
        scatter_kernel,
        out_shape=[struct((rank, rows), BF), struct((SLAB, rows), F32), triple, struct((6 * SLAB, rows), BF)],
        in_specs=[SMEM] + [VMEM] * 6,
        out_specs=[VMEM] * 4,
        scratch_shapes=[pltpu.VMEM((offsets * SLAB, rows), BF), pltpu.VMEM((table_rows, LOW), F32)],
        compiler_params=ROOMY,
        cost_estimate=estimate,
        name="scatter",
    )(halo, own_payload, arrived[1], arrived[3], arrived[2], core_rows, neighbours)

    def slabs_of(block, first, last):
        return block[first * SLAB : last * SLAB]

    reduced = slabs_of(cross, 0, 1)
    handed = crossed(cross, 1)
    pair = slabs_of(handed, 0, 1)
    far_other, far_same, near_other, near_same, mine = (
        slabs_of(handed, i, i + 1).astype(F32) for i in range(1, 6)
    )
    to_near = [slabs_of(kept, 0, 1) + near_same, slabs_of(kept, 1, 2) + near_other]
    to_far = [slabs_of(kept, 2, 3) + far_same, far_other]
    near = outward(jnp.concatenate([reduced, pair] + [x.astype(BF) for x in to_near], 0), 1)
    far = outward(jnp.concatenate([reduced, pair] + [x.astype(BF) for x in to_far], 0), 2)
    per_peer = slots * 64 // LOW
    near_tiles = rows // LOW + per_peer
    found = pl.pallas_call(
        near_gather_kernel,
        out_shape=struct((offsets * SLAB, rows), BF),
        in_specs=[SMEM] + [VMEM] * 3,
        out_specs=VMEM,
        scratch_shapes=[pltpu.VMEM((near_tiles * SLAB, LOW), BF)],
        compiler_params=ROOMY,
        cost_estimate=estimate,
        name="near_gather",
    )(halo, reduced, pair, neighbours)
    near, far, found = lax.optimization_barrier((near, far, found))
    near_pair, far_pair = slabs_of(near, 0, 2), slabs_of(far, 0, 2)
    passed = slabs_of(near, 3, 4).astype(F32) + slabs_of(far, 3, 4).astype(F32)
    beyond = crossed(jnp.concatenate([near_pair, far_pair, passed.astype(BF)], 0), 1)
    returned = (slabs_of(near, 2, 3).astype(F32) + slabs_of(far, 2, 3).astype(F32)) + slabs_of(beyond, 4, 5).astype(F32)
    grad_slab = (((own + mine) + returned) * keep.astype(F32)).astype(BF)

    mixed_part, gathered = pl.pallas_call(
        far_gather_kernel,
        out_shape=[struct((rank, rows), F32), struct((packed_width, rows), BF)],
        in_specs=[SMEM] + [VMEM] * 6,
        out_specs=[VMEM] * 2,
        scratch_shapes=[pltpu.VMEM((table_rows - near_tiles * SLAB, LOW), BF)],
        compiler_params=ROOMY,
        cost_estimate=estimate,
        name="far_gather",
    )(halo, found, near_pair, far_pair, beyond, core_rows, neighbours)
    grad_core = pl.pallas_call(
        core_gradient_kernel,
        out_shape=struct((rank, packed_width), F32),
        in_specs=[VMEM] * 2,
        out_specs=VMEM,
        compiler_params=SNUG,
        cost_estimate=pl.CostEstimate(flops=5 * 10**8, bytes_accessed=2**20, transcendentals=0),
        name="core_gradient",
    )(grad_mixed, gathered)

    shared = jnp.concatenate([grad_slab, mixed_part.astype(BF)], 0)
    exchanged = [shared] + [shifted(shared, "chan", j) for j in (2, 3, 1)]

    sums, full = struct((rank // 2, packed_width), F32), struct((rank, rows), BF)
    mine, give, grad_rows, mixed = pl.pallas_call(
        sums_kernel,
        out_shape=[sums, sums, full, full],
        in_specs=[VMEM] * 8,
        out_specs=[VMEM] * 4,
        compiler_params=SNUG,
        name="sums",
    )(mixed_part, *exchanged, features, cotangent, grad_core)
    grad_features, output = pl.pallas_call(
        outputs_kernel,
        out_shape=[struct((channels, rows), BF)] * 2,
        in_specs=[VMEM] * 4,
        out_specs=[VMEM] * 2,
        compiler_params=SNUG,
        cost_estimate=pl.CostEstimate(flops=5 * 10**8, bytes_accessed=2**20, transcendentals=0),
        name="outputs",
    )(grad_rows, mixed, in_factor, out_factor)
    mine, other = leaf_sum(mine, give)

    factor = float(rows * lax.axis_size("leaf")) ** (-0.5)
    grad_in, grad_core, grad_out = pl.pallas_call(
        lambda *refs: unpack_kernel(factor, *refs),
        out_shape=[struct((channels, rank), F32), struct((width, offsets, rank), F32), struct((rank, channels), F32)],
        in_specs=[VMEM] * 2,
        out_specs=[VMEM] * 3,
        scratch_shapes=[pltpu.VMEM((packed_width, rank), F32), pltpu.VMEM((rank, channels), F32)],
        compiler_params=SNUG,
        name="unpack",
    )(mine, other)
    return (output, grad_features, grad_in, jnp.transpose(grad_core, (1, 0, 2)), grad_out)


def solution(mesh):
    placed = (
        P("chan", "leaf"),
        P("chan", None),
        P(None, "chan", None),
        P(None, "chan"),
        P(None, "leaf"),
        P("leaf", None, None),
        P("leaf"),
        P("chan", "leaf"),
    )
    return jax.shard_map(
        body,
        mesh=mesh,
        in_specs=placed,
        out_specs=(
            P("chan", "leaf"),
            P("chan", "leaf"),
            P("chan", None),
            P(None, "chan", None),
            P(None, "chan"),
        ),
        check_vma=False,
    )
```

```python
import jax
import jax.numpy as jnp
from jax import lax
from jax.experimental import pallas as pl
from jax.experimental.pallas import tpu as pltpu
from jax.sharding import PartitionSpec as P

BF = jnp.bfloat16
F32 = jnp.float32
LOW = 256
SLAB = 16
VMEM = pl.BlockSpec(memory_space=pltpu.VMEM)
SMEM = pl.BlockSpec(memory_space=pltpu.SMEM)
ROOMY = pltpu.CompilerParams(vmem_limit_bytes=40 * 2**20)
SNUG = pltpu.CompilerParams(vmem_limit_bytes=12 * 2**20)


def dot(a, b, contract=((1,), (0,))):
    return lax.dot_general(a, b, (contract, ((), ())), preferred_element_type=F32)


NT = ((1,), (1,))
TN = ((0,), (0,))


def rank_picker(shape, slab_dim, group, group_count, width, sign):
    padded = lax.broadcasted_iota(jnp.int32, shape, slab_dim)
    rank = lax.broadcasted_iota(jnp.int32, shape, 1 - slab_dim)
    step = padded // SLAB
    lane = padded % SLAB
    slab = lax.rem(group + sign * step + group_count, group_count)
    hit = (rank == slab * width + lane) & (lane < width)
    return jnp.where(hit, 1.0, 0.0).astype(BF)


def project_kernel(feat_ref, in_ref, cot_ref, outf_ref, mask_ref, own_ref, *payload_refs):
    group_count = 1 + len(payload_refs)
    rank = in_ref.shape[1]
    width = rank // group_count
    pick = rank_picker((group_count * SLAB, rank), 0, lax.axis_index("chan"), group_count, width, 1)
    weights = dot(pick, in_ref[...], NT).astype(BF)
    reduced = dot(weights, feat_ref[...]) * mask_ref[...].astype(F32)
    grad_mixed = dot(outf_ref[...], cot_ref[...])
    own_ref[0:SLAB, :] = reduced[:SLAB]
    own_ref[SLAB:, :] = grad_mixed
    for j, payload_ref in enumerate(payload_refs):
        payload_ref[0:SLAB, :] = reduced[(j + 1) * SLAB : (j + 2) * SLAB].astype(BF)
        payload_ref[SLAB:, :] = grad_mixed.astype(BF)


def low_onehot(low):
    shape = (LOW, low.shape[1])
    want = jnp.broadcast_to(low.astype(F32), shape).astype(BF)
    have = lax.broadcasted_iota(jnp.int32, shape, 0).astype(F32).astype(BF)
    return jnp.where(have == want, jnp.ones((), BF), jnp.zeros((), BF))


def core_bit():
    return lax.axis_index("leaf") % 2


def first_octant(halo_ref, slot):
    return jnp.clip(halo_ref[slot, 0] & 15, 0, 8) * 64


def mirrored(core, view, near):
    return jnp.where(core == 0, view, near - 1 - view)


def scatter_kernel(halo_ref, p0, p1, p2, p3, core_ref, nbr_ref, gm_ref, own_ref, kept_ref,
                   cross_ref, terms_ref, acc_ref):
    rows = nbr_ref.shape[1]
    tiles = acc_ref.shape[0] // SLAB
    total = (p0[...] + p1[...].astype(F32)) + (p2[...].astype(F32) + p3[...].astype(F32))
    cross_ref[0:SLAB, :] = total[:SLAB].astype(BF)
    grad_mixed = total[SLAB:].astype(BF)
    gm_ref[...] = grad_mixed
    terms_ref[...] = dot(core_ref[...], grad_mixed).astype(BF)
    acc_ref[...] = jnp.zeros_like(acc_ref)

    def step(k, carry):
        index = nbr_ref[pl.ds(k, 1), :]
        onehot = low_onehot(index & (LOW - 1))
        high = jnp.broadcast_to((index >> 8).astype(F32), (SLAB, rows)).astype(BF)
        terms = terms_ref[pl.ds(pl.multiple_of(k * SLAB, SLAB), SLAB), :]
        spread = jnp.concatenate(
            [jnp.where(high == jnp.full((), t, BF), terms, jnp.zeros((), BF)) for t in range(tiles)], 0
        )
        acc_ref[...] += dot(spread, onehot, NT)
        return carry

    offsets = nbr_ref.shape[0]
    middle = offsets // 2
    lax.fori_loop(0, offsets - 1, lambda i, carry: step(i + (i >= middle), carry), 0, unroll=13)

    def tile(t):
        return acc_ref[pl.ds(pl.multiple_of(t * SLAB, SLAB), SLAB), :]

    own_tiles = rows // LOW
    itself = terms_ref[middle * SLAB : (middle + 1) * SLAB, :].astype(F32)
    own_ref[...] = jnp.concatenate([tile(t) for t in range(own_tiles)], 1) + itself
    near = halo_ref.shape[0]
    per_peer = (tiles - own_tiles) // near
    blank = jnp.zeros((SLAB, rows - per_peer * LOW), F32)
    for view in range(near):
        slot = mirrored(core_bit(), view, near)
        start = own_tiles + slot * per_peer
        window = jnp.concatenate([tile(start + i) for i in range(per_peer)] + [blank], 1)
        block = pltpu.roll(window, first_octant(halo_ref, slot), 1)
        if view < 5:
            cross_ref[(view + 1) * SLAB : (view + 2) * SLAB, :] = block.astype(BF)
        else:
            kept_ref[(view - 5) * SLAB : (view - 4) * SLAB, :] = block


def offset_index(nbr_ref, i):
    middle = nbr_ref.shape[0] // 2
    k = i + (i >= middle)
    index = nbr_ref[pl.ds(k, 1), :]
    return pl.ds(pl.multiple_of(k * SLAB, SLAB), SLAB), low_onehot(index & (LOW - 1)), index >> 8


def window_of(block, halo_ref, slot):
    return pltpu.roll(block.astype(F32), block.shape[1] - first_octant(halo_ref, slot), 1)


def near_gather_kernel(halo_ref, own_ref, pair_ref, nbr_ref, ga_ref, table_ref):
    offsets, rows = nbr_ref.shape
    own_tiles = rows // LOW
    per_peer = table_ref.shape[0] // SLAB - own_tiles
    for t in range(own_tiles):
        table_ref[t * SLAB : (t + 1) * SLAB, :] = own_ref[:, t * LOW : (t + 1) * LOW]
    slot = mirrored(core_bit(), 4, halo_ref.shape[0])
    window = window_of(pair_ref[...], halo_ref, slot).astype(BF)
    for i in range(per_peer):
        t = own_tiles + i
        table_ref[t * SLAB : (t + 1) * SLAB, :] = window[:, i * LOW : (i + 1) * LOW]
    highs = list(range(own_tiles)) + [own_tiles + slot * per_peer + i for i in range(per_peer)]

    def step(i, carry):
        place, onehot, high = offset_index(nbr_ref, i)
        high = jnp.broadcast_to(high, (SLAB, rows))
        picked = dot(table_ref[...], onehot)
        found = jnp.zeros((SLAB, rows), F32)
        for t, value in enumerate(highs):
            found = jnp.where(high == value, picked[t * SLAB : (t + 1) * SLAB], found)
        ga_ref[place, :] = found.astype(BF)
        return carry

    lax.fori_loop(0, offsets - 1, step, 0, unroll=13)
    middle = offsets // 2
    ga_ref[middle * SLAB : (middle + 1) * SLAB, :] = own_ref[...]


def far_gather_kernel(halo_ref, base_ref, near_ref, far_ref, cross_ref, core_ref, nbr_ref, mix_ref, ga_ref,
                      wide_ref, table_ref):
    offsets, rows = nbr_ref.shape
    own_tiles = rows // LOW
    near = halo_ref.shape[0]
    views = {
        0: far_ref[0:SLAB, :],
        1: far_ref[SLAB:, :],
        2: near_ref[0:SLAB, :],
        3: near_ref[SLAB:, :],
        5: cross_ref[SLAB : 2 * SLAB, :],
        6: cross_ref[0:SLAB, :],
        7: cross_ref[3 * SLAB : 4 * SLAB, :],
    }
    both = table_ref.shape[0] // len(views)
    width = both // 2
    highs = []
    for n, (view, block) in enumerate(views.items()):
        slot = mirrored(core_bit(), view, near)
        window = window_of(block, halo_ref, slot)
        wide_ref[n * both : n * both + width, :] = window[:width, :LOW]
        wide_ref[n * both + width : (n + 1) * both, :] = window[:width, LOW : 2 * LOW]
        highs.append(own_tiles + 2 * slot)
    table_ref[...] = wide_ref[...].astype(BF)
    second = (lax.broadcasted_iota(jnp.int32, (both, rows), 0) >= width).astype(jnp.int32)

    def step(i, carry):
        place, onehot, high = offset_index(nbr_ref, i)
        high = jnp.broadcast_to(high, (both, rows)) - second
        picked = dot(table_ref[...], onehot)
        found = jnp.zeros((both, rows), F32)
        for n, value in enumerate(highs):
            found = jnp.where(high == value, picked[n * both : (n + 1) * both], found)
        found = jnp.concatenate([found[:width] + found[width:], jnp.zeros((SLAB - width, rows), F32)], 0)
        ga_ref[place, :] = (base_ref[place, :].astype(F32) + found).astype(BF)
        return carry

    lax.fori_loop(0, offsets - 1, step, 0, unroll=13)
    used = core_ref.shape[0]
    middle = offsets // 2
    itself = slice(middle * SLAB, (middle + 1) * SLAB)
    ga_ref[itself, :] = base_ref[itself, :]
    ga_ref[used:, :] = jnp.zeros_like(ga_ref[used:, :])
    mix_ref[...] = dot(core_ref[...], ga_ref[:used, :], TN)


def core_gradient_kernel(gm_ref, ga_ref, gc_ref):
    gc_ref[...] = dot(gm_ref[...], ga_ref[...], NT)


def sums_kernel(mix_ref, e0, e2, e3, e1, feat_ref, cot_ref, gc_ref, keep_ref, give_ref, rows_ref, mixed_ref):
    rank, rows = mix_ref.shape
    wide = gc_ref.shape[1]
    group = lax.axis_index("chan")
    pick = rank_picker((rank, 4 * SLAB), 1, group, 4, rank // 4, -1)
    slabs = jnp.concatenate([e[0:SLAB, :] for e in (e0, e1, e2, e3)], 0)
    grad_rows = dot(pick, slabs).astype(BF)
    rows_ref[...] = grad_rows
    total = (mix_ref[...] + e1[SLAB:, :].astype(F32)) + (e2[SLAB:, :].astype(F32) + e3[SLAB:, :].astype(F32))
    mixed = total.astype(BF)
    mixed_ref[...] = mixed
    column = lax.broadcasted_iota(jnp.int32, (wide, rank), 0)
    wanted = lax.broadcasted_iota(jnp.int32, (wide, rank), 1)
    free = column % SLAB - (SLAB - 4)
    place = jnp.where((free >= 0) & (column // SLAB * 4 + free == wanted), 1.0, 0.0).astype(BF)
    left = dot(feat_ref[...], grad_rows, NT)
    high = left.astype(BF)
    rest = left - high.astype(F32)
    middle = rest.astype(BF)
    low = (rest - middle.astype(F32)).astype(BF)
    right = jnp.concatenate([jnp.zeros((48, rows), BF), cot_ref[...], jnp.zeros((32, rows), BF)], 0)
    tail = dot(mixed, right, NT)
    packed = gc_ref[...] + (dot(high, place, NT) + dot(middle, place, NT) + dot(low, place, NT))
    packed = jnp.concatenate([packed[:, : wide - 128], packed[:, wide - 128 :] + tail], 1)
    half = rank // 2
    first = core_bit() == 0
    keep_ref[...] = jnp.where(first, packed[:half], packed[half:])
    give_ref[...] = jnp.where(first, packed[half:], packed[:half])


def outputs_kernel(rows_ref, mixed_ref, in_ref, outf_ref, gf_ref, out_ref):
    gf_ref[...] = dot(in_ref[...], rows_ref[...]).astype(BF)
    out_ref[...] = dot(outf_ref[...], mixed_ref[...], TN).astype(BF)


def unpack_kernel(factor, mine_ref, other_ref, left_ref, core_ref, right_ref, flat_ref, turned_ref):
    width, offsets, rank = core_ref.shape
    mine, other = mine_ref[...] * factor, other_ref[...] * factor
    first = core_bit() == 0
    packed = jnp.concatenate([jnp.where(first, mine, other), jnp.where(first, other, mine)], 0)
    flat_ref[...] = packed.T
    for c in range(width):
        core_ref[c] = flat_ref[pl.ds(c, offsets, stride=SLAB), :]
    for j in range(4):
        turned_ref[pl.ds(j, rank // 4, stride=4), :] = flat_ref[pl.ds(width + j, rank // 4, stride=SLAB), :]
    left_ref[...] = turned_ref[...].T
    right_ref[...] = flat_ref[offsets * SLAB : offsets * SLAB + rank, :].T


def shifted(block, axis, distance):
    count = lax.axis_size(axis)
    return lax.ppermute(block, axis, [(i, (i + distance) % count) for i in range(count)])


def crossed(block, mask):
    return lax.ppermute(block, "leaf", [(i, i ^ mask) for i in range(lax.axis_size("leaf"))])


def outward(block, chips):
    count = lax.axis_size("leaf")
    return lax.ppermute(
        block, "leaf", [(i, (i + (2 * chips if i % 2 == 0 else -2 * chips)) % count) for i in range(count)]
    )


def leaf_sum(mine, give):
    mine = mine + crossed(give, 1)
    for masks in ((8,), (2, 6, 4), (16, 48, 32)):
        mine = mine + sum(crossed(mine, mask) for mask in masks)
    return mine, crossed(mine, 1)


def struct(shape, dtype):
    return jax.ShapeDtypeStruct(shape, dtype)


def body(features, in_factor, core, out_factor, neighbours, halo_blocks, row_mask, cotangent):
    channels, rows = features.shape
    offsets, width, rank = core.shape
    near, slots = halo_blocks.shape[1:]
    table_rows = (rows + near * slots * 64) // LOW * SLAB
    packed_width = (offsets * SLAB + 127) // 128 * 128
    keep = row_mask.reshape(1, rows)
    halo = halo_blocks[0]
    core_rows = jnp.pad(core, ((0, 0), (0, SLAB - width), (0, 0))).reshape(offsets * SLAB, rank)
    estimate = pl.CostEstimate(flops=5 * 10**9, bytes_accessed=2**20, transcendentals=0)

    own_payload, *payload = pl.pallas_call(
        project_kernel,
        out_shape=[struct((SLAB + rank, rows), F32)] + [struct((SLAB + rank, rows), BF)] * 3,
        in_specs=[VMEM] * 5,
        out_specs=[VMEM] * 4,
        name="project",
    )(features, in_factor, cotangent, out_factor, keep)
    arrived = {j: shifted(payload[j - 1], "chan", j) for j in (1, 3, 2)}

    triple = struct((3 * SLAB, rows), F32)
    grad_mixed, own, kept, cross = pl.pallas_call(
        scatter_kernel,
        out_shape=[struct((rank, rows), BF), struct((SLAB, rows), F32), triple, struct((6 * SLAB, rows), BF)],
        in_specs=[SMEM] + [VMEM] * 6,
        out_specs=[VMEM] * 4,
        scratch_shapes=[pltpu.VMEM((offsets * SLAB, rows), BF), pltpu.VMEM((table_rows, LOW), F32)],
        compiler_params=ROOMY,
        cost_estimate=estimate,
        name="scatter",
    )(halo, own_payload, arrived[1], arrived[3], arrived[2], core_rows, neighbours)

    def slabs_of(block, first, last):
        return block[first * SLAB : last * SLAB]

    reduced = slabs_of(cross, 0, 1)
    handed = crossed(cross, 1)
    pair = slabs_of(handed, 0, 1)
    far_other, far_same, near_other, near_same, mine = (
        slabs_of(handed, i, i + 1).astype(F32) for i in range(1, 6)
    )
    to_near = [slabs_of(kept, 0, 1) + near_same, slabs_of(kept, 1, 2) + near_other]
    to_far = [slabs_of(kept, 2, 3) + far_same, far_other]
    far = outward(jnp.concatenate([reduced, pair] + [x.astype(BF) for x in to_far], 0), 2)
    near = outward(jnp.concatenate([reduced, pair] + [x.astype(BF) for x in to_near], 0), 1)
    per_peer = slots * 64 // LOW
    near_tiles = rows // LOW + per_peer
    found = pl.pallas_call(
        near_gather_kernel,
        out_shape=struct((offsets * SLAB, rows), BF),
        in_specs=[SMEM] + [VMEM] * 3,
        out_specs=VMEM,
        scratch_shapes=[pltpu.VMEM((near_tiles * SLAB, LOW), BF)],
        compiler_params=ROOMY,
        cost_estimate=estimate,
        name="near_gather",
    )(halo, reduced, pair, neighbours)
    far, near, found = lax.optimization_barrier((far, near, found))
    near_pair, far_pair = slabs_of(near, 0, 2), slabs_of(far, 0, 2)
    passed = slabs_of(near, 3, 4).astype(F32) + slabs_of(far, 3, 4).astype(F32)
    beyond = crossed(jnp.concatenate([near_pair, far_pair, passed.astype(BF)], 0), 1)
    returned = (slabs_of(near, 2, 3).astype(F32) + slabs_of(far, 2, 3).astype(F32)) + slabs_of(beyond, 4, 5).astype(F32)
    grad_slab = (((own + mine) + returned) * keep.astype(F32)).astype(BF)

    mixed_part, gathered = pl.pallas_call(
        far_gather_kernel,
        out_shape=[struct((rank, rows), F32), struct((packed_width, rows), BF)],
        in_specs=[SMEM] + [VMEM] * 6,
        out_specs=[VMEM] * 2,
        scratch_shapes=[pltpu.VMEM((14 * width, LOW), F32), pltpu.VMEM((14 * width, LOW), BF)],
        compiler_params=ROOMY,
        cost_estimate=estimate,
        name="far_gather",
    )(halo, found, near_pair, far_pair, beyond, core_rows, neighbours)
    grad_core = pl.pallas_call(
        core_gradient_kernel,
        out_shape=struct((rank, packed_width), F32),
        in_specs=[VMEM] * 2,
        out_specs=VMEM,
        compiler_params=SNUG,
        cost_estimate=pl.CostEstimate(flops=5 * 10**8, bytes_accessed=2**20, transcendentals=0),
        name="core_gradient",
    )(grad_mixed, gathered)

    shared = jnp.concatenate([grad_slab, mixed_part.astype(BF)], 0)
    exchanged = [shared] + [shifted(shared, "chan", j) for j in (2, 3, 1)]

    sums, full = struct((rank // 2, packed_width), F32), struct((rank, rows), BF)
    mine, give, grad_rows, mixed = pl.pallas_call(
        sums_kernel,
        out_shape=[sums, sums, full, full],
        in_specs=[VMEM] * 8,
        out_specs=[VMEM] * 4,
        compiler_params=SNUG,
        name="sums",
    )(mixed_part, *exchanged, features, cotangent, grad_core)
    grad_features, output = pl.pallas_call(
        outputs_kernel,
        out_shape=[struct((channels, rows), BF)] * 2,
        in_specs=[VMEM] * 4,
        out_specs=[VMEM] * 2,
        compiler_params=SNUG,
        cost_estimate=pl.CostEstimate(flops=5 * 10**8, bytes_accessed=2**20, transcendentals=0),
        name="outputs",
    )(grad_rows, mixed, in_factor, out_factor)
    mine, other = leaf_sum(mine, give)

    factor = float(rows * lax.axis_size("leaf")) ** (-0.5)
    grad_in, grad_core, grad_out = pl.pallas_call(
        lambda *refs: unpack_kernel(factor, *refs),
        out_shape=[struct((channels, rank), F32), struct((width, offsets, rank), F32), struct((rank, channels), F32)],
        in_specs=[VMEM] * 2,
        out_specs=[VMEM] * 3,
        scratch_shapes=[pltpu.VMEM((packed_width, rank), F32), pltpu.VMEM((rank, channels), F32)],
        compiler_params=SNUG,
        name="unpack",
    )(mine, other)
    return (output, grad_features, grad_in, jnp.transpose(grad_core, (1, 0, 2)), grad_out)


def solution(mesh):
    placed = (
        P("chan", "leaf"),
        P("chan", None),
        P(None, "chan", None),
        P(None, "chan"),
        P(None, "leaf"),
        P("leaf", None, None),
        P("leaf"),
        P("chan", "leaf"),
    )
    return jax.shard_map(
        body,
        mesh=mesh,
        in_specs=placed,
        out_specs=(
            P("chan", "leaf"),
            P("chan", "leaf"),
            P("chan", None),
            P(None, "chan", None),
            P(None, "chan"),
        ),
        check_vma=False,
    )
```

```python
import jax
import jax.numpy as jnp
from jax import lax
from jax.experimental import pallas as pl
from jax.experimental.pallas import tpu as pltpu
from jax.sharding import PartitionSpec as P

BF = jnp.bfloat16
F32 = jnp.float32
LOW = 256
SLAB = 16
VMEM = pl.BlockSpec(memory_space=pltpu.VMEM)
SMEM = pl.BlockSpec(memory_space=pltpu.SMEM)
ROOMY = pltpu.CompilerParams(vmem_limit_bytes=40 * 2**20)
SNUG = pltpu.CompilerParams(vmem_limit_bytes=12 * 2**20)


def dot(a, b, contract=((1,), (0,))):
    return lax.dot_general(a, b, (contract, ((), ())), preferred_element_type=F32)


NT = ((1,), (1,))
TN = ((0,), (0,))


def rank_picker(shape, slab_dim, group, group_count, width, sign):
    padded = lax.broadcasted_iota(jnp.int32, shape, slab_dim)
    rank = lax.broadcasted_iota(jnp.int32, shape, 1 - slab_dim)
    step = padded // SLAB
    lane = padded % SLAB
    slab = lax.rem(group + sign * step + group_count, group_count)
    hit = (rank == slab * width + lane) & (lane < width)
    return jnp.where(hit, 1.0, 0.0).astype(BF)


def project_kernel(feat_ref, in_ref, cot_ref, outf_ref, mask_ref, own_ref, *payload_refs):
    group_count = 1 + len(payload_refs)
    rank = in_ref.shape[1]
    width = rank // group_count
    pick = rank_picker((group_count * SLAB, rank), 0, lax.axis_index("chan"), group_count, width, 1)
    weights = dot(pick, in_ref[...], NT).astype(BF)
    reduced = dot(weights, feat_ref[...]) * mask_ref[...].astype(F32)
    grad_mixed = dot(outf_ref[...], cot_ref[...])
    own_ref[0:SLAB, :] = reduced[:SLAB]
    own_ref[SLAB:, :] = grad_mixed
    for j, payload_ref in enumerate(payload_refs):
        payload_ref[0:SLAB, :] = reduced[(j + 1) * SLAB : (j + 2) * SLAB].astype(BF)
        payload_ref[SLAB:, :] = grad_mixed.astype(BF)


def low_onehot(low):
    shape = (LOW, low.shape[1])
    want = jnp.broadcast_to(low.astype(F32), shape).astype(BF)
    have = lax.broadcasted_iota(jnp.int32, shape, 0).astype(F32).astype(BF)
    return jnp.where(have == want, jnp.ones((), BF), jnp.zeros((), BF))


def core_bit():
    return lax.axis_index("leaf") % 2


def first_octant(halo_ref, slot):
    return jnp.clip(halo_ref[slot, 0] & 15, 0, 8) * 64


def mirrored(core, view, near):
    return jnp.where(core == 0, view, near - 1 - view)


def scatter_kernel(halo_ref, p0, p1, p2, p3, core_ref, nbr_ref, gm_ref, own_ref, kept_ref,
                   cross_ref, terms_ref, acc_ref):
    rows = nbr_ref.shape[1]
    tiles = acc_ref.shape[0] // SLAB
    total = (p0[...] + p1[...].astype(F32)) + (p2[...].astype(F32) + p3[...].astype(F32))
    cross_ref[0:SLAB, :] = total[:SLAB].astype(BF)
    grad_mixed = total[SLAB:].astype(BF)
    gm_ref[...] = grad_mixed
    terms_ref[...] = dot(core_ref[...], grad_mixed).astype(BF)
    acc_ref[...] = jnp.zeros_like(acc_ref)

    def step(k, carry):
        index = nbr_ref[pl.ds(k, 1), :]
        onehot = low_onehot(index & (LOW - 1))
        high = jnp.broadcast_to((index >> 8).astype(F32), (SLAB, rows)).astype(BF)
        terms = terms_ref[pl.ds(pl.multiple_of(k * SLAB, SLAB), SLAB), :]
        spread = jnp.concatenate(
            [jnp.where(high == jnp.full((), t, BF), terms, jnp.zeros((), BF)) for t in range(tiles)], 0
        )
        acc_ref[...] += dot(spread, onehot, NT)
        return carry

    offsets = nbr_ref.shape[0]
    middle = offsets // 2
    lax.fori_loop(0, offsets - 1, lambda i, carry: step(i + (i >= middle), carry), 0, unroll=13)

    def tile(t):
        return acc_ref[pl.ds(pl.multiple_of(t * SLAB, SLAB), SLAB), :]

    own_tiles = rows // LOW
    itself = terms_ref[middle * SLAB : (middle + 1) * SLAB, :].astype(F32)
    own_ref[...] = jnp.concatenate([tile(t) for t in range(own_tiles)], 1) + itself
    near = halo_ref.shape[0]
    per_peer = (tiles - own_tiles) // near
    blank = jnp.zeros((SLAB, rows - per_peer * LOW), F32)
    for view in range(near):
        slot = mirrored(core_bit(), view, near)
        start = own_tiles + slot * per_peer
        window = jnp.concatenate([tile(start + i) for i in range(per_peer)] + [blank], 1)
        block = pltpu.roll(window, first_octant(halo_ref, slot), 1)
        if view < 5:
            cross_ref[(view + 1) * SLAB : (view + 2) * SLAB, :] = block.astype(BF)
        else:
            kept_ref[(view - 5) * SLAB : (view - 4) * SLAB, :] = block


def offset_index(nbr_ref, i):
    middle = nbr_ref.shape[0] // 2
    k = i + (i >= middle)
    index = nbr_ref[pl.ds(k, 1), :]
    return pl.ds(pl.multiple_of(k * SLAB, SLAB), SLAB), low_onehot(index & (LOW - 1)), index >> 8


def window_of(block, halo_ref, slot):
    return pltpu.roll(block.astype(F32), block.shape[1] - first_octant(halo_ref, slot), 1)


def near_gather_kernel(halo_ref, own_ref, pair_ref, nbr_ref, ga_ref, table_ref):
    offsets, rows = nbr_ref.shape
    own_tiles = rows // LOW
    per_peer = table_ref.shape[0] // SLAB - own_tiles
    for t in range(own_tiles):
        table_ref[t * SLAB : (t + 1) * SLAB, :] = own_ref[:, t * LOW : (t + 1) * LOW]
    slot = mirrored(core_bit(), 4, halo_ref.shape[0])
    window = window_of(pair_ref[...], halo_ref, slot).astype(BF)
    for i in range(per_peer):
        t = own_tiles + i
        table_ref[t * SLAB : (t + 1) * SLAB, :] = window[:, i * LOW : (i + 1) * LOW]
    highs = list(range(own_tiles)) + [own_tiles + slot * per_peer + i for i in range(per_peer)]

    def step(i, carry):
        place, onehot, high = offset_index(nbr_ref, i)
        high = jnp.broadcast_to(high, (SLAB, rows))
        picked = dot(table_ref[...], onehot)
        found = jnp.zeros((SLAB, rows), F32)
        for t, value in enumerate(highs):
            found = jnp.where(high == value, picked[t * SLAB : (t + 1) * SLAB], found)
        ga_ref[place, :] = found.astype(BF)
        return carry

    lax.fori_loop(0, offsets - 1, step, 0, unroll=13)
    middle = offsets // 2
    ga_ref[middle * SLAB : (middle + 1) * SLAB, :] = own_ref[...]


def far_gather_kernel(halo_ref, base_ref, near_ref, far_ref, cross_ref, core_ref, nbr_ref, mix_ref, ga_ref,
                      wide_ref, table_ref):
    offsets, rows = nbr_ref.shape
    own_tiles = rows // LOW
    near = halo_ref.shape[0]
    views = {
        0: far_ref[0:SLAB, :],
        1: far_ref[SLAB:, :],
        2: near_ref[0:SLAB, :],
        3: near_ref[SLAB:, :],
        5: cross_ref[SLAB : 2 * SLAB, :],
        6: cross_ref[0:SLAB, :],
        7: cross_ref[3 * SLAB : 4 * SLAB, :],
    }
    both = table_ref.shape[0] // len(views)
    width = both // 2
    highs = []
    for n, (view, block) in enumerate(views.items()):
        slot = mirrored(core_bit(), view, near)
        window = window_of(block, halo_ref, slot)
        wide_ref[n * both : n * both + width, :] = window[:width, :LOW]
        wide_ref[n * both + width : (n + 1) * both, :] = window[:width, LOW : 2 * LOW]
        highs.append(own_tiles + 2 * slot)
    table_ref[...] = wide_ref[...].astype(BF)
    second = (lax.broadcasted_iota(jnp.int32, (both, rows), 0) >= width).astype(jnp.int32)

    def step(i, carry):
        place, onehot, high = offset_index(nbr_ref, i)
        high = jnp.broadcast_to(high, (both, rows)) - second
        picked = dot(table_ref[...], onehot)
        found = jnp.zeros((both, rows), F32)
        for n, value in enumerate(highs):
            found = jnp.where(high == value, picked[n * both : (n + 1) * both], found)
        found = jnp.concatenate([found[:width] + found[width:], jnp.zeros((SLAB - width, rows), F32)], 0)
        ga_ref[place, :] = (base_ref[place, :].astype(F32) + found).astype(BF)
        return carry

    lax.fori_loop(0, offsets - 1, step, 0, unroll=13)
    used = core_ref.shape[0]
    middle = offsets // 2
    itself = slice(middle * SLAB, (middle + 1) * SLAB)
    ga_ref[itself, :] = base_ref[itself, :]
    ga_ref[used:, :] = jnp.zeros_like(ga_ref[used:, :])
    mix_ref[...] = dot(core_ref[...], ga_ref[:used, :], TN)


def core_gradient_kernel(gm_ref, ga_ref, gc_ref):
    gc_ref[...] = dot(gm_ref[...], ga_ref[...], NT)


def sums_kernel(mix_ref, e0, e2, e3, e1, feat_ref, cot_ref, gc_ref, keep_ref, give_ref, rows_ref, mixed_ref):
    rank, rows = mix_ref.shape
    wide = gc_ref.shape[1]
    group = lax.axis_index("chan")
    pick = rank_picker((rank, 4 * SLAB), 1, group, 4, rank // 4, -1)
    slabs = jnp.concatenate([e[0:SLAB, :] for e in (e0, e1, e2, e3)], 0)
    grad_rows = dot(pick, slabs).astype(BF)
    rows_ref[...] = grad_rows
    total = (mix_ref[...] + e1[SLAB:, :].astype(F32)) + (e2[SLAB:, :].astype(F32) + e3[SLAB:, :].astype(F32))
    mixed = total.astype(BF)
    mixed_ref[...] = mixed
    column = lax.broadcasted_iota(jnp.int32, (wide, rank), 0)
    wanted = lax.broadcasted_iota(jnp.int32, (wide, rank), 1)
    free = column % SLAB - (SLAB - 4)
    place = jnp.where((free >= 0) & (column // SLAB * 4 + free == wanted), 1.0, 0.0).astype(BF)
    left = dot(feat_ref[...], grad_rows, NT)
    high = left.astype(BF)
    rest = left - high.astype(F32)
    middle = rest.astype(BF)
    low = (rest - middle.astype(F32)).astype(BF)
    right = jnp.concatenate([jnp.zeros((48, rows), BF), cot_ref[...], jnp.zeros((32, rows), BF)], 0)
    tail = dot(mixed, right, NT)
    packed = gc_ref[...] + (dot(high, place, NT) + dot(middle, place, NT) + dot(low, place, NT))
    packed = jnp.concatenate([packed[:, : wide - 128], packed[:, wide - 128 :] + tail], 1)
    half = rank // 2
    first = core_bit() == 0
    keep_ref[...] = jnp.where(first, packed[:half], packed[half:])
    give_ref[...] = jnp.where(first, packed[half:], packed[:half])


def outputs_kernel(rows_ref, mixed_ref, in_ref, outf_ref, gf_ref, out_ref):
    gf_ref[...] = dot(in_ref[...], rows_ref[...]).astype(BF)
    out_ref[...] = dot(outf_ref[...], mixed_ref[...], TN).astype(BF)


def unpack_kernel(factor, mine_ref, other_ref, left_ref, core_ref, right_ref, flat_ref, turned_ref):
    width, offsets, rank = core_ref.shape
    mine, other = mine_ref[...] * factor, other_ref[...] * factor
    first = core_bit() == 0
    packed = jnp.concatenate([jnp.where(first, mine, other), jnp.where(first, other, mine)], 0)
    flat_ref[...] = packed.T
    for c in range(width):
        core_ref[c] = flat_ref[pl.ds(c, offsets, stride=SLAB), :]
    for j in range(4):
        turned_ref[pl.ds(j, rank // 4, stride=4), :] = flat_ref[pl.ds(width + j, rank // 4, stride=SLAB), :]
    left_ref[...] = turned_ref[...].T
    right_ref[...] = flat_ref[offsets * SLAB : offsets * SLAB + rank, :].T


def shifted(block, axis, distance):
    count = lax.axis_size(axis)
    return lax.ppermute(block, axis, [(i, (i + distance) % count) for i in range(count)])


def crossed(block, mask):
    return lax.ppermute(block, "leaf", [(i, i ^ mask) for i in range(lax.axis_size("leaf"))])


def outward(block, chips):
    count = lax.axis_size("leaf")
    return lax.ppermute(
        block, "leaf", [(i, (i + (2 * chips if i % 2 == 0 else -2 * chips)) % count) for i in range(count)]
    )


def from_z(block, even, odd):
    count = lax.axis_size("leaf")
    return lax.ppermute(
        block, "leaf", [((i + 8 * (odd if i // 8 % 2 else even)) % count, i) for i in range(count)]
    )


def leaf_sum(mine, give):
    mine = mine + crossed(give, 1)
    for masks in ((8,), (2, 6, 4)):
        mine = mine + sum(crossed(mine, mask) for mask in masks)
    mine = mine + sum(from_z(mine, even, odd) for even, odd in ((-1, 1), (2, -2), (-3, 3)))
    return mine, crossed(mine, 1)


def struct(shape, dtype):
    return jax.ShapeDtypeStruct(shape, dtype)


def body(features, in_factor, core, out_factor, neighbours, halo_blocks, row_mask, cotangent):
    channels, rows = features.shape
    offsets, width, rank = core.shape
    near, slots = halo_blocks.shape[1:]
    table_rows = (rows + near * slots * 64) // LOW * SLAB
    packed_width = (offsets * SLAB + 127) // 128 * 128
    keep = row_mask.reshape(1, rows)
    halo = halo_blocks[0]
    core_rows = jnp.pad(core, ((0, 0), (0, SLAB - width), (0, 0))).reshape(offsets * SLAB, rank)
    estimate = pl.CostEstimate(flops=5 * 10**9, bytes_accessed=2**20, transcendentals=0)

    own_payload, *payload = pl.pallas_call(
        project_kernel,
        out_shape=[struct((SLAB + rank, rows), F32)] + [struct((SLAB + rank, rows), BF)] * 3,
        in_specs=[VMEM] * 5,
        out_specs=[VMEM] * 4,
        name="project",
    )(features, in_factor, cotangent, out_factor, keep)
    arrived = {j: shifted(payload[j - 1], "chan", j) for j in (1, 3, 2)}

    triple = struct((3 * SLAB, rows), F32)
    grad_mixed, own, kept, cross = pl.pallas_call(
        scatter_kernel,
        out_shape=[struct((rank, rows), BF), struct((SLAB, rows), F32), triple, struct((6 * SLAB, rows), BF)],
        in_specs=[SMEM] + [VMEM] * 6,
        out_specs=[VMEM] * 4,
        scratch_shapes=[pltpu.VMEM((offsets * SLAB, rows), BF), pltpu.VMEM((table_rows, LOW), F32)],
        compiler_params=ROOMY,
        cost_estimate=estimate,
        name="scatter",
    )(halo, own_payload, arrived[1], arrived[3], arrived[2], core_rows, neighbours)

    def slabs_of(block, first, last):
        return block[first * SLAB : last * SLAB]

    reduced = slabs_of(cross, 0, 1)
    handed = crossed(cross, 1)
    pair = slabs_of(handed, 0, 1)
    far_other, far_same, near_other, near_same, mine = (
        slabs_of(handed, i, i + 1).astype(F32) for i in range(1, 6)
    )
    to_near = [slabs_of(kept, 0, 1) + near_same, slabs_of(kept, 1, 2) + near_other]
    to_far = [slabs_of(kept, 2, 3) + far_same, far_other]
    far = outward(jnp.concatenate([reduced, pair] + [x.astype(BF) for x in to_far], 0), 2)
    near = outward(jnp.concatenate([reduced, pair] + [x.astype(BF) for x in to_near], 0), 1)
    per_peer = slots * 64 // LOW
    near_tiles = rows // LOW + per_peer
    found = pl.pallas_call(
        near_gather_kernel,
        out_shape=struct((offsets * SLAB, rows), BF),
        in_specs=[SMEM] + [VMEM] * 3,
        out_specs=VMEM,
        scratch_shapes=[pltpu.VMEM((near_tiles * SLAB, LOW), BF)],
        compiler_params=ROOMY,
        cost_estimate=estimate,
        name="near_gather",
    )(halo, reduced, pair, neighbours)
    far, near, found = lax.optimization_barrier((far, near, found))
    near_pair, far_pair = slabs_of(near, 0, 2), slabs_of(far, 0, 2)
    passed = slabs_of(near, 3, 4).astype(F32) + slabs_of(far, 3, 4).astype(F32)
    beyond = crossed(jnp.concatenate([near_pair, far_pair, passed.astype(BF)], 0), 1)
    returned = (slabs_of(near, 2, 3).astype(F32) + slabs_of(far, 2, 3).astype(F32)) + slabs_of(beyond, 4, 5).astype(F32)
    grad_slab = (((own + mine) + returned) * keep.astype(F32)).astype(BF)

    mixed_part, gathered = pl.pallas_call(
        far_gather_kernel,
        out_shape=[struct((rank, rows), F32), struct((packed_width, rows), BF)],
        in_specs=[SMEM] + [VMEM] * 6,
        out_specs=[VMEM] * 2,
        scratch_shapes=[pltpu.VMEM((14 * width, LOW), F32), pltpu.VMEM((14 * width, LOW), BF)],
        compiler_params=ROOMY,
        cost_estimate=estimate,
        name="far_gather",
    )(halo, found, near_pair, far_pair, beyond, core_rows, neighbours)
    grad_core = pl.pallas_call(
        core_gradient_kernel,
        out_shape=struct((rank, packed_width), F32),
        in_specs=[VMEM] * 2,
        out_specs=VMEM,
        compiler_params=SNUG,
        cost_estimate=pl.CostEstimate(flops=5 * 10**8, bytes_accessed=2**20, transcendentals=0),
        name="core_gradient",
    )(grad_mixed, gathered)

    shared = jnp.concatenate([grad_slab, mixed_part.astype(BF)], 0)
    exchanged = [shared] + [shifted(shared, "chan", j) for j in (2, 3, 1)]

    sums, full = struct((rank // 2, packed_width), F32), struct((rank, rows), BF)
    mine, give, grad_rows, mixed = pl.pallas_call(
        sums_kernel,
        out_shape=[sums, sums, full, full],
        in_specs=[VMEM] * 8,
        out_specs=[VMEM] * 4,
        compiler_params=SNUG,
        name="sums",
    )(mixed_part, *exchanged, features, cotangent, grad_core)
    grad_features, output = pl.pallas_call(
        outputs_kernel,
        out_shape=[struct((channels, rows), BF)] * 2,
        in_specs=[VMEM] * 4,
        out_specs=[VMEM] * 2,
        compiler_params=SNUG,
        cost_estimate=pl.CostEstimate(flops=5 * 10**8, bytes_accessed=2**20, transcendentals=0),
        name="outputs",
    )(grad_rows, mixed, in_factor, out_factor)
    mine, other = leaf_sum(mine, give)

    factor = float(rows * lax.axis_size("leaf")) ** (-0.5)
    grad_in, grad_core, grad_out = pl.pallas_call(
        lambda *refs: unpack_kernel(factor, *refs),
        out_shape=[struct((channels, rank), F32), struct((width, offsets, rank), F32), struct((rank, channels), F32)],
        in_specs=[VMEM] * 2,
        out_specs=[VMEM] * 3,
        scratch_shapes=[pltpu.VMEM((packed_width, rank), F32), pltpu.VMEM((rank, channels), F32)],
        compiler_params=SNUG,
        name="unpack",
    )(mine, other)
    return (output, grad_features, grad_in, jnp.transpose(grad_core, (1, 0, 2)), grad_out)


def solution(mesh):
    placed = (
        P("chan", "leaf"),
        P("chan", None),
        P(None, "chan", None),
        P(None, "chan"),
        P(None, "leaf"),
        P("leaf", None, None),
        P("leaf"),
        P("chan", "leaf"),
    )
    return jax.shard_map(
        body,
        mesh=mesh,
        in_specs=placed,
        out_specs=(
            P("chan", "leaf"),
            P("chan", "leaf"),
            P("chan", None),
            P(None, "chan", None),
            P(None, "chan"),
        ),
        check_vma=False,
    )
```

```python
import jax
import jax.numpy as jnp
from jax import lax
from jax.experimental import pallas as pl
from jax.experimental.pallas import tpu as pltpu
from jax.sharding import PartitionSpec as P

BF = jnp.bfloat16
F32 = jnp.float32
LOW = 256
SLAB = 16
VMEM = pl.BlockSpec(memory_space=pltpu.VMEM)
SMEM = pl.BlockSpec(memory_space=pltpu.SMEM)
ROOMY = pltpu.CompilerParams(vmem_limit_bytes=40 * 2**20)
SNUG = pltpu.CompilerParams(vmem_limit_bytes=12 * 2**20)


def dot(a, b, contract=((1,), (0,))):
    return lax.dot_general(a, b, (contract, ((), ())), preferred_element_type=F32)


NT = ((1,), (1,))
TN = ((0,), (0,))


def rank_picker(shape, slab_dim, group, group_count, width, sign):
    padded = lax.broadcasted_iota(jnp.int32, shape, slab_dim)
    rank = lax.broadcasted_iota(jnp.int32, shape, 1 - slab_dim)
    step = padded // SLAB
    lane = padded % SLAB
    slab = lax.rem(group + sign * step + group_count, group_count)
    hit = (rank == slab * width + lane) & (lane < width)
    return jnp.where(hit, 1.0, 0.0).astype(BF)


def project_kernel(feat_ref, in_ref, cot_ref, outf_ref, mask_ref, own_ref, *payload_refs):
    group_count = 1 + len(payload_refs)
    rank = in_ref.shape[1]
    width = rank // group_count
    pick = rank_picker((group_count * SLAB, rank), 0, lax.axis_index("chan"), group_count, width, 1)
    weights = dot(pick, in_ref[...], NT).astype(BF)
    reduced = dot(weights, feat_ref[...]) * mask_ref[...].astype(F32)
    grad_mixed = dot(outf_ref[...], cot_ref[...])
    own_ref[0:SLAB, :] = reduced[:SLAB]
    own_ref[SLAB:, :] = grad_mixed
    for j, payload_ref in enumerate(payload_refs):
        payload_ref[0:SLAB, :] = reduced[(j + 1) * SLAB : (j + 2) * SLAB].astype(BF)
        payload_ref[SLAB:, :] = grad_mixed.astype(BF)


def low_onehot(low):
    shape = (LOW, low.shape[1])
    want = jnp.broadcast_to(low.astype(F32), shape).astype(BF)
    have = lax.broadcasted_iota(jnp.int32, shape, 0).astype(F32).astype(BF)
    return jnp.where(have == want, jnp.ones((), BF), jnp.zeros((), BF))


def core_bit():
    return lax.axis_index("leaf") % 2


def first_octant(halo_ref, slot):
    return jnp.clip(halo_ref[slot, 0] & 15, 0, 8) * 64


def mirrored(core, view, near):
    return jnp.where(core == 0, view, near - 1 - view)


def scatter_kernel(halo_ref, p0, p1, p2, p3, core_ref, nbr_ref, gm_ref, own_ref, kept_ref,
                   cross_ref, terms_ref, acc_ref):
    rows = nbr_ref.shape[1]
    tiles = acc_ref.shape[0] // SLAB
    total = (p0[...] + p1[...].astype(F32)) + (p2[...].astype(F32) + p3[...].astype(F32))
    cross_ref[0:SLAB, :] = total[:SLAB].astype(BF)
    grad_mixed = total[SLAB:].astype(BF)
    gm_ref[...] = grad_mixed
    terms_ref[...] = dot(core_ref[...], grad_mixed).astype(BF)
    acc_ref[...] = jnp.zeros_like(acc_ref)
    offsets, rows = nbr_ref.shape
    middle = offsets // 2
    copies = 4
    tall = core_ref.shape[0] // offsets
    width = tall // copies
    own_tiles = rows // LOW
    near = halo_ref.shape[0]
    per_peer = halo_ref.shape[1] * 64 // LOW
    groups = (own_tiles + near * per_peer) // copies
    spare = jnp.zeros((acc_ref.shape[0] - groups * tall, rows), BF)
    nth = (lax.broadcasted_iota(jnp.int32, (tall, rows), 0) // width).astype(F32)

    def step(i, carry):
        k = i + (i >= middle)
        index = nbr_ref[pl.ds(k, 1), :]
        onehot = low_onehot(index & (LOW - 1))
        high = (jnp.broadcast_to((index >> 8).astype(F32), (tall, rows)) - nth).astype(BF)
        terms = terms_ref[pl.ds(pl.multiple_of(k * tall, tall), tall), :]
        spread = [
            jnp.where(high == jnp.full((), g * copies, BF), terms, jnp.zeros((), BF)) for g in range(groups)
        ]
        acc_ref[...] += dot(jnp.concatenate(spread + [spare], 0), onehot, NT)
        return carry

    lax.fori_loop(0, offsets - 1, step, 0, unroll=13)

    def tile(t):
        return acc_ref[t * width : (t + 1) * width, :]

    pad = jnp.zeros((SLAB - width, rows), F32)
    itself = terms_ref[middle * tall : middle * tall + SLAB, :].astype(F32)
    own = jnp.concatenate([tile(t) for t in range(own_tiles)], 1) + itself[:width]
    own_ref[...] = jnp.concatenate([own, pad], 0)
    blank = jnp.zeros((width, rows - per_peer * LOW), F32)
    blocks = []
    for slot in range(near):
        start = own_tiles + slot * per_peer
        window = jnp.concatenate([tile(start + i) for i in range(per_peer)] + [blank], 1)
        window = jnp.concatenate([window, pad], 0)
        blocks.append(pltpu.roll(window, first_octant(halo_ref, slot), 1))
    first_core = core_bit() == 0
    for view in range(near):
        block = jnp.where(first_core, blocks[view], blocks[near - 1 - view])
        if view < 5:
            cross_ref[(view + 1) * SLAB : (view + 2) * SLAB, :] = block.astype(BF)
        else:
            kept_ref[(view - 5) * SLAB : (view - 4) * SLAB, :] = block


def offset_index(nbr_ref, i):
    middle = nbr_ref.shape[0] // 2
    k = i + (i >= middle)
    index = nbr_ref[pl.ds(k, 1), :]
    return pl.ds(pl.multiple_of(k * SLAB, SLAB), SLAB), low_onehot(index & (LOW - 1)), index >> 8


def window_of(block, halo_ref, slot):
    return pltpu.roll(block.astype(F32), block.shape[1] - first_octant(halo_ref, slot), 1)


def near_gather_kernel(halo_ref, own_ref, pair_ref, nbr_ref, ga_ref, table_ref):
    offsets, rows = nbr_ref.shape
    own_tiles = rows // LOW
    per_peer = table_ref.shape[0] // SLAB - own_tiles
    for t in range(own_tiles):
        table_ref[t * SLAB : (t + 1) * SLAB, :] = own_ref[:, t * LOW : (t + 1) * LOW]
    slot = mirrored(core_bit(), 4, halo_ref.shape[0])
    window = window_of(pair_ref[...], halo_ref, slot).astype(BF)
    for i in range(per_peer):
        t = own_tiles + i
        table_ref[t * SLAB : (t + 1) * SLAB, :] = window[:, i * LOW : (i + 1) * LOW]
    highs = list(range(own_tiles)) + [own_tiles + slot * per_peer + i for i in range(per_peer)]

    def step(i, carry):
        place, onehot, high = offset_index(nbr_ref, i)
        high = jnp.broadcast_to(high, (SLAB, rows))
        picked = dot(table_ref[...], onehot)
        found = jnp.zeros((SLAB, rows), F32)
        for t, value in enumerate(highs):
            found = jnp.where(high == value, picked[t * SLAB : (t + 1) * SLAB], found)
        ga_ref[place, :] = found.astype(BF)
        return carry

    lax.fori_loop(0, offsets - 1, step, 0, unroll=13)
    middle = offsets // 2
    ga_ref[middle * SLAB : (middle + 1) * SLAB, :] = own_ref[...]


def far_gather_kernel(halo_ref, base_ref, near_ref, far_ref, cross_ref, core_ref, nbr_ref, mix_ref, ga_ref,
                      wide_ref, table_ref):
    offsets, rows = nbr_ref.shape
    own_tiles = rows // LOW
    near = halo_ref.shape[0]
    views = {
        0: far_ref[0:SLAB, :],
        1: far_ref[SLAB:, :],
        2: near_ref[0:SLAB, :],
        3: near_ref[SLAB:, :],
        5: cross_ref[SLAB : 2 * SLAB, :],
        6: cross_ref[0:SLAB, :],
        7: cross_ref[3 * SLAB : 4 * SLAB, :],
    }
    both = table_ref.shape[0] // len(views)
    width = both // 2
    highs = []
    for n, (view, block) in enumerate(views.items()):
        slot = mirrored(core_bit(), view, near)
        window = window_of(block, halo_ref, slot)
        wide_ref[n * both : n * both + width, :] = window[:width, :LOW]
        wide_ref[n * both + width : (n + 1) * both, :] = window[:width, LOW : 2 * LOW]
        highs.append(own_tiles + 2 * slot)
    table_ref[...] = wide_ref[...].astype(BF)
    second = (lax.broadcasted_iota(jnp.int32, (both, rows), 0) >= width).astype(jnp.int32)

    def step(i, carry):
        place, onehot, high = offset_index(nbr_ref, i)
        high = jnp.broadcast_to(high, (both, rows)) - second
        picked = dot(table_ref[...], onehot)
        found = jnp.zeros((both, rows), F32)
        for n, value in enumerate(highs):
            found = jnp.where(high == value, picked[n * both : (n + 1) * both], found)
        found = jnp.concatenate([found[:width] + found[width:], jnp.zeros((SLAB - width, rows), F32)], 0)
        ga_ref[place, :] = (base_ref[place, :].astype(F32) + found).astype(BF)
        return carry

    lax.fori_loop(0, offsets - 1, step, 0, unroll=13)
    used = core_ref.shape[0]
    middle = offsets // 2
    itself = slice(middle * SLAB, (middle + 1) * SLAB)
    ga_ref[itself, :] = base_ref[itself, :]
    ga_ref[used:, :] = jnp.zeros_like(ga_ref[used:, :])
    mix_ref[...] = dot(core_ref[...], ga_ref[:used, :], TN)


def core_gradient_kernel(gm_ref, ga_ref, gc_ref):
    gc_ref[...] = dot(gm_ref[...], ga_ref[...], NT)


def sums_kernel(mix_ref, e0, e2, e3, e1, feat_ref, cot_ref, gc_ref, keep_ref, give_ref, rows_ref, mixed_ref):
    rank, rows = mix_ref.shape
    wide = gc_ref.shape[1]
    group = lax.axis_index("chan")
    pick = rank_picker((rank, 4 * SLAB), 1, group, 4, rank // 4, -1)
    slabs = jnp.concatenate([e[0:SLAB, :] for e in (e0, e1, e2, e3)], 0)
    grad_rows = dot(pick, slabs).astype(BF)
    rows_ref[...] = grad_rows
    total = (mix_ref[...] + e1[SLAB:, :].astype(F32)) + (e2[SLAB:, :].astype(F32) + e3[SLAB:, :].astype(F32))
    mixed = total.astype(BF)
    mixed_ref[...] = mixed
    column = lax.broadcasted_iota(jnp.int32, (wide, rank), 0)
    wanted = lax.broadcasted_iota(jnp.int32, (wide, rank), 1)
    free = column % SLAB - (SLAB - 4)
    place = jnp.where((free >= 0) & (column // SLAB * 4 + free == wanted), 1.0, 0.0).astype(BF)
    left = dot(feat_ref[...], grad_rows, NT)
    high = left.astype(BF)
    rest = left - high.astype(F32)
    middle = rest.astype(BF)
    low = (rest - middle.astype(F32)).astype(BF)
    right = jnp.concatenate([jnp.zeros((48, rows), BF), cot_ref[...], jnp.zeros((32, rows), BF)], 0)
    tail = dot(mixed, right, NT)
    packed = gc_ref[...] + (dot(high, place, NT) + dot(middle, place, NT) + dot(low, place, NT))
    packed = jnp.concatenate([packed[:, : wide - 128], packed[:, wide - 128 :] + tail], 1)
    half = rank // 2
    first = core_bit() == 0
    keep_ref[...] = jnp.where(first, packed[:half], packed[half:])
    give_ref[...] = jnp.where(first, packed[half:], packed[:half])


def outputs_kernel(rows_ref, mixed_ref, in_ref, outf_ref, gf_ref, out_ref):
    gf_ref[...] = dot(in_ref[...], rows_ref[...]).astype(BF)
    out_ref[...] = dot(outf_ref[...], mixed_ref[...], TN).astype(BF)


def unpack_kernel(factor, mine_ref, other_ref, left_ref, core_ref, right_ref, flat_ref, turned_ref):
    width, offsets, rank = core_ref.shape
    mine, other = mine_ref[...] * factor, other_ref[...] * factor
    first = core_bit() == 0
    packed = jnp.concatenate([jnp.where(first, mine, other), jnp.where(first, other, mine)], 0)
    flat_ref[...] = packed.T
    for c in range(width):
        core_ref[c] = flat_ref[pl.ds(c, offsets, stride=SLAB), :]
    for j in range(4):
        turned_ref[pl.ds(j, rank // 4, stride=4), :] = flat_ref[pl.ds(width + j, rank // 4, stride=SLAB), :]
    left_ref[...] = turned_ref[...].T
    right_ref[...] = flat_ref[offsets * SLAB : offsets * SLAB + rank, :].T


def shifted(block, axis, distance):
    count = lax.axis_size(axis)
    return lax.ppermute(block, axis, [(i, (i + distance) % count) for i in range(count)])


def crossed(block, mask):
    return lax.ppermute(block, "leaf", [(i, i ^ mask) for i in range(lax.axis_size("leaf"))])


def outward(block, chips):
    count = lax.axis_size("leaf")
    return lax.ppermute(
        block, "leaf", [(i, (i + (2 * chips if i % 2 == 0 else -2 * chips)) % count) for i in range(count)]
    )


def from_z(block, even, odd):
    count = lax.axis_size("leaf")
    return lax.ppermute(
        block, "leaf", [((i + 8 * (odd if i // 8 % 2 else even)) % count, i) for i in range(count)]
    )


def leaf_sum(mine, give):
    mine = mine + crossed(give, 1)
    for masks in ((8,), (2, 6, 4)):
        mine = mine + sum(crossed(mine, mask) for mask in masks)
    mine = mine + sum(from_z(mine, even, odd) for even, odd in ((-3, 3), (2, -2), (-1, 1)))
    return mine, crossed(mine, 1)


def struct(shape, dtype):
    return jax.ShapeDtypeStruct(shape, dtype)


def body(features, in_factor, core, out_factor, neighbours, halo_blocks, row_mask, cotangent):
    channels, rows = features.shape
    offsets, width, rank = core.shape
    near, slots = halo_blocks.shape[1:]
    table_rows = (rows + near * slots * 64) // LOW * SLAB
    packed_width = (offsets * SLAB + 127) // 128 * 128
    keep = row_mask.reshape(1, rows)
    halo = halo_blocks[0]
    core_rows = jnp.pad(core, ((0, 0), (0, SLAB - width), (0, 0))).reshape(offsets * SLAB, rank)
    core_copies = jnp.tile(core[:, None], (1, 4, 1, 1)).reshape(offsets * 4 * width, rank)
    estimate = pl.CostEstimate(flops=5 * 10**9, bytes_accessed=2**20, transcendentals=0)

    own_payload, *payload = pl.pallas_call(
        project_kernel,
        out_shape=[struct((SLAB + rank, rows), F32)] + [struct((SLAB + rank, rows), BF)] * 3,
        in_specs=[VMEM] * 5,
        out_specs=[VMEM] * 4,
        name="project",
    )(features, in_factor, cotangent, out_factor, keep)
    arrived = {j: shifted(payload[j - 1], "chan", j) for j in (1, 3, 2)}

    triple = struct((3 * SLAB, rows), F32)
    grad_mixed, own, kept, cross = pl.pallas_call(
        scatter_kernel,
        out_shape=[struct((rank, rows), BF), struct((SLAB, rows), F32), triple, struct((6 * SLAB, rows), BF)],
        in_specs=[SMEM] + [VMEM] * 6,
        out_specs=[VMEM] * 4,
        scratch_shapes=[pltpu.VMEM((offsets * 4 * width, rows), BF), pltpu.VMEM((256, LOW), F32)],
        compiler_params=ROOMY,
        cost_estimate=estimate,
        name="scatter",
    )(halo, own_payload, arrived[1], arrived[3], arrived[2], core_copies, neighbours)

    def slabs_of(block, first, last):
        return block[first * SLAB : last * SLAB]

    reduced = slabs_of(cross, 0, 1)
    handed = crossed(cross, 1)
    pair = slabs_of(handed, 0, 1)
    far_other, far_same, near_other, near_same, mine = (
        slabs_of(handed, i, i + 1).astype(F32) for i in range(1, 6)
    )
    to_near = [slabs_of(kept, 0, 1) + near_same, slabs_of(kept, 1, 2) + near_other]
    to_far = [slabs_of(kept, 2, 3) + far_same, far_other]
    far = outward(jnp.concatenate([reduced, pair] + [x.astype(BF) for x in to_far], 0), 2)
    near = outward(jnp.concatenate([reduced, pair] + [x.astype(BF) for x in to_near], 0), 1)
    per_peer = slots * 64 // LOW
    near_tiles = rows // LOW + per_peer
    found = pl.pallas_call(
        near_gather_kernel,
        out_shape=struct((offsets * SLAB, rows), BF),
        in_specs=[SMEM] + [VMEM] * 3,
        out_specs=VMEM,
        scratch_shapes=[pltpu.VMEM((near_tiles * SLAB, LOW), BF)],
        compiler_params=ROOMY,
        cost_estimate=estimate,
        name="near_gather",
    )(halo, reduced, pair, neighbours)
    far, near, found = lax.optimization_barrier((far, near, found))
    near_pair, far_pair = slabs_of(near, 0, 2), slabs_of(far, 0, 2)
    passed = slabs_of(near, 3, 4).astype(F32) + slabs_of(far, 3, 4).astype(F32)
    beyond = crossed(jnp.concatenate([near_pair, far_pair, passed.astype(BF)], 0), 1)
    returned = (slabs_of(near, 2, 3).astype(F32) + slabs_of(far, 2, 3).astype(F32)) + slabs_of(beyond, 4, 5).astype(F32)
    grad_slab = (((own + mine) + returned) * keep.astype(F32)).astype(BF)

    mixed_part, gathered = pl.pallas_call(
        far_gather_kernel,
        out_shape=[struct((rank, rows), F32), struct((packed_width, rows), BF)],
        in_specs=[SMEM] + [VMEM] * 6,
        out_specs=[VMEM] * 2,
        scratch_shapes=[pltpu.VMEM((14 * width, LOW), F32), pltpu.VMEM((14 * width, LOW), BF)],
        compiler_params=ROOMY,
        cost_estimate=estimate,
        name="far_gather",
    )(halo, found, near_pair, far_pair, beyond, core_rows, neighbours)
    grad_core = pl.pallas_call(
        core_gradient_kernel,
        out_shape=struct((rank, packed_width), F32),
        in_specs=[VMEM] * 2,
        out_specs=VMEM,
        compiler_params=SNUG,
        cost_estimate=pl.CostEstimate(flops=5 * 10**8, bytes_accessed=2**20, transcendentals=0),
        name="core_gradient",
    )(grad_mixed, gathered)

    shared = jnp.concatenate([grad_slab, mixed_part.astype(BF)], 0)
    exchanged = [shared] + [shifted(shared, "chan", j) for j in (2, 3, 1)]

    sums, full = struct((rank // 2, packed_width), F32), struct((rank, rows), BF)
    mine, give, grad_rows, mixed = pl.pallas_call(
        sums_kernel,
        out_shape=[sums, sums, full, full],
        in_specs=[VMEM] * 8,
        out_specs=[VMEM] * 4,
        compiler_params=SNUG,
        name="sums",
    )(mixed_part, *exchanged, features, cotangent, grad_core)
    grad_features, output = pl.pallas_call(
        outputs_kernel,
        out_shape=[struct((channels, rows), BF)] * 2,
        in_specs=[VMEM] * 4,
        out_specs=[VMEM] * 2,
        compiler_params=SNUG,
        cost_estimate=pl.CostEstimate(flops=5 * 10**8, bytes_accessed=2**20, transcendentals=0),
        name="outputs",
    )(grad_rows, mixed, in_factor, out_factor)
    mine, other = leaf_sum(mine, give)

    factor = float(rows * lax.axis_size("leaf")) ** (-0.5)
    grad_in, grad_core, grad_out = pl.pallas_call(
        lambda *refs: unpack_kernel(factor, *refs),
        out_shape=[struct((channels, rank), F32), struct((width, offsets, rank), F32), struct((rank, channels), F32)],
        in_specs=[VMEM] * 2,
        out_specs=[VMEM] * 3,
        scratch_shapes=[pltpu.VMEM((packed_width, rank), F32), pltpu.VMEM((rank, channels), F32)],
        compiler_params=SNUG,
        name="unpack",
    )(mine, other)
    return (output, grad_features, grad_in, jnp.transpose(grad_core, (1, 0, 2)), grad_out)


def solution(mesh):
    placed = (
        P("chan", "leaf"),
        P("chan", None),
        P(None, "chan", None),
        P(None, "chan"),
        P(None, "leaf"),
        P("leaf", None, None),
        P("leaf"),
        P("chan", "leaf"),
    )
    return jax.shard_map(
        body,
        mesh=mesh,
        in_specs=placed,
        out_specs=(
            P("chan", "leaf"),
            P("chan", "leaf"),
            P("chan", None),
            P(None, "chan", None),
            P(None, "chan"),
        ),
        check_vma=False,
    )
```

```python
import jax
import jax.numpy as jnp
from jax import lax
from jax.experimental import pallas as pl
from jax.experimental.pallas import tpu as pltpu
from jax.sharding import PartitionSpec as P

BF = jnp.bfloat16
F32 = jnp.float32
LOW = 256
SLAB = 16
VMEM = pl.BlockSpec(memory_space=pltpu.VMEM)
SMEM = pl.BlockSpec(memory_space=pltpu.SMEM)
ROOMY = pltpu.CompilerParams(vmem_limit_bytes=40 * 2**20)
SNUG = pltpu.CompilerParams(vmem_limit_bytes=12 * 2**20)


def dot(a, b, contract=((1,), (0,))):
    return lax.dot_general(a, b, (contract, ((), ())), preferred_element_type=F32)


NT = ((1,), (1,))
TN = ((0,), (0,))


def rank_picker(shape, slab_dim, group, group_count, width, sign):
    padded = lax.broadcasted_iota(jnp.int32, shape, slab_dim)
    rank = lax.broadcasted_iota(jnp.int32, shape, 1 - slab_dim)
    step = padded // SLAB
    lane = padded % SLAB
    slab = lax.rem(group + sign * step + group_count, group_count)
    hit = (rank == slab * width + lane) & (lane < width)
    return jnp.where(hit, 1.0, 0.0).astype(BF)


def project_kernel(feat_ref, in_ref, cot_ref, outf_ref, mask_ref, own_ref, *payload_refs):
    group_count = 1 + len(payload_refs)
    rank = in_ref.shape[1]
    width = rank // group_count
    pick = rank_picker((group_count * SLAB, rank), 0, lax.axis_index("chan"), group_count, width, 1)
    weights = dot(pick, in_ref[...], NT).astype(BF)
    reduced = dot(weights, feat_ref[...]) * mask_ref[...].astype(F32)
    grad_mixed = dot(outf_ref[...], cot_ref[...])
    own_ref[0:SLAB, :] = reduced[:SLAB]
    own_ref[SLAB:, :] = grad_mixed
    for j, payload_ref in enumerate(payload_refs):
        payload_ref[0:SLAB, :] = reduced[(j + 1) * SLAB : (j + 2) * SLAB].astype(BF)
        payload_ref[SLAB:, :] = grad_mixed.astype(BF)


def low_onehot(low):
    shape = (LOW, low.shape[1])
    want = jnp.broadcast_to(low.astype(F32), shape).astype(BF)
    have = lax.broadcasted_iota(jnp.int32, shape, 0).astype(F32).astype(BF)
    return jnp.where(have == want, jnp.ones((), BF), jnp.zeros((), BF))


def core_bit():
    return lax.axis_index("leaf") % 2


def first_octant(halo_ref, slot):
    return jnp.clip(halo_ref[slot, 0] & 15, 0, 8) * 64


def mirrored(core, view, near):
    return jnp.where(core == 0, view, near - 1 - view)


def scatter_kernel(halo_ref, p0, p1, p2, p3, core_ref, nbr_ref, gm_ref, own_ref, kept_ref,
                   cross_ref, terms_ref, acc_ref):
    rows = nbr_ref.shape[1]
    tiles = acc_ref.shape[0] // SLAB
    total = (p0[...] + p1[...].astype(F32)) + (p2[...].astype(F32) + p3[...].astype(F32))
    cross_ref[0:SLAB, :] = total[:SLAB].astype(BF)
    grad_mixed = total[SLAB:].astype(BF)
    gm_ref[...] = grad_mixed
    terms_ref[...] = dot(core_ref[...], grad_mixed).astype(BF)
    acc_ref[...] = jnp.zeros_like(acc_ref)
    offsets, rows = nbr_ref.shape
    middle = offsets // 2
    copies = 4
    tall = core_ref.shape[0] // offsets
    width = tall // copies
    own_tiles = rows // LOW
    near = halo_ref.shape[0]
    per_peer = halo_ref.shape[1] * 64 // LOW
    groups = (own_tiles + near * per_peer) // copies
    spare = jnp.zeros((acc_ref.shape[0] - groups * tall, rows), BF)
    nth = (lax.broadcasted_iota(jnp.int32, (tall, rows), 0) // width).astype(F32)

    def step(i, carry):
        k = i + (i >= middle)
        index = nbr_ref[pl.ds(k, 1), :]
        onehot = low_onehot(index & (LOW - 1))
        high = (jnp.broadcast_to((index >> 8).astype(F32), (tall, rows)) - nth).astype(BF)
        terms = terms_ref[pl.ds(pl.multiple_of(k * tall, tall), tall), :]
        spread = [
            jnp.where(high == jnp.full((), g * copies, BF), terms, jnp.zeros((), BF)) for g in range(groups)
        ]
        acc_ref[...] += dot(jnp.concatenate(spread + [spare], 0), onehot, NT)
        return carry

    lax.fori_loop(0, offsets - 1, step, 0, unroll=13)

    def tile(t):
        return acc_ref[t * width : (t + 1) * width, :]

    pad = jnp.zeros((SLAB - width, rows), F32)
    itself = terms_ref[middle * tall : middle * tall + SLAB, :].astype(F32)
    own = jnp.concatenate([tile(t) for t in range(own_tiles)], 1) + itself[:width]
    own_ref[...] = jnp.concatenate([own, pad], 0)
    blank = jnp.zeros((width, rows - per_peer * LOW), F32)
    blocks = []
    for slot in range(near):
        start = own_tiles + slot * per_peer
        window = jnp.concatenate([tile(start + i) for i in range(per_peer)] + [blank], 1)
        window = jnp.concatenate([window, pad], 0)
        blocks.append(pltpu.roll(window, first_octant(halo_ref, slot), 1))
    first_core = core_bit() == 0
    for view in range(near):
        block = jnp.where(first_core, blocks[view], blocks[near - 1 - view])
        if view < 5:
            cross_ref[(view + 1) * SLAB : (view + 2) * SLAB, :] = block.astype(BF)
        else:
            kept_ref[(view - 5) * SLAB : (view - 4) * SLAB, :] = block


def offset_index(nbr_ref, i):
    middle = nbr_ref.shape[0] // 2
    k = i + (i >= middle)
    index = nbr_ref[pl.ds(k, 1), :]
    return pl.ds(pl.multiple_of(k * SLAB, SLAB), SLAB), low_onehot(index & (LOW - 1)), index >> 8


def window_of(block, halo_ref, slot):
    return pltpu.roll(block.astype(F32), block.shape[1] - first_octant(halo_ref, slot), 1)


def near_gather_kernel(halo_ref, own_ref, pair_ref, nbr_ref, ga_ref, table_ref):
    offsets, rows = nbr_ref.shape
    own_tiles = rows // LOW
    per_peer = table_ref.shape[0] // SLAB - own_tiles
    for t in range(own_tiles):
        table_ref[t * SLAB : (t + 1) * SLAB, :] = own_ref[:, t * LOW : (t + 1) * LOW]
    slot = mirrored(core_bit(), 4, halo_ref.shape[0])
    window = window_of(pair_ref[...], halo_ref, slot).astype(BF)
    for i in range(per_peer):
        t = own_tiles + i
        table_ref[t * SLAB : (t + 1) * SLAB, :] = window[:, i * LOW : (i + 1) * LOW]
    highs = list(range(own_tiles)) + [own_tiles + slot * per_peer + i for i in range(per_peer)]

    def step(i, carry):
        place, onehot, high = offset_index(nbr_ref, i)
        high = jnp.broadcast_to(high, (SLAB, rows))
        picked = dot(table_ref[...], onehot)
        found = jnp.zeros((SLAB, rows), F32)
        for t, value in enumerate(highs):
            found = jnp.where(high == value, picked[t * SLAB : (t + 1) * SLAB], found)
        ga_ref[place, :] = found.astype(BF)
        return carry

    lax.fori_loop(0, offsets - 1, step, 0, unroll=13)
    middle = offsets // 2
    ga_ref[middle * SLAB : (middle + 1) * SLAB, :] = own_ref[...]


def far_gather_kernel(halo_ref, base_ref, near_ref, far_ref, cross_ref, core_ref, nbr_ref, mix_ref, ga_ref,
                      wide_ref, table_ref):
    offsets, rows = nbr_ref.shape
    own_tiles = rows // LOW
    near = halo_ref.shape[0]
    views = {
        0: far_ref[0:SLAB, :],
        1: far_ref[SLAB:, :],
        2: near_ref[0:SLAB, :],
        3: near_ref[SLAB:, :],
        5: cross_ref[SLAB : 2 * SLAB, :],
        6: cross_ref[0:SLAB, :],
        7: cross_ref[3 * SLAB : 4 * SLAB, :],
    }
    both = table_ref.shape[0] // len(views)
    width = both // 2
    highs = []
    for n, (view, block) in enumerate(views.items()):
        slot = mirrored(core_bit(), view, near)
        window = window_of(block, halo_ref, slot)
        wide_ref[n * both : n * both + width, :] = window[:width, :LOW]
        wide_ref[n * both + width : (n + 1) * both, :] = window[:width, LOW : 2 * LOW]
        highs.append(own_tiles + 2 * slot)
    table_ref[...] = wide_ref[...].astype(BF)
    second = (lax.broadcasted_iota(jnp.int32, (both, rows), 0) >= width).astype(jnp.int32)

    def step(i, carry):
        place, onehot, high = offset_index(nbr_ref, i)
        high = jnp.broadcast_to(high, (both, rows)) - second
        picked = dot(table_ref[...], onehot)
        found = jnp.zeros((both, rows), F32)
        for n, value in enumerate(highs):
            found = jnp.where(high == value, picked[n * both : (n + 1) * both], found)
        found = jnp.concatenate([found[:width] + found[width:], jnp.zeros((SLAB - width, rows), F32)], 0)
        ga_ref[place, :] = (base_ref[place, :].astype(F32) + found).astype(BF)
        return carry

    lax.fori_loop(0, offsets - 1, step, 0, unroll=13)
    used = core_ref.shape[0]
    middle = offsets // 2
    itself = slice(middle * SLAB, (middle + 1) * SLAB)
    ga_ref[itself, :] = base_ref[itself, :]
    ga_ref[used:, :] = jnp.zeros_like(ga_ref[used:, :])
    mix_ref[...] = dot(core_ref[...], ga_ref[:used, :], TN)


def core_gradient_kernel(gm_ref, ga_ref, gc_ref):
    gc_ref[...] = dot(gm_ref[...], ga_ref[...], NT)


def sums_kernel(mix_ref, e0, e2, e3, e1, feat_ref, cot_ref, gc_ref, keep_ref, give_ref, rows_ref, mixed_ref):
    rank, rows = mix_ref.shape
    wide = gc_ref.shape[1]
    group = lax.axis_index("chan")
    pick = rank_picker((rank, 4 * SLAB), 1, group, 4, rank // 4, -1)
    slabs = jnp.concatenate([e[0:SLAB, :] for e in (e0, e1, e2, e3)], 0)
    grad_rows = dot(pick, slabs).astype(BF)
    rows_ref[...] = grad_rows
    total = (mix_ref[...] + e1[SLAB:, :].astype(F32)) + (e2[SLAB:, :].astype(F32) + e3[SLAB:, :].astype(F32))
    mixed = total.astype(BF)
    mixed_ref[...] = mixed
    column = lax.broadcasted_iota(jnp.int32, (wide, rank), 0)
    wanted = lax.broadcasted_iota(jnp.int32, (wide, rank), 1)
    free = column % SLAB - (SLAB - 4)
    place = jnp.where((free >= 0) & (column // SLAB * 4 + free == wanted), 1.0, 0.0).astype(BF)
    left = dot(feat_ref[...], grad_rows, NT)
    high = left.astype(BF)
    rest = left - high.astype(F32)
    middle = rest.astype(BF)
    low = (rest - middle.astype(F32)).astype(BF)
    right = jnp.concatenate([jnp.zeros((48, rows), BF), cot_ref[...], jnp.zeros((32, rows), BF)], 0)
    tail = dot(mixed, right, NT)
    packed = gc_ref[...] + (dot(high, place, NT) + dot(middle, place, NT) + dot(low, place, NT))
    packed = jnp.concatenate([packed[:, : wide - 128], packed[:, wide - 128 :] + tail], 1)
    half = rank // 2
    first = core_bit() == 0
    keep_ref[...] = jnp.where(first, packed[:half], packed[half:])
    give_ref[...] = jnp.where(first, packed[half:], packed[:half])


def outputs_kernel(rows_ref, mixed_ref, in_ref, outf_ref, gf_ref, out_ref):
    gf_ref[...] = dot(in_ref[...], rows_ref[...]).astype(BF)
    out_ref[...] = dot(outf_ref[...], mixed_ref[...], TN).astype(BF)


def unpack_kernel(factor, mine_ref, other_ref, left_ref, core_ref, right_ref, flat_ref, turned_ref):
    width, offsets, rank = core_ref.shape
    mine, other = mine_ref[...] * factor, other_ref[...] * factor
    first = core_bit() == 0
    packed = jnp.concatenate([jnp.where(first, mine, other), jnp.where(first, other, mine)], 0)
    flat_ref[...] = packed.T
    for c in range(width):
        core_ref[c] = flat_ref[pl.ds(c, offsets, stride=SLAB), :]
    for j in range(4):
        turned_ref[pl.ds(j, rank // 4, stride=4), :] = flat_ref[pl.ds(width + j, rank // 4, stride=SLAB), :]
    left_ref[...] = turned_ref[...].T
    right_ref[...] = flat_ref[offsets * SLAB : offsets * SLAB + rank, :].T


def shifted(block, axis, distance):
    count = lax.axis_size(axis)
    return lax.ppermute(block, axis, [(i, (i + distance) % count) for i in range(count)])


def crossed(block, mask):
    return lax.ppermute(block, "leaf", [(i, i ^ mask) for i in range(lax.axis_size("leaf"))])


def outward(block, chips):
    count = lax.axis_size("leaf")
    return lax.ppermute(
        block, "leaf", [(i, (i + (2 * chips if i % 2 == 0 else -2 * chips)) % count) for i in range(count)]
    )


def from_z(block, even, odd):
    count = lax.axis_size("leaf")
    return lax.ppermute(
        block, "leaf", [((i + 8 * (odd if i // 8 % 2 else even)) % count, i) for i in range(count)]
    )


def leaf_sum(mine, give):
    mine = mine + crossed(give, 1)
    for masks in ((8,), (2, 6, 4)):
        mine = mine + sum(crossed(mine, mask) for mask in masks)
    mine = mine + sum(from_z(mine, even, odd) for even, odd in ((-1, 1), (2, -2), (-3, 3)))
    return mine, crossed(mine, 1)


def struct(shape, dtype):
    return jax.ShapeDtypeStruct(shape, dtype)


def body(features, in_factor, core, out_factor, neighbours, halo_blocks, row_mask, cotangent):
    channels, rows = features.shape
    offsets, width, rank = core.shape
    near, slots = halo_blocks.shape[1:]
    table_rows = (rows + near * slots * 64) // LOW * SLAB
    packed_width = (offsets * SLAB + 127) // 128 * 128
    keep = row_mask.reshape(1, rows)
    halo = halo_blocks[0]
    core_rows = jnp.pad(core, ((0, 0), (0, SLAB - width), (0, 0))).reshape(offsets * SLAB, rank)
    core_copies = jnp.tile(core[:, None], (1, 4, 1, 1)).reshape(offsets * 4 * width, rank)
    estimate = pl.CostEstimate(flops=5 * 10**9, bytes_accessed=2**20, transcendentals=0)

    own_payload, *payload = pl.pallas_call(
        project_kernel,
        out_shape=[struct((SLAB + rank, rows), F32)] + [struct((SLAB + rank, rows), BF)] * 3,
        in_specs=[VMEM] * 5,
        out_specs=[VMEM] * 4,
        name="project",
    )(features, in_factor, cotangent, out_factor, keep)
    arrived = {j: shifted(payload[j - 1], "chan", j) for j in (1, 3, 2)}

    triple = struct((3 * SLAB, rows), F32)
    grad_mixed, own, kept, cross = pl.pallas_call(
        scatter_kernel,
        out_shape=[struct((rank, rows), BF), struct((SLAB, rows), F32), triple, struct((6 * SLAB, rows), BF)],
        in_specs=[SMEM] + [VMEM] * 6,
        out_specs=[VMEM] * 4,
        scratch_shapes=[pltpu.VMEM((offsets * 4 * width, rows), BF), pltpu.VMEM((256, LOW), F32)],
        compiler_params=ROOMY,
        cost_estimate=estimate,
        name="scatter",
    )(halo, own_payload, arrived[1], arrived[3], arrived[2], core_copies, neighbours)

    def slabs_of(block, first, last):
        return block[first * SLAB : last * SLAB]

    reduced = slabs_of(cross, 0, 1)
    handed = crossed(cross, 1)
    pair = slabs_of(handed, 0, 1)
    far_other, far_same, near_other, near_same, mine = (
        slabs_of(handed, i, i + 1).astype(F32) for i in range(1, 6)
    )
    to_near = [slabs_of(kept, 0, 1) + near_same, slabs_of(kept, 1, 2) + near_other]
    to_far = [slabs_of(kept, 2, 3) + far_same, far_other]
    far = outward(jnp.concatenate([reduced, pair] + [x.astype(BF) for x in to_far], 0), 2)
    near = outward(jnp.concatenate([reduced, pair] + [x.astype(BF) for x in to_near], 0), 1)
    per_peer = slots * 64 // LOW
    near_tiles = rows // LOW + per_peer
    found = pl.pallas_call(
        near_gather_kernel,
        out_shape=struct((offsets * SLAB, rows), BF),
        in_specs=[SMEM] + [VMEM] * 3,
        out_specs=VMEM,
        scratch_shapes=[pltpu.VMEM((near_tiles * SLAB, LOW), BF)],
        compiler_params=ROOMY,
        cost_estimate=estimate,
        name="near_gather",
    )(halo, reduced, pair, neighbours)
    far, near, found = lax.optimization_barrier((far, near, found))
    near_pair, far_pair = slabs_of(near, 0, 2), slabs_of(far, 0, 2)
    passed = slabs_of(near, 3, 4).astype(F32) + slabs_of(far, 3, 4).astype(F32)
    beyond = crossed(jnp.concatenate([near_pair, far_pair, passed.astype(BF)], 0), 1)
    returned = (slabs_of(near, 2, 3).astype(F32) + slabs_of(far, 2, 3).astype(F32)) + slabs_of(beyond, 4, 5).astype(F32)
    grad_slab = (((own + mine) + returned) * keep.astype(F32)).astype(BF)

    mixed_part, gathered = pl.pallas_call(
        far_gather_kernel,
        out_shape=[struct((rank, rows), F32), struct((packed_width, rows), BF)],
        in_specs=[SMEM] + [VMEM] * 6,
        out_specs=[VMEM] * 2,
        scratch_shapes=[pltpu.VMEM((14 * width, LOW), F32), pltpu.VMEM((14 * width, LOW), BF)],
        compiler_params=ROOMY,
        cost_estimate=estimate,
        name="far_gather",
    )(halo, found, near_pair, far_pair, beyond, core_rows, neighbours)
    grad_core = pl.pallas_call(
        core_gradient_kernel,
        out_shape=struct((rank, packed_width), F32),
        in_specs=[VMEM] * 2,
        out_specs=VMEM,
        compiler_params=SNUG,
        cost_estimate=pl.CostEstimate(flops=5 * 10**8, bytes_accessed=2**20, transcendentals=0),
        name="core_gradient",
    )(grad_mixed, gathered)

    shared = jnp.concatenate([grad_slab, mixed_part.astype(BF)], 0)
    exchanged = [shared] + [shifted(shared, "chan", j) for j in (2, 3, 1)]

    sums, full = struct((rank // 2, packed_width), F32), struct((rank, rows), BF)
    mine, give, grad_rows, mixed = pl.pallas_call(
        sums_kernel,
        out_shape=[sums, sums, full, full],
        in_specs=[VMEM] * 8,
        out_specs=[VMEM] * 4,
        compiler_params=SNUG,
        name="sums",
    )(mixed_part, *exchanged, features, cotangent, grad_core)
    grad_features, output = pl.pallas_call(
        outputs_kernel,
        out_shape=[struct((channels, rows), BF)] * 2,
        in_specs=[VMEM] * 4,
        out_specs=[VMEM] * 2,
        compiler_params=SNUG,
        cost_estimate=pl.CostEstimate(flops=5 * 10**8, bytes_accessed=2**20, transcendentals=0),
        name="outputs",
    )(grad_rows, mixed, in_factor, out_factor)
    mine, other = leaf_sum(mine, give)

    factor = float(rows * lax.axis_size("leaf")) ** (-0.5)
    grad_in, grad_core, grad_out = pl.pallas_call(
        lambda *refs: unpack_kernel(factor, *refs),
        out_shape=[struct((channels, rank), F32), struct((width, offsets, rank), F32), struct((rank, channels), F32)],
        in_specs=[VMEM] * 2,
        out_specs=[VMEM] * 3,
        scratch_shapes=[pltpu.VMEM((packed_width, rank), F32), pltpu.VMEM((rank, channels), F32)],
        compiler_params=SNUG,
        name="unpack",
    )(mine, other)
    return (output, grad_features, grad_in, jnp.transpose(grad_core, (1, 0, 2)), grad_out)


def solution(mesh):
    placed = (
        P("chan", "leaf"),
        P("chan", None),
        P(None, "chan", None),
        P(None, "chan"),
        P(None, "leaf"),
        P("leaf", None, None),
        P("leaf"),
        P("chan", "leaf"),
    )
    return jax.shard_map(
        body,
        mesh=mesh,
        in_specs=placed,
        out_specs=(
            P("chan", "leaf"),
            P("chan", "leaf"),
            P("chan", None),
            P(None, "chan", None),
            P(None, "chan"),
        ),
        check_vma=False,
    )
```

```python
import jax
import jax.numpy as jnp
from jax import lax
from jax.experimental import pallas as pl
from jax.experimental.pallas import tpu as pltpu
from jax.sharding import PartitionSpec as P

BF = jnp.bfloat16
F32 = jnp.float32
LOW = 256
SLAB = 16
VMEM = pl.BlockSpec(memory_space=pltpu.VMEM)
SMEM = pl.BlockSpec(memory_space=pltpu.SMEM)
ROOMY = pltpu.CompilerParams(vmem_limit_bytes=40 * 2**20)
SNUG = pltpu.CompilerParams(vmem_limit_bytes=12 * 2**20)


def dot(a, b, contract=((1,), (0,))):
    return lax.dot_general(a, b, (contract, ((), ())), preferred_element_type=F32)


NT = ((1,), (1,))
TN = ((0,), (0,))


def rank_picker(shape, slab_dim, group, group_count, width, sign):
    padded = lax.broadcasted_iota(jnp.int32, shape, slab_dim)
    rank = lax.broadcasted_iota(jnp.int32, shape, 1 - slab_dim)
    step = padded // SLAB
    lane = padded % SLAB
    slab = lax.rem(group + sign * step + group_count, group_count)
    hit = (rank == slab * width + lane) & (lane < width)
    return jnp.where(hit, 1.0, 0.0).astype(BF)


def project_kernel(feat_ref, in_ref, cot_ref, outf_ref, mask_ref, own_ref, *payload_refs):
    group_count = 1 + len(payload_refs)
    rank = in_ref.shape[1]
    width = rank // group_count
    pick = rank_picker((group_count * SLAB, rank), 0, lax.axis_index("chan"), group_count, width, 1)
    weights = dot(pick, in_ref[...], NT).astype(BF)
    reduced = dot(weights, feat_ref[...]) * mask_ref[...].astype(F32)
    grad_mixed = dot(outf_ref[...], cot_ref[...])
    own_ref[0:SLAB, :] = reduced[:SLAB]
    own_ref[SLAB:, :] = grad_mixed
    for j, payload_ref in enumerate(payload_refs):
        payload_ref[0:SLAB, :] = reduced[(j + 1) * SLAB : (j + 2) * SLAB].astype(BF)
        payload_ref[SLAB:, :] = grad_mixed.astype(BF)


def low_onehot(low):
    shape = (LOW, low.shape[1])
    want = jnp.broadcast_to(low.astype(F32), shape).astype(BF)
    have = lax.broadcasted_iota(jnp.int32, shape, 0).astype(F32).astype(BF)
    return jnp.where(have == want, jnp.ones((), BF), jnp.zeros((), BF))


def core_bit():
    return lax.axis_index("leaf") % 2


def first_octant(halo_ref, slot):
    return jnp.clip(halo_ref[slot, 0] & 15, 0, 8) * 64


def mirrored(core, view, near):
    return jnp.where(core == 0, view, near - 1 - view)


def scatter_kernel(halo_ref, p0, p1, p2, p3, core_ref, nbr_ref, gm_ref, own_ref, kept_ref,
                   cross_ref, terms_ref, acc_ref):
    rows = nbr_ref.shape[1]
    tiles = acc_ref.shape[0] // SLAB
    total = (p0[...] + p1[...].astype(F32)) + (p2[...].astype(F32) + p3[...].astype(F32))
    cross_ref[0:SLAB, :] = total[:SLAB].astype(BF)
    grad_mixed = total[SLAB:].astype(BF)
    gm_ref[...] = grad_mixed
    terms_ref[...] = dot(core_ref[...], grad_mixed).astype(BF)
    acc_ref[...] = jnp.zeros_like(acc_ref)
    offsets, rows = nbr_ref.shape
    middle = offsets // 2
    copies = 4
    tall = core_ref.shape[0] // offsets
    width = tall // copies
    own_tiles = rows // LOW
    near = halo_ref.shape[0]
    per_peer = halo_ref.shape[1] * 64 // LOW
    groups = (own_tiles + near * per_peer) // copies
    spare = jnp.zeros((acc_ref.shape[0] - groups * tall, rows), BF)
    nth = (lax.broadcasted_iota(jnp.int32, (tall, rows), 0) // width).astype(F32)

    def step(i, carry):
        k = i + (i >= middle)
        index = nbr_ref[pl.ds(k, 1), :]
        onehot = low_onehot(index & (LOW - 1))
        high = (jnp.broadcast_to((index >> 8).astype(F32), (tall, rows)) - nth).astype(BF)
        terms = terms_ref[pl.ds(pl.multiple_of(k * tall, tall), tall), :]
        spread = [
            jnp.where(high == jnp.full((), g * copies, BF), terms, jnp.zeros((), BF)) for g in range(groups)
        ]
        acc_ref[...] += dot(jnp.concatenate(spread + [spare], 0), onehot, NT)
        return carry

    lax.fori_loop(0, offsets - 1, step, 0, unroll=13)

    def tile(t):
        return acc_ref[t * width : (t + 1) * width, :]

    pad = jnp.zeros((SLAB - width, rows), F32)
    itself = terms_ref[middle * tall : middle * tall + SLAB, :].astype(F32)
    own = jnp.concatenate([tile(t) for t in range(own_tiles)], 1) + itself[:width]
    own_ref[...] = jnp.concatenate([own, pad], 0)
    blank = jnp.zeros((width, rows - per_peer * LOW), F32)
    blocks = []
    for slot in range(near):
        start = own_tiles + slot * per_peer
        window = jnp.concatenate([tile(start + i) for i in range(per_peer)] + [blank], 1)
        window = jnp.concatenate([window, pad], 0)
        blocks.append(pltpu.roll(window, first_octant(halo_ref, slot), 1))
    first_core = core_bit() == 0
    for view in range(near):
        block = jnp.where(first_core, blocks[view], blocks[near - 1 - view])
        if view < 5:
            cross_ref[(view + 1) * SLAB : (view + 2) * SLAB, :] = block.astype(BF)
        else:
            kept_ref[(view - 5) * SLAB : (view - 4) * SLAB, :] = block


def offset_index(nbr_ref, i):
    middle = nbr_ref.shape[0] // 2
    k = i + (i >= middle)
    index = nbr_ref[pl.ds(k, 1), :]
    return pl.ds(pl.multiple_of(k * SLAB, SLAB), SLAB), low_onehot(index & (LOW - 1)), index >> 8


def window_of(block, halo_ref, slot):
    return pltpu.roll(block.astype(F32), block.shape[1] - first_octant(halo_ref, slot), 1)


def near_gather_kernel(halo_ref, own_ref, pair_ref, nbr_ref, ga_ref, table_ref):
    offsets, rows = nbr_ref.shape
    own_tiles = rows // LOW
    per_peer = table_ref.shape[0] // SLAB - own_tiles
    for t in range(own_tiles):
        table_ref[t * SLAB : (t + 1) * SLAB, :] = own_ref[:, t * LOW : (t + 1) * LOW]
    slot = mirrored(core_bit(), 4, halo_ref.shape[0])
    window = window_of(pair_ref[...], halo_ref, slot).astype(BF)
    for i in range(per_peer):
        t = own_tiles + i
        table_ref[t * SLAB : (t + 1) * SLAB, :] = window[:, i * LOW : (i + 1) * LOW]
    highs = list(range(own_tiles)) + [own_tiles + slot * per_peer + i for i in range(per_peer)]

    def step(i, carry):
        place, onehot, high = offset_index(nbr_ref, i)
        high = jnp.broadcast_to(high, (SLAB, rows))
        picked = dot(table_ref[...], onehot)
        found = jnp.zeros((SLAB, rows), F32)
        for t, value in enumerate(highs):
            found = jnp.where(high == value, picked[t * SLAB : (t + 1) * SLAB], found)
        ga_ref[place, :] = found.astype(BF)
        return carry

    lax.fori_loop(0, offsets - 1, step, 0, unroll=13)
    middle = offsets // 2
    ga_ref[middle * SLAB : (middle + 1) * SLAB, :] = own_ref[...]


def far_gather_kernel(halo_ref, base_ref, near_ref, far_ref, cross_ref, core_ref, nbr_ref, mix_ref, ga_ref,
                      wide_ref, table_ref):
    offsets, rows = nbr_ref.shape
    own_tiles = rows // LOW
    near = halo_ref.shape[0]
    views = {
        0: far_ref[0:SLAB, :],
        1: far_ref[SLAB:, :],
        2: near_ref[0:SLAB, :],
        3: near_ref[SLAB:, :],
        5: cross_ref[SLAB : 2 * SLAB, :],
        6: cross_ref[0:SLAB, :],
        7: cross_ref[3 * SLAB : 4 * SLAB, :],
    }
    both = table_ref.shape[0] // len(views)
    width = both // 2
    highs = []
    for n, (view, block) in enumerate(views.items()):
        slot = mirrored(core_bit(), view, near)
        window = window_of(block, halo_ref, slot)
        wide_ref[n * both : n * both + width, :] = window[:width, :LOW]
        wide_ref[n * both + width : (n + 1) * both, :] = window[:width, LOW : 2 * LOW]
        highs.append(own_tiles + 2 * slot)
    table_ref[...] = wide_ref[...].astype(BF)
    second = (lax.broadcasted_iota(jnp.int32, (both, rows), 0) >= width).astype(jnp.int32)

    def step(i, carry):
        place, onehot, high = offset_index(nbr_ref, i)
        high = jnp.broadcast_to(high, (both, rows)) - second
        picked = dot(table_ref[...], onehot)
        found = jnp.zeros((both, rows), F32)
        for n, value in enumerate(highs):
            found = jnp.where(high == value, picked[n * both : (n + 1) * both], found)
        found = jnp.concatenate([found[:width] + found[width:], jnp.zeros((SLAB - width, rows), F32)], 0)
        ga_ref[place, :] = (base_ref[place, :].astype(F32) + found).astype(BF)
        return carry

    lax.fori_loop(0, offsets - 1, step, 0, unroll=13)
    used = core_ref.shape[0]
    middle = offsets // 2
    itself = slice(middle * SLAB, (middle + 1) * SLAB)
    ga_ref[itself, :] = base_ref[itself, :]
    ga_ref[used:, :] = jnp.zeros_like(ga_ref[used:, :])
    mix_ref[...] = dot(core_ref[...], ga_ref[:used, :], TN)


def core_gradient_kernel(gm_ref, ga_ref, gc_ref):
    gc_ref[...] = dot(gm_ref[...], ga_ref[...], NT)


def sums_kernel(mix_ref, e0, e2, e3, e1, feat_ref, cot_ref, gc_ref, keep_ref, give_ref, rows_ref, mixed_ref):
    rank, rows = mix_ref.shape
    wide = gc_ref.shape[1]
    group = lax.axis_index("chan")
    pick = rank_picker((rank, 4 * SLAB), 1, group, 4, rank // 4, -1)
    slabs = jnp.concatenate([e[0:SLAB, :] for e in (e0, e1, e2, e3)], 0)
    grad_rows = dot(pick, slabs).astype(BF)
    rows_ref[...] = grad_rows
    total = (mix_ref[...] + e1[SLAB:, :].astype(F32)) + (e2[SLAB:, :].astype(F32) + e3[SLAB:, :].astype(F32))
    mixed = total.astype(BF)
    mixed_ref[...] = mixed
    column = lax.broadcasted_iota(jnp.int32, (wide, rank), 0)
    wanted = lax.broadcasted_iota(jnp.int32, (wide, rank), 1)
    free = column % SLAB - (SLAB - 4)
    place = jnp.where((free >= 0) & (column // SLAB * 4 + free == wanted), 1.0, 0.0).astype(BF)
    left = dot(feat_ref[...], grad_rows, NT)
    high = left.astype(BF)
    rest = left - high.astype(F32)
    middle = rest.astype(BF)
    low = (rest - middle.astype(F32)).astype(BF)
    right = jnp.concatenate([jnp.zeros((48, rows), BF), cot_ref[...], jnp.zeros((32, rows), BF)], 0)
    tail = dot(mixed, right, NT)
    packed = gc_ref[...] + (dot(high, place, NT) + dot(middle, place, NT) + dot(low, place, NT))
    packed = jnp.concatenate([packed[:, : wide - 128], packed[:, wide - 128 :] + tail], 1)
    half = rank // 2
    first = core_bit() == 0
    keep_ref[...] = jnp.where(first, packed[:half], packed[half:])
    give_ref[...] = jnp.where(first, packed[half:], packed[:half])


def outputs_kernel(rows_ref, mixed_ref, in_ref, outf_ref, gf_ref, out_ref):
    gf_ref[...] = dot(in_ref[...], rows_ref[...]).astype(BF)
    out_ref[...] = dot(outf_ref[...], mixed_ref[...], TN).astype(BF)


def unpack_kernel(factor, mine_ref, other_ref, left_ref, core_ref, right_ref, flat_ref, turned_ref):
    width, offsets, rank = core_ref.shape
    mine, other = mine_ref[...] * factor, other_ref[...] * factor
    first = core_bit() == 0
    packed = jnp.concatenate([jnp.where(first, mine, other), jnp.where(first, other, mine)], 0)
    flat_ref[...] = packed.T
    for c in range(width):
        core_ref[c] = flat_ref[pl.ds(c, offsets, stride=SLAB), :]
    for j in range(4):
        turned_ref[pl.ds(j, rank // 4, stride=4), :] = flat_ref[pl.ds(width + j, rank // 4, stride=SLAB), :]
    left_ref[...] = turned_ref[...].T
    right_ref[...] = flat_ref[offsets * SLAB : offsets * SLAB + rank, :].T


def shifted(block, axis, distance):
    count = lax.axis_size(axis)
    return lax.ppermute(block, axis, [(i, (i + distance) % count) for i in range(count)])


def crossed(block, mask):
    return lax.ppermute(block, "leaf", [(i, i ^ mask) for i in range(lax.axis_size("leaf"))])


def outward(block, chips):
    count = lax.axis_size("leaf")
    return lax.ppermute(
        block, "leaf", [(i, (i + (2 * chips if i % 2 == 0 else -2 * chips)) % count) for i in range(count)]
    )


def from_z(block, even, odd):
    count = lax.axis_size("leaf")
    return lax.ppermute(
        block, "leaf", [((i + 8 * (odd if i // 8 % 2 else even)) % count, i) for i in range(count)]
    )


def leaf_sum(mine, give):
    mine = mine + crossed(give, 1)
    for masks in ((8,), (2, 6, 4)):
        mine = mine + sum(crossed(mine, mask) for mask in masks)
    mine = mine + sum(from_z(mine, even, odd) for even, odd in ((2, -2), (-1, 1), (-3, 3)))
    return mine, crossed(mine, 1)


def struct(shape, dtype):
    return jax.ShapeDtypeStruct(shape, dtype)


def body(features, in_factor, core, out_factor, neighbours, halo_blocks, row_mask, cotangent):
    channels, rows = features.shape
    offsets, width, rank = core.shape
    near, slots = halo_blocks.shape[1:]
    table_rows = (rows + near * slots * 64) // LOW * SLAB
    packed_width = (offsets * SLAB + 127) // 128 * 128
    keep = row_mask.reshape(1, rows)
    halo = halo_blocks[0]
    core_rows = jnp.pad(core, ((0, 0), (0, SLAB - width), (0, 0))).reshape(offsets * SLAB, rank)
    core_copies = jnp.tile(core[:, None], (1, 4, 1, 1)).reshape(offsets * 4 * width, rank)
    estimate = pl.CostEstimate(flops=5 * 10**9, bytes_accessed=2**20, transcendentals=0)

    own_payload, *payload = pl.pallas_call(
        project_kernel,
        out_shape=[struct((SLAB + rank, rows), F32)] + [struct((SLAB + rank, rows), BF)] * 3,
        in_specs=[VMEM] * 5,
        out_specs=[VMEM] * 4,
        name="project",
    )(features, in_factor, cotangent, out_factor, keep)
    arrived = {j: shifted(payload[j - 1], "chan", j) for j in (1, 3, 2)}

    triple = struct((3 * SLAB, rows), F32)
    grad_mixed, own, kept, cross = pl.pallas_call(
        scatter_kernel,
        out_shape=[struct((rank, rows), BF), struct((SLAB, rows), F32), triple, struct((6 * SLAB, rows), BF)],
        in_specs=[SMEM] + [VMEM] * 6,
        out_specs=[VMEM] * 4,
        scratch_shapes=[pltpu.VMEM((offsets * 4 * width, rows), BF), pltpu.VMEM((256, LOW), F32)],
        compiler_params=ROOMY,
        cost_estimate=estimate,
        name="scatter",
    )(halo, own_payload, arrived[1], arrived[3], arrived[2], core_copies, neighbours)

    def slabs_of(block, first, last):
        return block[first * SLAB : last * SLAB]

    reduced = slabs_of(cross, 0, 1)
    handed = crossed(cross, 1)
    pair = slabs_of(handed, 0, 1)
    far_other, far_same, near_other, near_same, mine = (
        slabs_of(handed, i, i + 1).astype(F32) for i in range(1, 6)
    )
    to_near = [slabs_of(kept, 0, 1) + near_same, slabs_of(kept, 1, 2) + near_other]
    to_far = [slabs_of(kept, 2, 3) + far_same, far_other]
    far = outward(jnp.concatenate([reduced, pair] + [x.astype(BF) for x in to_far], 0), 2)
    near = outward(jnp.concatenate([reduced, pair] + [x.astype(BF) for x in to_near], 0), 1)
    per_peer = slots * 64 // LOW
    near_tiles = rows // LOW + per_peer
    found = pl.pallas_call(
        near_gather_kernel,
        out_shape=struct((offsets * SLAB, rows), BF),
        in_specs=[SMEM] + [VMEM] * 3,
        out_specs=VMEM,
        scratch_shapes=[pltpu.VMEM((near_tiles * SLAB, LOW), BF)],
        compiler_params=ROOMY,
        cost_estimate=estimate,
        name="near_gather",
    )(halo, reduced, pair, neighbours)
    far, near, found = lax.optimization_barrier((far, near, found))
    near_pair, far_pair = slabs_of(near, 0, 2), slabs_of(far, 0, 2)
    passed = slabs_of(near, 3, 4).astype(F32) + slabs_of(far, 3, 4).astype(F32)
    beyond = crossed(jnp.concatenate([near_pair, far_pair, passed.astype(BF)], 0), 1)
    returned = (slabs_of(near, 2, 3).astype(F32) + slabs_of(far, 2, 3).astype(F32)) + slabs_of(beyond, 4, 5).astype(F32)
    grad_slab = (((own + mine) + returned) * keep.astype(F32)).astype(BF)

    mixed_part, gathered = pl.pallas_call(
        far_gather_kernel,
        out_shape=[struct((rank, rows), F32), struct((packed_width, rows), BF)],
        in_specs=[SMEM] + [VMEM] * 6,
        out_specs=[VMEM] * 2,
        scratch_shapes=[pltpu.VMEM((14 * width, LOW), F32), pltpu.VMEM((14 * width, LOW), BF)],
        compiler_params=ROOMY,
        cost_estimate=estimate,
        name="far_gather",
    )(halo, found, near_pair, far_pair, beyond, core_rows, neighbours)
    grad_core = pl.pallas_call(
        core_gradient_kernel,
        out_shape=struct((rank, packed_width), F32),
        in_specs=[VMEM] * 2,
        out_specs=VMEM,
        compiler_params=SNUG,
        cost_estimate=pl.CostEstimate(flops=5 * 10**8, bytes_accessed=2**20, transcendentals=0),
        name="core_gradient",
    )(grad_mixed, gathered)

    shared = jnp.concatenate([grad_slab, mixed_part.astype(BF)], 0)
    exchanged = [shared] + [shifted(shared, "chan", j) for j in (2, 3, 1)]

    sums, full = struct((rank // 2, packed_width), F32), struct((rank, rows), BF)
    mine, give, grad_rows, mixed = pl.pallas_call(
        sums_kernel,
        out_shape=[sums, sums, full, full],
        in_specs=[VMEM] * 8,
        out_specs=[VMEM] * 4,
        compiler_params=SNUG,
        name="sums",
    )(mixed_part, *exchanged, features, cotangent, grad_core)
    grad_features, output = pl.pallas_call(
        outputs_kernel,
        out_shape=[struct((channels, rows), BF)] * 2,
        in_specs=[VMEM] * 4,
        out_specs=[VMEM] * 2,
        compiler_params=SNUG,
        cost_estimate=pl.CostEstimate(flops=5 * 10**8, bytes_accessed=2**20, transcendentals=0),
        name="outputs",
    )(grad_rows, mixed, in_factor, out_factor)
    mine, other = leaf_sum(mine, give)

    factor = float(rows * lax.axis_size("leaf")) ** (-0.5)
    grad_in, grad_core, grad_out = pl.pallas_call(
        lambda *refs: unpack_kernel(factor, *refs),
        out_shape=[struct((channels, rank), F32), struct((width, offsets, rank), F32), struct((rank, channels), F32)],
        in_specs=[VMEM] * 2,
        out_specs=[VMEM] * 3,
        scratch_shapes=[pltpu.VMEM((packed_width, rank), F32), pltpu.VMEM((rank, channels), F32)],
        compiler_params=SNUG,
        name="unpack",
    )(mine, other)
    return (output, grad_features, grad_in, jnp.transpose(grad_core, (1, 0, 2)), grad_out)


def solution(mesh):
    placed = (
        P("chan", "leaf"),
        P("chan", None),
        P(None, "chan", None),
        P(None, "chan"),
        P(None, "leaf"),
        P("leaf", None, None),
        P("leaf"),
        P("chan", "leaf"),
    )
    return jax.shard_map(
        body,
        mesh=mesh,
        in_specs=placed,
        out_specs=(
            P("chan", "leaf"),
            P("chan", "leaf"),
            P("chan", None),
            P(None, "chan", None),
            P(None, "chan"),
        ),
        check_vma=False,
    )
```
